32 devices in a mesh: section: 2 (over y), ctx: 8 (over z, core), tp: 2 (over x).
Axes of the slice: x: 2, y: 2, z: 4, core: 2. Of those that a mesh axis runs over, the one named last changes fastest.
Arguments:
- x_in: bfloat16 [2, 2048, 2688], P(None, ('ctx', 'tp')), may hold values from -180 to 180
- norm_gain: bfloat16 [2, 2688], P('section'), may hold values from 0.099609375 to 1.8984375
- w_query: bfloat16 [2, 2688, 2048], P('section', None, 'tp'), may hold values from -1 to 1
- w_key: bfloat16 [2, 2688, 1024], P('section', 'ctx', 'tp'), may hold values from -3 to 3
- value_projection: bfloat16 [2, 2688, 1024], P('section', 'ctx', 'tp'), may hold values from -0.125 to 0.125
- w_out: bfloat16 [2, 2048, 2688], P('section', 'tp', 'ctx'), may hold values from -0.125 to 0.125
- doc_ids: int32 [2, 16], replicated, may hold values from 0 to 3, never falling along the last dimension, each value on 1 to 6 neighbouring positions
Outputs:
- layer_out: bfloat16 [2, 2, 2048, 2688], P('section', None, ('ctx', 'tp'))
The draws below stay inside these ranges and needn't reach their ends.
Inputs may be any that keep to these rules, and one draw needn't show every extreme that they name: Along each row doc_ids never falls, so each document covers whole consecutive blocks of 128 tokens.
All inputs are finite; a program needn't handle non-finite values.
Results may differ from the reference program's by a relative error of at most 0.018.
Values may be sent and summed in bfloat16 or wider, within the bound.
No kernel may reach another device: no remote copies, remote signals or barrier semaphores. Data moves between devices by JAX's collectives and lax.ppermute only.
A program may use at most 128 MiB of HBM per device.

```python
import math
import jax
import jax.numpy as jnp
import numpy as np
from jax import lax

MODEL_DIM = 2688
QUERY_HEADS = 16
KEY_VALUE_HEADS = 8
HEAD_SIZE = 128
WINDOW = 1024
BLOCK = 128
MICRO = 2
TOK_DEV = 256
PACKED_TOKENS = 2048
NBLK = 16
LAYER_COUNT = 2


def query_rotary_base(key):
    random_noise = jax.random.normal(jax.random.fold_in(key, 11), (LAYER_COUNT, MODEL_DIM, QUERY_HEADS * HEAD_SIZE), jnp.float32)
    return jnp.clip(random_noise, -5.0, 5.0) * MODEL_DIM ** (-0.5)


def draw_w_query(key, part):
    return query_rotary_base(key).astype(jnp.bfloat16)


def draw_w_key(key, part):
    random_noise = jax.random.normal(jax.random.fold_in(key, 12), (LAYER_COUNT, MODEL_DIM, KEY_VALUE_HEADS * HEAD_SIZE), jnp.float32)
    layer_result = jnp.clip(random_noise, -5.0, 5.0) * MODEL_DIM ** (-0.5)
    return layer_result.astype(jnp.bfloat16)


def draw_x_in(key, part):
    random_noise = jnp.clip(jax.random.normal(jax.random.fold_in(key, 21), (MICRO, PACKED_TOKENS, MODEL_DIM), jnp.float32), -5.0, 5.0)
    layer_result = random_noise
    return layer_result.astype(jnp.bfloat16)


def block_scale(key, extent, pieces, smallest, high):
    def one(dim, parts):
        heights = jax.random.uniform(jax.random.fold_in(jax.random.fold_in(key, 6), dim), (parts,), jnp.float32, smallest / len(pieces), high / len(pieces))
        return jnp.repeat(jnp.exp(heights), extent[dim] // parts).reshape((-1,) + (1,) * (len(extent) - dim - 1))

    factor_of = one(*pieces[0])
    for cut in pieces[1:]:
        factor_of = factor_of * one(*cut)
    return factor_of


def profile(amount, total, limit, lean):
    loads = [(1 << 20) // math.isqrt(grade ** lean) + 1 for grade in range(2, amount + 1)]
    rest, counts = total - limit - (amount - 1), [1] * (amount - 1)
    while rest > 0:
        free = [i for i in range(amount - 1) if counts[i] < limit]
        pool, left = sum([loads[i] for i in free]), rest
        for i in free:
            more = min(limit - counts[i], max(1, left * loads[i] // pool), rest)
            counts[i] = counts[i] + more
            rest = rest - more
    return np.array([limit] + counts)


def uneven_parts(key, count, total, most, slope):
    if count == 2:
        one = jax.random.randint(key, (), max(1, total - most), min(most, total - 1) + 1)
        return jnp.stack([one, total - one])
    sizes = jnp.asarray(profile(count, total, most, slope), jnp.int32)
    twos = (count - 1) // 2
    giver, taker = sizes[1:1 + 2 * twos:2], sizes[2:2 + 2 * twos:2]
    margin = jnp.minimum(giver - 1, most - taker)
    moved = jax.random.randint(jax.random.fold_in(key, 1), (twos,), 0, 1 << 20) % (margin + 1)
    sizes = sizes.at[1:1 + 2 * twos:2].set(giver - moved).at[2:2 + 2 * twos:2].set(taker + moved)
    return sizes[jax.random.permutation(jax.random.fold_in(key, 2), count)]


def bell_draw(own_key, extent, width, bound, shards=(), kind=jnp.bfloat16):
    values = jax.random.normal(own_key, extent, jnp.float32) * width
    if len(shards) > 0:
        values = block_scale(own_key, extent, shards, -0.22, 0.18) * values
    return jnp.clip(values, min=-bound, max=bound).astype(kind)


def setup_inputs(seed: int = 0) -> dict:
    splits = jax.random.split(jax.random.key(seed), 8)
    return {
        "x_in": draw_x_in(jax.random.fold_in(splits[7], 71), 0),
        "norm_gain": jnp.clip(1.0 + 0.18 * jax.random.normal(splits[1], (LAYER_COUNT, MODEL_DIM), jnp.float32), 0.099609375, 1.8984375).astype(jnp.bfloat16),
        "w_query": draw_w_query(jax.random.fold_in(splits[7], 71), 0),
        "w_key": draw_w_key(jax.random.fold_in(splits[7], 71), 0),
        "value_projection": bell_draw(splits[4], (LAYER_COUNT, MODEL_DIM, KEY_VALUE_HEADS * HEAD_SIZE), MODEL_DIM ** -0.5, 0.125, ((0, 2), (1, 8), (2, 2))),
        "w_out": bell_draw(splits[5], (LAYER_COUNT, QUERY_HEADS * HEAD_SIZE, MODEL_DIM), (QUERY_HEADS * HEAD_SIZE) ** -0.5, 0.125, ((0, 2), (1, 2), (2, 8))),
        "doc_ids": jax.vmap(lambda own: jnp.searchsorted(jnp.cumsum(uneven_parts(own, max(NBLK // 4, 1), NBLK, min(6, NBLK - max(NBLK // 4, 1) + 1), 0)), jnp.arange(NBLK), side="right"))(jax.random.split(splits[6], MICRO)).reshape((MICRO, NBLK)).astype(jnp.int32),
    }


query_scale = 168.0 ** (-0.5)
rope_base = 10000.0

def rms_normed(hidden, gain_row):
    widened = hidden.astype(jnp.float32)
    mean_square = lax.optimization_barrier(jnp.mean(widened * widened, axis=-1, keepdims=True))
    return (widened * lax.rsqrt(mean_square + 1e-06) * gain_row.astype(jnp.float32)).astype(jnp.bfloat16)

def rotary_apply(tensor, token_position):
    half_dim = tensor.shape[-1] // 2
    frequency = rope_base ** (-(jnp.arange(half_dim, dtype=jnp.float32) * 2.0) / tensor.shape[-1])
    angles = token_position.astype(jnp.float32)[:, None] * frequency[None, :]
    cosine_table = jnp.cos(angles)[:, None, :]
    sine_table = jnp.sin(angles)[:, None, :]
    first_half = tensor[..., :half_dim]
    second_half = tensor[..., half_dim:]
    return jnp.concatenate([first_half * cosine_table - second_half * sine_table, second_half * cosine_table + first_half * sine_table], axis=-1)

def doc_lookup(ids_row, token_index, block):
    block_count = ids_row.shape[0]
    start_block = lax.optimization_barrier(jnp.sum((ids_row[None, :] < ids_row[:, None]).astype(jnp.int32), axis=1))
    block_of = jnp.clip(token_index // block, 0, block_count - 1)
    onehot = (block_of[:, None] == jnp.arange(block_count, dtype=jnp.int32)[None, :]).astype(jnp.int32)
    start_of = lax.optimization_barrier(jnp.sum(onehot * start_block[None, :], axis=1))
    doc_of = lax.optimization_barrier(jnp.sum(onehot * ids_row[None, :], axis=1))
    return (token_index - start_of * block, doc_of)

def attention_rows(grouped_heads, key_matrix_rows, value_rows, query_index, query_doc, key_index, key_doc):
    scores = jnp.einsum('qgrd,kgd->grqk', grouped_heads.astype(jnp.float32), key_matrix_rows.astype(jnp.float32)) * query_scale
    allowed = (key_index[None, :] >= 0) & (key_index[None, :] <= query_index[:, None])
    allowed = allowed & (query_index[:, None] - key_index[None, :] < WINDOW) & (key_doc[None, :] == query_doc[:, None])
    scores = jnp.where(allowed[None, None], scores, -1e+30)
    peak_score = lax.optimization_barrier(jnp.max(scores, axis=-1, keepdims=True))
    raised = jnp.exp(scores - peak_score)
    weights = (raised / lax.optimization_barrier(jnp.sum(raised, axis=-1, keepdims=True))).astype(jnp.bfloat16)
    layer_result = jnp.einsum('grqk,kgd->qgrd', weights.astype(jnp.float32), value_rows.astype(jnp.float32))
    return layer_result.astype(jnp.bfloat16).reshape(grouped_heads.shape[0], -1)

def one_layer(hidden, gain_row, query_weight, key_matrix, value_matrix, out_weight, ids_row):
    normalized_input = rms_normed(hidden, gain_row)
    token_index = jnp.arange(PACKED_TOKENS, dtype=jnp.int32)
    token_position, doc_of = doc_lookup(ids_row, token_index, BLOCK)
    query_matrix_rows = rotary_apply(jnp.dot(normalized_input, query_weight, preferred_element_type=jnp.float32).reshape(PACKED_TOKENS, QUERY_HEADS, HEAD_SIZE), token_position).astype(jnp.bfloat16)
    key_matrix_rows = rotary_apply(jnp.dot(normalized_input, key_matrix, preferred_element_type=jnp.float32).reshape(PACKED_TOKENS, KEY_VALUE_HEADS, HEAD_SIZE), token_position).astype(jnp.bfloat16)
    value_rows = jnp.dot(normalized_input, value_matrix, preferred_element_type=jnp.float32).astype(jnp.bfloat16).reshape(PACKED_TOKENS, KEY_VALUE_HEADS, HEAD_SIZE)
    grouped_heads = query_matrix_rows.reshape(PACKED_TOKENS, KEY_VALUE_HEADS, QUERY_HEADS // KEY_VALUE_HEADS, HEAD_SIZE)

    def block_rows(row_start):
        query_block = lax.dynamic_slice_in_dim(grouped_heads, row_start, TOK_DEV, 0)
        query_index = row_start + jnp.arange(TOK_DEV, dtype=jnp.int32)
        query_doc = lax.dynamic_slice_in_dim(doc_of, row_start, TOK_DEV, 0)
        return attention_rows(query_block, key_matrix_rows, value_rows, query_index, query_doc, token_index, doc_of)
    starts = jnp.arange(PACKED_TOKENS // TOK_DEV, dtype=jnp.int32) * TOK_DEV
    attended = lax.map(block_rows, starts).reshape(PACKED_TOKENS, QUERY_HEADS * HEAD_SIZE)
    mixed_rows = jnp.dot(attended, out_weight, preferred_element_type=jnp.float32)
    return (hidden.astype(jnp.float32) + mixed_rows).astype(jnp.bfloat16)

def reference(x_in, norm_gain, w_query, w_key, value_projection, w_out, doc_ids):
    per_layer = [[None] * MICRO for layer_num in range(LAYER_COUNT)]
    for micro_num in range(MICRO):
        hidden = x_in[micro_num]
        for layer_num in range(LAYER_COUNT):
            hidden = one_layer(hidden, norm_gain[layer_num], w_query[layer_num], w_key[layer_num], value_projection[layer_num], w_out[layer_num], doc_ids[micro_num])
            per_layer[layer_num][micro_num] = hidden
    return jnp.stack([jnp.stack(row_list) for row_list in per_layer])
```

```python
import jax
import jax.numpy as jnp
from jax import lax
from jax.experimental import pallas as pl
from jax.experimental.pallas import tpu as pltpu
from jax.sharding import PartitionSpec as P

HEAD_SIZE = 128
WINDOW = 1024
BLOCK = 128


query_scale = 168.0 ** (-0.5)
rope_base = 10000.0


def shifted(shard, axis, by):
    count = lax.axis_size(axis)
    pairs = [(i, i + by) for i in range(count) if 0 <= i + by < count]
    return lax.ppermute(shard, axis, pairs)


def rms_normed(hidden, gain_row):
    widened = hidden.astype(jnp.float32)
    mean_square = jnp.mean(widened * widened, axis=-1, keepdims=True)
    return (widened * lax.rsqrt(mean_square + 1e-06) * gain_row.astype(jnp.float32)).astype(
        jnp.bfloat16
    )


def rotary_apply(tensor, token_position):
    half_dim = tensor.shape[-1] // 2
    frequency = rope_base ** (-(jnp.arange(half_dim, dtype=jnp.float32) * 2.0) / tensor.shape[-1])
    angles = token_position.astype(jnp.float32)[:, None] * frequency[None, :]
    cosine_table = jnp.cos(angles)[:, None, :]
    sine_table = jnp.sin(angles)[:, None, :]
    first_half = tensor[..., :half_dim]
    second_half = tensor[..., half_dim:]
    return jnp.concatenate(
        [
            first_half * cosine_table - second_half * sine_table,
            second_half * cosine_table + first_half * sine_table,
        ],
        axis=-1,
    )


def doc_lookup(ids_row, token_index, block):
    block_count = ids_row.shape[0]
    start_block = jnp.sum((ids_row[None, :] < ids_row[:, None]).astype(jnp.int32), axis=1)
    block_of = jnp.clip(token_index // block, 0, block_count - 1)
    onehot = (block_of[:, None] == jnp.arange(block_count, dtype=jnp.int32)[None, :]).astype(
        jnp.int32
    )
    start_of = jnp.sum(onehot * start_block[None, :], axis=1)
    doc_of = jnp.sum(onehot * ids_row[None, :], axis=1)
    return (token_index - start_of * block, doc_of)


def attention_rows(
    grouped_heads, key_matrix_rows, value_rows, query_index, query_doc, key_index, key_doc
):
    scores = (
        jnp.einsum(
            "qgrd,kgd->grqk", grouped_heads, key_matrix_rows, preferred_element_type=jnp.float32
        )
        * query_scale
    )
    allowed = (key_index[None, :] >= 0) & (key_index[None, :] <= query_index[:, None])
    allowed = (
        allowed
        & (query_index[:, None] - key_index[None, :] < WINDOW)
        & (key_doc[None, :] == query_doc[:, None])
    )
    scores = jnp.where(allowed[None, None], scores, -1e30)
    peak_score = jnp.max(scores, axis=-1, keepdims=True)
    raised = jnp.exp(scores - peak_score)
    weights = (raised / jnp.sum(raised, axis=-1, keepdims=True)).astype(jnp.bfloat16)
    layer_result = jnp.einsum(
        "grqk,kgd->qgrd", weights, value_rows, preferred_element_type=jnp.float32
    )
    return layer_result.astype(jnp.bfloat16).reshape(grouped_heads.shape[0], -1)


def local(x_in, norm_gain, w_query, w_key, value_projection, w_out, doc_ids):
    section_num = lax.axis_index("section")
    section_count = lax.axis_size("section")
    ctx_num = lax.axis_index("ctx")
    ctx_count = lax.axis_size("ctx")
    tp_count = lax.axis_size("tp")
    micro_count, half_rows, model_width = x_in.shape
    key_full, value_full, out_part = (
        lax.all_gather(w_key, "ctx", axis=1, tiled=True),
        lax.all_gather(value_projection, "ctx", axis=1, tiled=True),
        lax.all_gather(w_out, "ctx", axis=2, tiled=True),
    )
    query_weight = w_query[0]
    key_matrix = key_full[0]
    value_matrix = value_full[0]
    out_weight = out_part[0]
    tok_rows = half_rows * tp_count
    gain_row = norm_gain[0]
    query_heads = query_weight.shape[1] // HEAD_SIZE
    kv_heads = key_matrix.shape[1] // HEAD_SIZE
    group_size = query_heads // kv_heads
    reach_hops = min(-(-WINDOW // tok_rows), ctx_count - 1)
    token_index = ctx_num * tok_rows + jnp.arange(tok_rows, dtype=jnp.int32)
    key_index = (ctx_num - reach_hops) * tok_rows + jnp.arange(
        (reach_hops + 1) * tok_rows, dtype=jnp.int32
    )

    def project(operands):
        whole_rows, token_position = operands
        normalized_input = rms_normed(whole_rows, gain_row)
        query_matrix_rows = rotary_apply(
            jnp.dot(normalized_input, query_weight, preferred_element_type=jnp.float32).reshape(
                tok_rows, query_heads, HEAD_SIZE
            ),
            token_position,
        )
        key_matrix_rows = rotary_apply(
            jnp.dot(normalized_input, key_matrix, preferred_element_type=jnp.float32).reshape(
                tok_rows, kv_heads, HEAD_SIZE
            ),
            token_position,
        )
        value_rows = jnp.dot(
            normalized_input, value_matrix, preferred_element_type=jnp.float32
        ).astype(jnp.bfloat16)
        stacked = jnp.stack(
            [
                key_matrix_rows.astype(jnp.bfloat16).reshape(tok_rows, kv_heads * HEAD_SIZE),
                value_rows,
            ]
        )
        return (
            query_matrix_rows.astype(jnp.bfloat16).reshape(tok_rows, query_heads * HEAD_SIZE),
            stacked,
        )

    def skip_project(operands):
        return (
            jnp.zeros((tok_rows, query_heads * HEAD_SIZE), jnp.bfloat16),
            jnp.zeros((2, tok_rows, kv_heads * HEAD_SIZE), jnp.bfloat16),
        )

    def skip_attend(operands):
        return jnp.zeros((tok_rows, query_heads * HEAD_SIZE), jnp.bfloat16)

    def out_local(operands):
        return jnp.dot(operands, out_weight, preferred_element_type=jnp.float32)

    def skip_out(operands):
        return jnp.zeros((operands.shape[0], out_weight.shape[1]), jnp.float32)

    def step(step_num, carry):
        received, results = carry
        micro_num = step_num - section_num
        active = (micro_num >= 0) & (micro_num < micro_count)
        micro_at = jnp.clip(micro_num, 0, micro_count - 1)
        fresh_rows = lax.dynamic_index_in_dim(x_in, micro_at, 0, keepdims=False)
        current = jnp.where(section_num == 0, fresh_rows, received)
        whole_rows = lax.all_gather(current, "tp", axis=0, tiled=True)
        ids_row = lax.dynamic_index_in_dim(doc_ids, micro_at, 0, keepdims=False)
        token_position, query_doc = doc_lookup(ids_row, token_index, BLOCK)
        unused, key_doc = doc_lookup(ids_row, key_index, BLOCK)
        query_matrix_rows, stacked = lax.cond(
            active, project, skip_project, (whole_rows, token_position)
        )
        pieces = [shifted(stacked, "ctx", distance) for distance in range(reach_hops, 0, -1)]
        window_kv = jnp.concatenate(pieces + [stacked], axis=1)

        def attend(operands):
            query_part, window_part = operands
            grouped_heads = query_part.reshape(tok_rows, kv_heads, group_size, HEAD_SIZE)
            key_matrix_rows = window_part[0].reshape(-1, kv_heads, HEAD_SIZE)
            value_rows = window_part[1].reshape(-1, kv_heads, HEAD_SIZE)
            return attention_rows(
                grouped_heads,
                key_matrix_rows,
                value_rows,
                token_index,
                query_doc,
                key_index,
                key_doc,
            )

        attended = lax.cond(active, attend, skip_attend, (query_matrix_rows, window_kv))
        summed = lax.psum_scatter(
            lax.cond(active, out_local, skip_out, attended), "tp", scatter_dimension=0, tiled=True
        )
        updated = (current.astype(jnp.float32) + summed).astype(jnp.bfloat16)
        previous = lax.dynamic_index_in_dim(results, micro_at, 0, keepdims=False)
        results = lax.dynamic_update_index_in_dim(
            results, jnp.where(active, updated, previous), micro_at, 0
        )
        received = shifted(updated, "section", 1)
        return (received, results)

    start_carry = (
        jnp.zeros((half_rows, model_width), jnp.bfloat16),
        jnp.zeros((micro_count, half_rows, model_width), jnp.bfloat16),
    )
    unused_received, results = lax.fori_loop(0, micro_count + section_count - 1, step, start_carry)
    return results[None]


LANES = 128


def swapped(shard, axis):
    return lax.ppermute(shard, axis, [(0, 1), (1, 0)])


def core_swapped(shard, ctx_count):
    return lax.ppermute(shard, "ctx", [(i, i ^ 1) for i in range(ctx_count)])


def chip_xor(shard, ctx_count, by):
    return lax.ppermute(shard, "ctx", [(i, i ^ (2 * by)) for i in range(ctx_count)])


def chip_shift(shard, ctx_count, by):
    return lax.ppermute(
        shard, "ctx", [(i, i + 2 * by) for i in range(ctx_count) if i + 2 * by < ctx_count]
    )


def columns(array, block, width):
    return lax.dynamic_slice_in_dim(array, block * width, width, 1)


def own_first(flag, own, other):
    return jnp.where(flag == 0, own, other), jnp.where(flag == 0, other, own)


def attention_kernel(low_ref, query_ref, far_ref, near_ref, own_ref, out_ref, window_ref):
    size = HEAD_SIZE
    window_ref[0:BLOCK, :] = far_ref[...]
    for block in range(4):
        at = (0, 2, 1, 3)[block] * BLOCK
        window_ref[(1 + block) * BLOCK : (2 + block) * BLOCK, :] = near_ref[at : at + BLOCK, :]
        window_ref[(5 + block) * BLOCK : (6 + block) * BLOCK, :] = own_ref[at : at + BLOCK, :]
    span = 6 * BLOCK
    row = lax.broadcasted_iota(jnp.int32, (2 * BLOCK, span), 0) % BLOCK
    col = lax.broadcasted_iota(jnp.int32, (2 * BLOCK, span), 1)
    causal = col - 5 * BLOCK <= row
    for block in range(4):
        at = (0, 2, 1, 3)[block] * BLOCK
        rows = slice(block * BLOCK, (block + 6) * BLOCK)
        query = jnp.concatenate(
            [query_ref[at : at + BLOCK, 0:size], query_ref[at : at + BLOCK, size : 2 * size]], axis=0
        )
        scores = lax.dot_general(
            query,
            window_ref[rows, 0:size],
            (((1,), (1,)), ((), ())),
            preferred_element_type=jnp.float32,
        )
        allowed = causal & (col >= low_ref[block] * BLOCK)
        scores = jnp.where(allowed, scores * query_scale, -1e30)
        raised = jnp.exp(scores - jnp.max(scores, axis=-1, keepdims=True))
        total = jnp.sum(raised, axis=-1, keepdims=True)
        mixed = jnp.dot(
            raised.astype(jnp.bfloat16),
            window_ref[rows, size : 2 * size],
            preferred_element_type=jnp.float32,
        )
        mixed = (mixed / total).astype(jnp.bfloat16)
        out_ref[at : at + BLOCK, 0:size] = mixed[0:BLOCK]
        out_ref[at : at + BLOCK, size : 2 * size] = mixed[BLOCK:]


def attend_heads(low, query, far, near, own):
    vmem = pl.BlockSpec(memory_space=pltpu.VMEM)
    return pl.pallas_call(
        attention_kernel,
        out_shape=jax.ShapeDtypeStruct(query.shape, jnp.bfloat16),
        in_specs=[pl.BlockSpec(memory_space=pltpu.SMEM), vmem, vmem, vmem, vmem],
        out_specs=vmem,
        scratch_shapes=[pltpu.VMEM((9 * BLOCK, 2 * HEAD_SIZE), jnp.bfloat16)],
        compiler_params=pltpu.CompilerParams(vmem_limit_bytes=32 * 2**20),
        cost_estimate=pl.CostEstimate(
            flops=4 * 4 * 2 * BLOCK * 6 * BLOCK * HEAD_SIZE,
            bytes_accessed=2 * 2**20,
            transcendentals=4 * 2 * BLOCK * 6 * BLOCK,
        ),
    )(low, query, far, near, own)


def split_heads(x_in, norm_gain, w_query, w_key, value_projection, w_out, doc_ids):
    section = lax.axis_index("section")
    ctx = lax.axis_index("ctx")
    tp = lax.axis_index("tp")
    ctx_count = lax.axis_size("ctx")
    chips = ctx_count // 2
    chip, core = ctx // 2, ctx % 2
    micro_count, half_rows, width = x_in.shape
    chip_rows = 4 * half_rows
    slab = width // ctx_count
    layers = range(2)
    head = HEAD_SIZE

    def of_core(which):
        parts = []
        for sec in (0, 1):
            for weight in (w_key[0], value_projection[0]):
                parts.append(columns(weight, sec * 2 + which, head))
        return jnp.concatenate(parts, axis=1)

    mine = of_core(core)
    theirs = core_swapped(of_core(1 - core), ctx_count)
    chip_kv = jnp.concatenate(own_first(core, mine, theirs), axis=0)
    kv_own = columns(chip_kv, section, 2 * head)
    kv_other = swapped(columns(chip_kv, 1 - section, 2 * head), "section")
    kv_shards = own_first(section, kv_own, kv_other)
    gains = own_first(section, norm_gain[0], swapped(norm_gain[0], "section"))

    out_t = w_out[0].T
    crossed = lax.ppermute(
        out_t,
        ("section", "ctx"),
        [(s * ctx_count + i, (1 - s) * ctx_count + i) for s in (0, 1) for i in range(ctx_count) if i % 2 != s],
    )
    out_shards = own_first(section, out_t, crossed)

    def gather_kv(shard):
        whole = jnp.zeros((width, 2 * head), jnp.bfloat16)
        for by in range(chips):
            part = shard if by == 0 else chip_xor(shard, ctx_count, by)
            whole = lax.dynamic_update_slice_in_dim(whole, part, (chip ^ by) * 2 * slab, 0)
        return whole

    def gather_out(shard):
        got = [
            lax.ppermute(
                shard,
                ("section", "ctx"),
                [
                    (s * ctx_count + 2 * i + s, s * ctx_count + 2 * (i ^ by) + i // 2)
                    for s in (0, 1)
                    for i in range(chips)
                ],
            )
            for by in range(chips)
        ]
        high = (chip // 2) ^ core
        even = jnp.where(high == 1, got[2], got[0])
        odd = jnp.where(high == 1, got[3], got[1])
        low = chip % 2
        rows = jnp.concatenate(own_first(low, even, odd), axis=0)
        me = 2 * section + core
        return jnp.concatenate([columns(rows, me ^ by, 2 * head) for by in range(4)], axis=1)

    block_count = doc_ids.shape[1]
    start = jnp.sum((doc_ids[:, None, :] < doc_ids[:, :, None]).astype(jnp.int32), axis=2)
    chip_start = lax.dynamic_slice_in_dim(start, chip * 4, 4, 1)
    inside = chip * 4 + jnp.arange(4, dtype=jnp.int32)[None, :] - chip_start
    lows = 5 - inside
    order = inside.reshape(micro_count, 2, 2).transpose(0, 2, 1).reshape(micro_count, 4)
    position = (order[:, :, None] * BLOCK + jnp.arange(BLOCK, dtype=jnp.int32)).reshape(
        micro_count, chip_rows
    )
    half = head // 2
    frequency = rope_base ** (-(jnp.arange(half, dtype=jnp.float32) * 2.0) / head)
    angles = position.astype(jnp.float32)[:, :, None] * frequency
    cosine, sine = jnp.cos(angles), jnp.sin(angles)
    cosine = jnp.concatenate([cosine, cosine], axis=-1)
    sine = jnp.concatenate([-sine, sine], axis=-1)

    def rope(array, micro):
        heads = []
        for at in range(0, array.shape[1], head):
            one = array[:, at : at + head]
            turned = jnp.concatenate([one[:, half:], one[:, :half]], axis=1)
            heads.append(one * cosine[micro] + turned * sine[micro])
        return jnp.concatenate(heads, axis=1).astype(jnp.bfloat16)

    def first_hidden(micro):
        mine = x_in[micro].T
        pair = jnp.concatenate(own_first(tp, mine, swapped(mine, "tp")), axis=1)
        other = core_swapped(pair, ctx_count)
        first, second = own_first(core, pair, other)
        return jnp.concatenate(
            [first[:, :half_rows], second[:, :half_rows], first[:, half_rows:], second[:, half_rows:]],
            axis=1,
        )

    query_weight = jnp.concatenate(
        [columns(w_query[0], sec * 2 + core, 2 * head) for sec in (0, 1)], axis=1
    )

    def tn(left, right):
        return lax.dot_general(
            left, right, (((0,), (0,)), ((), ())), preferred_element_type=jnp.float32
        )

    def project(layer, micro, hidden, kv_weight):
        widened = hidden.astype(jnp.float32)
        mean_square = jnp.mean(widened * widened, axis=0, keepdims=True)
        normed = (
            widened * lax.rsqrt(mean_square + 1e-06) * gains[layer].astype(jnp.float32)[:, None]
        ).astype(jnp.bfloat16)
        query = rope(tn(normed, query_weight), micro)
        key_value = tn(normed, kv_weight)
        key_value = jnp.concatenate(
            [rope(key_value[:, :head], micro), key_value[:, head:].astype(jnp.bfloat16)], axis=1
        )
        sent = lax.ppermute(
            columns(query, 1 - section, 2 * head), "section", [(layer, 1 - layer)]
        )
        query = jnp.where(section == layer, columns(query, section, 2 * head), sent)
        near = chip_shift(key_value, ctx_count, 1)
        far = chip_shift(key_value[3 * BLOCK :], ctx_count, 2)
        return attend_heads(lows[micro], query, far, near, key_value)

    def mix(layer, hidden, attended, out_weight):
        across = swapped(attended, "section")
        pair = jnp.concatenate([attended, across], axis=1)
        four = core_swapped(pair, ctx_count)
        every = jnp.concatenate(
            [attended, four[:, : 2 * head], across, four[:, 2 * head :]], axis=1
        )
        partial = lax.dot_general(
            out_weight, every, (((1,), (1,)), ((), ())), preferred_element_type=jnp.float32
        )
        half_tokens = chip_rows // 2
        arrived = swapped(columns(partial, 1 - tp, half_tokens).astype(jnp.bfloat16), "tp")
        mine = columns(hidden, tp, half_tokens)
        residual = jnp.concatenate(
            [
                lax.dynamic_slice_in_dim(mine, (4 * core + section) * slab, slab, 0),
                lax.dynamic_slice_in_dim(mine, (4 * core + 2 + section) * slab, slab, 0),
            ],
            axis=0,
        ).astype(jnp.float32)
        return (
            residual + columns(partial, tp, half_tokens) + arrived.astype(jnp.float32)
        ).astype(jnp.bfloat16)

    def by_section(own, other):
        first, second = own_first(section, own, other)
        return jnp.concatenate(
            [first[:slab], second[:slab], first[slab:], second[slab:]], axis=0
        )

    def spread(piece):
        left, right = piece[:, :half_rows], piece[:, half_rows:]
        left_x = swapped(left, "tp")
        right_y = swapped(right, "section")
        left_y = swapped(jnp.concatenate([left, left_x], axis=1), "section")
        right_x = swapped(jnp.concatenate([right, right_y], axis=1), "tp")
        here = by_section(piece, jnp.concatenate([left_y[:, :half_rows], right_y], axis=1))
        there = by_section(
            jnp.concatenate([left_x, right_x[:, :half_rows]], axis=1),
            jnp.concatenate([left_y[:, half_rows:], right_x[:, half_rows:]], axis=1),
        )
        both = jnp.concatenate(own_first(tp, here, there), axis=1)
        return jnp.concatenate(own_first(core, both, core_swapped(both, ctx_count)), axis=0)

    def finish(piece):
        got = lax.ppermute(piece, "section", [(0, 1)])
        both = by_section(piece, got)
        other = core_swapped(columns(both, 1 - core, half_rows), ctx_count)
        return jnp.concatenate(own_first(core, columns(both, core, half_rows), other), axis=0).T

    micros = range(micro_count)
    hidden = [first_hidden(micro) for micro in micros]
    results = []
    for layer in layers:
        kv_weight = gather_kv(kv_shards[layer])
        out_weight = gather_out(out_shards[layer])
        attended = [project(layer, micro, hidden[micro], kv_weight) for micro in micros]
        pieces = [mix(layer, hidden[micro], attended[micro], out_weight) for micro in micros]
        if layer == 0:
            hidden = [spread(piece) for piece in pieces]
            results.append(
                jnp.stack([columns(one, 2 * tp + core, half_rows).T for one in hidden])
            )
        else:
            results.append(jnp.stack([finish(piece) for piece in pieces]))
    return jnp.where(section == 0, results[0], results[1])[None]


def solution(mesh):
    in_specs = (
        P(None, ("ctx", "tp"), None),
        P("section", None),
        P("section", None, "tp"),
        P("section", "ctx", "tp"),
        P("section", "ctx", "tp"),
        P("section", "tp", "ctx"),
        P(),
    )
    out_specs = P("section", None, ("ctx", "tp"), None)
    sizes = mesh.shape
    fits = sizes["section"] == 2 and sizes["tp"] == 2 and sizes["ctx"] == 8
    body = split_heads if fits else local
    return jax.shard_map(body, mesh=mesh, in_specs=in_specs, out_specs=out_specs, check_vma=False)
```

```python
import functools

import numpy as np
import jax
import jax.numpy as jnp
from jax import lax
from jax.experimental import pallas as pl
from jax.experimental.pallas import tpu as pltpu
from jax.sharding import PartitionSpec as P

HEAD_SIZE = 128
WINDOW = 1024
BLOCK = 128


query_scale = 168.0 ** (-0.5)
rope_base = 10000.0


def shifted(shard, axis, by):
    count = lax.axis_size(axis)
    pairs = [(i, i + by) for i in range(count) if 0 <= i + by < count]
    return lax.ppermute(shard, axis, pairs)


def rms_normed(hidden, gain_row):
    widened = hidden.astype(jnp.float32)
    mean_square = jnp.mean(widened * widened, axis=-1, keepdims=True)
    return (widened * lax.rsqrt(mean_square + 1e-06) * gain_row.astype(jnp.float32)).astype(
        jnp.bfloat16
    )


def rotary_apply(tensor, token_position):
    half_dim = tensor.shape[-1] // 2
    frequency = rope_base ** (-(jnp.arange(half_dim, dtype=jnp.float32) * 2.0) / tensor.shape[-1])
    angles = token_position.astype(jnp.float32)[:, None] * frequency[None, :]
    cosine_table = jnp.cos(angles)[:, None, :]
    sine_table = jnp.sin(angles)[:, None, :]
    first_half = tensor[..., :half_dim]
    second_half = tensor[..., half_dim:]
    return jnp.concatenate(
        [
            first_half * cosine_table - second_half * sine_table,
            second_half * cosine_table + first_half * sine_table,
        ],
        axis=-1,
    )


def doc_lookup(ids_row, token_index, block):
    block_count = ids_row.shape[0]
    start_block = jnp.sum((ids_row[None, :] < ids_row[:, None]).astype(jnp.int32), axis=1)
    block_of = jnp.clip(token_index // block, 0, block_count - 1)
    onehot = (block_of[:, None] == jnp.arange(block_count, dtype=jnp.int32)[None, :]).astype(
        jnp.int32
    )
    start_of = jnp.sum(onehot * start_block[None, :], axis=1)
    doc_of = jnp.sum(onehot * ids_row[None, :], axis=1)
    return (token_index - start_of * block, doc_of)


def attention_rows(
    grouped_heads, key_matrix_rows, value_rows, query_index, query_doc, key_index, key_doc
):
    scores = (
        jnp.einsum(
            "qgrd,kgd->grqk", grouped_heads, key_matrix_rows, preferred_element_type=jnp.float32
        )
        * query_scale
    )
    allowed = (key_index[None, :] >= 0) & (key_index[None, :] <= query_index[:, None])
    allowed = (
        allowed
        & (query_index[:, None] - key_index[None, :] < WINDOW)
        & (key_doc[None, :] == query_doc[:, None])
    )
    scores = jnp.where(allowed[None, None], scores, -1e30)
    peak_score = jnp.max(scores, axis=-1, keepdims=True)
    raised = jnp.exp(scores - peak_score)
    weights = (raised / jnp.sum(raised, axis=-1, keepdims=True)).astype(jnp.bfloat16)
    layer_result = jnp.einsum(
        "grqk,kgd->qgrd", weights, value_rows, preferred_element_type=jnp.float32
    )
    return layer_result.astype(jnp.bfloat16).reshape(grouped_heads.shape[0], -1)


def local(x_in, norm_gain, w_query, w_key, value_projection, w_out, doc_ids):
    section_num = lax.axis_index("section")
    section_count = lax.axis_size("section")
    ctx_num = lax.axis_index("ctx")
    ctx_count = lax.axis_size("ctx")
    tp_count = lax.axis_size("tp")
    micro_count, half_rows, model_width = x_in.shape
    key_full, value_full, out_part = (
        lax.all_gather(w_key, "ctx", axis=1, tiled=True),
        lax.all_gather(value_projection, "ctx", axis=1, tiled=True),
        lax.all_gather(w_out, "ctx", axis=2, tiled=True),
    )
    query_weight = w_query[0]
    key_matrix = key_full[0]
    value_matrix = value_full[0]
    out_weight = out_part[0]
    tok_rows = half_rows * tp_count
    gain_row = norm_gain[0]
    query_heads = query_weight.shape[1] // HEAD_SIZE
    kv_heads = key_matrix.shape[1] // HEAD_SIZE
    group_size = query_heads // kv_heads
    reach_hops = min(-(-WINDOW // tok_rows), ctx_count - 1)
    token_index = ctx_num * tok_rows + jnp.arange(tok_rows, dtype=jnp.int32)
    key_index = (ctx_num - reach_hops) * tok_rows + jnp.arange(
        (reach_hops + 1) * tok_rows, dtype=jnp.int32
    )

    def project(operands):
        whole_rows, token_position = operands
        normalized_input = rms_normed(whole_rows, gain_row)
        query_matrix_rows = rotary_apply(
            jnp.dot(normalized_input, query_weight, preferred_element_type=jnp.float32).reshape(
                tok_rows, query_heads, HEAD_SIZE
            ),
            token_position,
        )
        key_matrix_rows = rotary_apply(
            jnp.dot(normalized_input, key_matrix, preferred_element_type=jnp.float32).reshape(
                tok_rows, kv_heads, HEAD_SIZE
            ),
            token_position,
        )
        value_rows = jnp.dot(
            normalized_input, value_matrix, preferred_element_type=jnp.float32
        ).astype(jnp.bfloat16)
        stacked = jnp.stack(
            [
                key_matrix_rows.astype(jnp.bfloat16).reshape(tok_rows, kv_heads * HEAD_SIZE),
                value_rows,
            ]
        )
        return (
            query_matrix_rows.astype(jnp.bfloat16).reshape(tok_rows, query_heads * HEAD_SIZE),
            stacked,
        )

    def skip_project(operands):
        return (
            jnp.zeros((tok_rows, query_heads * HEAD_SIZE), jnp.bfloat16),
            jnp.zeros((2, tok_rows, kv_heads * HEAD_SIZE), jnp.bfloat16),
        )

    def skip_attend(operands):
        return jnp.zeros((tok_rows, query_heads * HEAD_SIZE), jnp.bfloat16)

    def out_local(operands):
        return jnp.dot(operands, out_weight, preferred_element_type=jnp.float32)

    def skip_out(operands):
        return jnp.zeros((operands.shape[0], out_weight.shape[1]), jnp.float32)

    def step(step_num, carry):
        received, results = carry
        micro_num = step_num - section_num
        active = (micro_num >= 0) & (micro_num < micro_count)
        micro_at = jnp.clip(micro_num, 0, micro_count - 1)
        fresh_rows = lax.dynamic_index_in_dim(x_in, micro_at, 0, keepdims=False)
        current = jnp.where(section_num == 0, fresh_rows, received)
        whole_rows = lax.all_gather(current, "tp", axis=0, tiled=True)
        ids_row = lax.dynamic_index_in_dim(doc_ids, micro_at, 0, keepdims=False)
        token_position, query_doc = doc_lookup(ids_row, token_index, BLOCK)
        unused, key_doc = doc_lookup(ids_row, key_index, BLOCK)
        query_matrix_rows, stacked = lax.cond(
            active, project, skip_project, (whole_rows, token_position)
        )
        pieces = [shifted(stacked, "ctx", distance) for distance in range(reach_hops, 0, -1)]
        window_kv = jnp.concatenate(pieces + [stacked], axis=1)

        def attend(operands):
            query_part, window_part = operands
            grouped_heads = query_part.reshape(tok_rows, kv_heads, group_size, HEAD_SIZE)
            key_matrix_rows = window_part[0].reshape(-1, kv_heads, HEAD_SIZE)
            value_rows = window_part[1].reshape(-1, kv_heads, HEAD_SIZE)
            return attention_rows(
                grouped_heads,
                key_matrix_rows,
                value_rows,
                token_index,
                query_doc,
                key_index,
                key_doc,
            )

        attended = lax.cond(active, attend, skip_attend, (query_matrix_rows, window_kv))
        summed = lax.psum_scatter(
            lax.cond(active, out_local, skip_out, attended), "tp", scatter_dimension=0, tiled=True
        )
        updated = (current.astype(jnp.float32) + summed).astype(jnp.bfloat16)
        previous = lax.dynamic_index_in_dim(results, micro_at, 0, keepdims=False)
        results = lax.dynamic_update_index_in_dim(
            results, jnp.where(active, updated, previous), micro_at, 0
        )
        received = shifted(updated, "section", 1)
        return (received, results)

    start_carry = (
        jnp.zeros((half_rows, model_width), jnp.bfloat16),
        jnp.zeros((micro_count, half_rows, model_width), jnp.bfloat16),
    )
    unused_received, results = lax.fori_loop(0, micro_count + section_count - 1, step, start_carry)
    return results[None]


SECTION, CORE, TP, CHIP = range(4)


def swapped(shard, axis):
    return lax.ppermute(shard, axis, [(0, 1), (1, 0)])


def core_swapped(shard, ctx_count):
    return lax.ppermute(shard, "ctx", [(i, i ^ 1) for i in range(ctx_count)])


def chip_xor(shard, ctx_count, by):
    return lax.ppermute(shard, "ctx", [(i, i ^ (2 * by)) for i in range(ctx_count)])


def chip_shift(shard, ctx_count, by):
    return lax.ppermute(
        shard, "ctx", [(i, i + 2 * by) for i in range(ctx_count) if i + 2 * by < ctx_count]
    )


def own_first(flag, own, other):
    return jnp.where(flag == 0, own, other), jnp.where(flag == 0, other, own)


def together(*values):
    return lax.optimization_barrier(values)


def call(kernel, scalars, operands, outputs, scratch=()):
    vmem = pl.BlockSpec(memory_space=pltpu.VMEM)
    smem = pl.BlockSpec(memory_space=pltpu.SMEM)
    return pl.pallas_call(
        kernel,
        out_shape=[jax.ShapeDtypeStruct(shape, kind) for shape, kind in outputs],
        in_specs=[smem] * len(scalars) + [vmem] * len(operands),
        out_specs=[vmem] * len(outputs),
        scratch_shapes=list(scratch),
        compiler_params=pltpu.CompilerParams(vmem_limit_bytes=16 * 2**20),
        cost_estimate=pl.CostEstimate(flops=1024, bytes_accessed=1024, transcendentals=0),
    )(*scalars, *operands)


def aligned(index, size):
    return pl.ds(pl.multiple_of(index * size, size), size)


def pick_kernel(place, key_ref, value_ref, mine_ref, theirs_ref):
    core = place[CORE]
    for out_ref, which in ((mine_ref, core), (theirs_ref, 1 - core)):
        for sec in (0, 1):
            for kind, ref in enumerate((key_ref, value_ref)):
                at = (2 * sec + kind) * HEAD_SIZE
                out_ref[:, at : at + HEAD_SIZE] = ref[:, aligned(2 * sec + which, HEAD_SIZE)]


def halve_kernel(place, mine_ref, theirs_ref, own_ref, other_ref):
    core, section = place[CORE], place[SECTION]
    rows, pair = mine_ref.shape[0], 2 * HEAD_SIZE
    for out_ref, sec in ((own_ref, section), (other_ref, 1 - section)):
        out_ref[aligned(core, rows), :] = mine_ref[:, aligned(sec, pair)]
        out_ref[aligned(1 - core, rows), :] = theirs_ref[:, aligned(sec, pair)]


def query_columns_kernel(place, weight_ref, out_ref):
    out_ref[...] = weight_ref[...]


def turned(array, cosine, sine):
    return array * cosine + pltpu.roll(array, HEAD_SIZE // 2, 1) * sine


def rope_tables(inside, tables):
    row_cos, row_sin, block_cos, block_sin = tables
    cosine, sine = [], []
    for at in range(4):
        block = pl.ds(inside[at], 1)
        first, second = block_cos[block, :], block_sin[block, :]
        cosine.append(first * row_cos[...] - second * row_sin[...])
        sine.append(second * row_cos[...] + first * row_sin[...])
    lane = lax.broadcasted_iota(jnp.int32, (4 * BLOCK, HEAD_SIZE), 1)
    sine = jnp.concatenate(sine, axis=0)
    return jnp.concatenate(cosine, axis=0), jnp.where(lane < HEAD_SIZE // 2, -sine, sine)


def host_tables(block_count):
    lane = np.arange(HEAD_SIZE) % (HEAD_SIZE // 2)
    frequency = rope_base ** (-(lane * 2.0) / HEAD_SIZE)
    rows = np.arange(BLOCK)[:, None] * frequency
    blocks = np.arange(block_count)[:, None] * (BLOCK * frequency)
    angles = (np.cos(rows), np.sin(rows), np.cos(blocks), np.sin(blocks))
    return [jnp.asarray(one, jnp.float32) for one in angles]


def store_queries(place, query, rope, own_ref, other_ref):
    heads = [
        turned(query[:, at : at + HEAD_SIZE], *rope).astype(jnp.bfloat16)
        for at in range(0, query.shape[1], HEAD_SIZE)
    ]
    for sec in (0, 1):

        @pl.when(place[SECTION] == sec)
        def _():
            for out_ref, first in ((own_ref, 2 * sec), (other_ref, 2 - 2 * sec)):
                out_ref[:, :HEAD_SIZE] = heads[first]
                out_ref[:, HEAD_SIZE:] = heads[first + 1]


def store_keys(key_value, rope, out_ref, far_ref):
    size = HEAD_SIZE
    key = turned(key_value[:, :size], *rope).astype(jnp.bfloat16)
    value = key_value[:, size:].astype(jnp.bfloat16)
    out_ref[:, :size] = key
    out_ref[:, size:] = value
    far_ref[:, :size] = key[-BLOCK:]
    far_ref[:, size:] = value[-BLOCK:]


def first_query_kernel(place, inside, *refs):
    pieces, tables, (gain, weight, normed_ref, own_ref, other_ref) = refs[:4], refs[4:8], refs[8:]
    for by, ref in enumerate(pieces):
        rows = ref[...].astype(jnp.float32)
        mean_square = jnp.mean(rows * rows, axis=-1, keepdims=True)
        rows = rows * lax.rsqrt(mean_square + 1e-06) * gain[...].astype(jnp.float32)
        at = 2 * (place[TP] ^ (by & 1)) + (place[CORE] ^ (by >> 1))
        normed_ref[aligned(at, BLOCK), :] = rows.astype(jnp.bfloat16)
    query = jnp.dot(normed_ref[...], weight[...], preferred_element_type=jnp.float32)
    store_queries(place, query, rope_tables(inside, tables), own_ref, other_ref)


def first_keys_kernel(place, inside, normed, *refs):
    parts, tables, (out_ref, far_ref, weight) = refs[:4], refs[4:8], refs[8:]
    for by, ref in enumerate(parts):
        weight[aligned(place[CHIP] ^ by, ref.shape[0]), :] = ref[...]
    key_value = jnp.dot(normed[...], weight[...], preferred_element_type=jnp.float32)
    store_keys(key_value, rope_tables(inside, tables), out_ref, far_ref)


def tn(left, right):
    return lax.dot_general(
        left, right, (((0,), (0,)), ((), ())), preferred_element_type=jnp.float32
    )


def keys_kernel(place, inside, *refs):
    pieces, tables, (gain, weight, out_ref, far_ref, normed) = refs[:16], refs[16:20], refs[20:]
    me = 2 * place[SECTION] + place[CORE]
    width = 4 * pieces[0].shape[0]
    for by_tp in (0, 1):
        for half in (0, 1):
            rows = [pieces[4 * block + 2 * by_tp + half][...].astype(jnp.float32) for block in range(4)]
            total = sum(jnp.sum(one * one, axis=0, keepdims=True) for one in rows)
            scale = lax.rsqrt(total / width + 1e-06)
            at = 2 * (place[TP] ^ by_tp) + half
            for block, one in enumerate(rows):
                normed[block, :, aligned(at, BLOCK)] = (one * scale * gain[me ^ block]).astype(
                    jnp.bfloat16
                )
    key_value = sum(tn(normed[block], weight[me ^ block]) for block in range(4))
    store_keys(key_value, rope_tables(inside, tables), out_ref, far_ref)


def query_kernel(place, inside, normed, weight, *refs):
    tables, (own_ref, other_ref) = refs[:4], refs[4:]
    me = 2 * place[SECTION] + place[CORE]
    query = sum(tn(normed[block], weight[me ^ block]) for block in range(4))
    store_queries(place, query, rope_tables(inside, tables), own_ref, other_ref)


def attention_kernel(
    layer, place, low_ref, kept_ref, sent_ref, far_ref, near_ref, own_ref, out_ref, window_ref
):
    size = HEAD_SIZE
    window_ref[0:BLOCK, :] = far_ref[...]
    for block in range(4):
        at = (0, 2, 1, 3)[block] * BLOCK
        window_ref[(1 + block) * BLOCK : (2 + block) * BLOCK, :] = near_ref[at : at + BLOCK, :]
        window_ref[(5 + block) * BLOCK : (6 + block) * BLOCK, :] = own_ref[at : at + BLOCK, :]
    span = 6 * BLOCK
    row = lax.broadcasted_iota(jnp.int32, (2 * BLOCK, span), 0) % BLOCK
    col = lax.broadcasted_iota(jnp.int32, (2 * BLOCK, span), 1)
    causal = col - 5 * BLOCK <= row
    home = place[SECTION] == layer
    for block in range(4):
        at = (0, 2, 1, 3)[block] * BLOCK
        rows = slice(block * BLOCK, (block + 6) * BLOCK)
        query = jnp.where(home, kept_ref[at : at + BLOCK, :], sent_ref[at : at + BLOCK, :])
        query = jnp.concatenate([query[:, :size], query[:, size:]], axis=0)
        scores = lax.dot_general(
            query,
            window_ref[rows, 0:size],
            (((1,), (1,)), ((), ())),
            preferred_element_type=jnp.float32,
        )
        allowed = causal & (col >= low_ref[block] * BLOCK)
        scores = jnp.where(allowed, scores * query_scale, -1e30)
        raised = jnp.exp(scores - jnp.max(scores, axis=-1, keepdims=True))
        total = jnp.sum(raised, axis=-1, keepdims=True)
        mixed = jnp.dot(
            raised.astype(jnp.bfloat16),
            window_ref[rows, size : 2 * size],
            preferred_element_type=jnp.float32,
        )
        mixed = (mixed / total).astype(jnp.bfloat16)
        out_ref[at : at + BLOCK, 0:size] = mixed[0:BLOCK]
        out_ref[at : at + BLOCK, size : 2 * size] = mixed[BLOCK:]


def mix_kernel(place, own, core_, across, both, weight, keep_ref, send_ref):
    me = 2 * place[SECTION] + place[CORE]
    half = keep_ref.shape[1]
    for out_ref, tp in ((keep_ref, place[TP]), (send_ref, 1 - place[TP])):
        total = sum(
            lax.dot_general(
                weight[:, aligned(me ^ by, 2 * HEAD_SIZE)],
                ref[aligned(tp, half), :],
                (((1,), (1,)), ((), ())),
                preferred_element_type=jnp.float32,
            )
            for by, ref in enumerate((own, core_, across, both))
        )
        out_ref[...] = total.astype(out_ref.dtype)


def add_kernel(residual, keep, arrived, *out_refs):
    total = residual[...].astype(jnp.float32) + keep[...] + arrived[...].astype(jnp.float32)
    total = total.astype(jnp.bfloat16)
    for at, ref in enumerate(out_refs):
        count = ref.shape[1]
        ref[...] = total[:, at * count : (at + 1) * count]


def split_heads(x_in, norm_gain, w_query, w_key, value_projection, w_out, doc_ids):
    section = lax.axis_index("section")
    ctx = lax.axis_index("ctx")
    tp = lax.axis_index("tp")
    ctx_count = lax.axis_size("ctx")
    chips = ctx_count // 2
    chip, core = ctx // 2, ctx % 2
    place = jnp.stack([section, core, tp, chip]).astype(jnp.int32)
    micro_count, half_rows, width = x_in.shape
    tokens = 4 * half_rows
    slab = width // ctx_count
    head, pair = HEAD_SIZE, 2 * HEAD_SIZE
    block_rows = width // 4
    micros = range(micro_count)
    b16, f32 = jnp.bfloat16, jnp.float32

    mine, theirs = call(
        pick_kernel, [place], [w_key[0], value_projection[0]], [((slab, 2 * pair), b16)] * 2
    )
    theirs = core_swapped(theirs, ctx_count)
    kv_own, kv_other = call(
        halve_kernel, [place], [mine, theirs], [((2 * slab, pair), b16)] * 2
    )
    kv_other = swapped(kv_other, "section")

    gain_other = swapped(norm_gain[0], "section")
    kv_other, gain_other = together(kv_other, gain_other)
    gains = own_first(section, norm_gain[0], gain_other)
    kv_shards = own_first(section, kv_own, kv_other)
    parts = [kv_shards[0]] + [chip_xor(kv_shards[0], ctx_count, by) for by in range(1, chips)]

    pieces = []
    for micro in micros:
        own = x_in[micro]
        tp_other, parts[1 + micro] = together(swapped(own, "tp"), parts[1 + micro])
        pieces.append([own, tp_other, core_swapped(own, ctx_count), core_swapped(tp_other, ctx_count)])
    w_out, parts[1] = together(w_out, parts[1])

    start = jnp.sum((doc_ids[:, None, :] < doc_ids[:, :, None]).astype(jnp.int32), axis=2)
    chip_start = lax.dynamic_slice_in_dim(start, chip * 4, 4, 1)
    inside = chip * 4 + jnp.arange(4, dtype=jnp.int32)[None, :] - chip_start
    lows = 5 - inside
    order = inside.reshape(micro_count, 2, 2).transpose(0, 2, 1).reshape(micro_count, 4)
    tables = host_tables(doc_ids.shape[1])

    def query_columns():
        vmem = pltpu.VMEM
        return pl.pallas_call(
            query_columns_kernel,
            out_shape=jax.ShapeDtypeStruct((width, 2 * pair), b16),
            grid_spec=pltpu.PrefetchScalarGridSpec(
                num_scalar_prefetch=1,
                grid=(2,),
                in_specs=[pl.BlockSpec((width, pair), lambda i, at: (0, 2 * i + at[CORE]), memory_space=vmem)],
                out_specs=pl.BlockSpec((width, pair), lambda i, at: (0, i), memory_space=vmem),
            ),
            compiler_params=pltpu.CompilerParams(vmem_limit_bytes=16 * 2**20),
            cost_estimate=pl.CostEstimate(flops=1024, bytes_accessed=1024, transcendentals=0),
        )(place, w_query[0])

    query_weight = query_columns()

    def by_block(weight):
        columns = weight.shape[1]
        weight = weight.reshape(chips, 4, slab // 2, columns).transpose(1, 0, 2, 3)
        return weight.reshape(4, block_rows, columns)

    def up(shard):
        return chip_shift(shard, ctx_count, 1)

    def down(shard):
        return lax.ppermute(shard, "ctx", [(i, i - 2) for i in range(2, ctx_count)])

    def onward(shard):
        return lax.ppermute(shard, "ctx", [(2, 0), (3, 1), (4, 6), (5, 7)])

    def from_all_chips(shard):
        from_below, from_above, across = up(shard), down(shard), chip_xor(shard, ctx_count, 2)
        far = onward(across)
        one = jnp.where(chip % 2 == 0, from_above, from_below)
        three = jnp.where(chip == 1, from_above, jnp.where(chip == 2, from_below, far))
        return [shard, one, across, three]

    def whole(parts):
        rows = parts[0].shape[0]
        out = jnp.zeros((chips * rows, parts[0].shape[1]), parts[0].dtype)
        for by, part in enumerate(parts):
            out = lax.dynamic_update_slice_in_dim(out, part, (chip ^ by) * rows, 0)
        return out

    out_t = w_out[0].T
    crossed = lax.ppermute(
        out_t,
        ("section", "ctx"),
        [(s * ctx_count + i, (1 - s) * ctx_count + i) for s in (0, 1) for i in range(ctx_count) if i % 2 != s],
    )

    def half_slab(shard):
        sent = core_swapped(
            lax.dynamic_slice_in_dim(shard, (1 - core) * (slab // 2), slab // 2, 0), ctx_count
        )
        kept = lax.dynamic_slice_in_dim(shard, core * (slab // 2), slab // 2, 0)
        return jnp.where(core == section, kept, sent)

    out_shards = own_first(section, out_t, crossed)
    half_slabs = [half_slab(shard) for shard in out_shards]

    def shifted(key_value, far):
        return chip_shift(key_value, ctx_count, 1), chip_shift(far, ctx_count, 2)

    def attend(layer, micro, query, key_value, window):
        own, other = query
        sent = lax.ppermute(other, "section", [(layer, 1 - layer)])
        near, far = window
        return call(
            functools.partial(attention_kernel, layer),
            [place, lows[micro]],
            [own, sent, far, near, key_value],
            [((tokens, pair), b16)],
            [pltpu.VMEM((9 * BLOCK, pair), b16)],
        )[0]

    def mix(attended, out_weight, residual, count):
        across = swapped(attended, "section")
        keep, send = call(
            mix_kernel,
            [place],
            [
                attended,
                core_swapped(attended, ctx_count),
                across,
                core_swapped(across, ctx_count),
                out_weight,
            ],
            [((block_rows, tokens // 2), f32), ((block_rows, tokens // 2), b16)],
        )
        arrived = swapped(send, "tp")
        return call(
            add_kernel,
            [],
            [residual, keep, arrived],
            [((block_rows, tokens // 2 // count), b16)] * count,
        )

    def spread(left, right):
        left_x, right_y = swapped(left, "tp"), swapped(right, "section")
        left_y, right_x = swapped(left, "section"), swapped(right, "tp")
        left_xy, right_xy = swapped(left_x, "section"), swapped(right_y, "tp")
        here = [left, right, left_x, right_x]
        there = [left_y, right_y, left_xy, right_xy]
        over = [core_swapped(one, ctx_count) for one in here + there]
        return here + over[:4] + there + over[4:]

    def in_order(blocks):
        by_section = [own_first(core, blocks[0], blocks[1]), own_first(core, blocks[2], blocks[3])]
        low = own_first(section, by_section[0][0], by_section[1][0])
        high = own_first(section, by_section[0][1], by_section[1][1])
        whole = jnp.stack([low[0], high[0], low[1], high[1]])
        count = whole.shape[-1]
        whole = whole.reshape(4, chips, slab // 2, count).transpose(1, 0, 2, 3)
        return whole.reshape(width, count)

    queries, keys, windows, residuals = [], [], [], []
    for micro in micros:
        normed, *query = call(
            first_query_kernel,
            [place, order[micro]],
            [*pieces[micro], *tables, gains[0][None], query_weight],
            [((tokens, width), b16), ((tokens, pair), b16), ((tokens, pair), b16)],
        )
        key_value, far = call(
            first_keys_kernel,
            [place, order[micro]],
            [normed, *parts, *tables],
            [((tokens, pair), b16), ((BLOCK, pair), b16)],
            [pltpu.VMEM((width, pair), b16)],
        )
        queries.append(query)
        keys.append(key_value)
        windows.append(shifted(key_value, far))
        own, _, core_other, _ = pieces[micro]
        residual = jnp.concatenate(own_first(core, own, core_other), axis=0).T
        residual = residual.reshape(chips, 4, slab // 2, tokens // 2)
        residual = lax.dynamic_index_in_dim(residual, 2 * section + core, 1, keepdims=False)
        residuals.append(residual.reshape(block_rows, tokens // 2))
    near, far = windows[1]
    near, far, shard = together(near, far, half_slabs[0])
    windows[1] = near, far
    out_parts = [shard] + [chip_xor(shard, ctx_count, by) for by in range(1, chips)]
    attended = [attend(0, m, queries[m], keys[m], windows[m]) for m in micros]
    *out_parts, kv_shard = together(*out_parts, kv_shards[1])
    out_weight = whole(out_parts)
    kv_parts = from_all_chips(kv_shard)
    *kv_parts, shard = together(*kv_parts, half_slabs[1])
    next_kv = by_block(whole(kv_parts))
    next_out = whole(from_all_chips(shard))
    halves = [mix(attended[m], out_weight, residuals[m], 2) for m in micros]
    pieces = [spread(*halves[micro]) for micro in micros]
    results = [
        jnp.stack(
            [
                in_order([jnp.where(core == 0, one[4 * i], one[4 * i + 1]) for i in range(4)]).T
                for one in pieces
            ]
        )
    ]

    gain = jnp.broadcast_to(by_block(gains[1].astype(f32)[:, None]), (4, block_rows, BLOCK))
    query_weight = by_block(query_weight)
    attended = []
    for micro in micros:
        key_value, far, normed = call(
            keys_kernel,
            [place, order[micro]],
            [*pieces[micro], *tables, gain, next_kv],
            [((tokens, pair), b16), ((BLOCK, pair), b16), ((4, block_rows, tokens), b16)],
        )
        query = call(
            query_kernel,
            [place, order[micro]],
            [normed, query_weight, *tables],
            [((tokens, pair), b16)] * 2,
        )
        attended.append(attend(1, micro, query, key_value, shifted(key_value, far)))
    last = []
    for micro in micros:
        (piece,) = mix(attended[micro], next_out, jnp.concatenate(halves[micro], axis=1), 1)
        blocks = []
        for one in (piece, lax.ppermute(piece, "section", [(0, 1)])):
            kept, passed = own_first(core, one[:, :BLOCK], one[:, BLOCK:])
            blocks += [kept, core_swapped(passed, ctx_count)]
        last.append(in_order(blocks).T)
    results.append(jnp.stack(last))
    return jnp.where(section == 0, results[0], results[1])[None]


def solution(mesh):
    in_specs = (
        P(None, ("ctx", "tp"), None),
        P("section", None),
        P("section", None, "tp"),
        P("section", "ctx", "tp"),
        P("section", "ctx", "tp"),
        P("section", "tp", "ctx"),
        P(),
    )
    out_specs = P("section", None, ("ctx", "tp"), None)
    sizes = mesh.shape
    fits = sizes["section"] == 2 and sizes["tp"] == 2 and sizes["ctx"] == 8
    body = split_heads if fits else local
    return jax.shard_map(body, mesh=mesh, in_specs=in_specs, out_specs=out_specs, check_vma=False)
```

```python
import functools

import numpy as np
import jax
import jax.numpy as jnp
from jax import lax
from jax.experimental import pallas as pl
from jax.experimental.pallas import tpu as pltpu
from jax.sharding import PartitionSpec as P

HEAD_SIZE = 128
WINDOW = 1024
BLOCK = 128


query_scale = 168.0 ** (-0.5)
rope_base = 10000.0


def shifted(shard, axis, by):
    count = lax.axis_size(axis)
    pairs = [(i, i + by) for i in range(count) if 0 <= i + by < count]
    return lax.ppermute(shard, axis, pairs)


def rms_normed(hidden, gain_row):
    widened = hidden.astype(jnp.float32)
    mean_square = jnp.mean(widened * widened, axis=-1, keepdims=True)
    return (widened * lax.rsqrt(mean_square + 1e-06) * gain_row.astype(jnp.float32)).astype(
        jnp.bfloat16
    )


def rotary_apply(tensor, token_position):
    half_dim = tensor.shape[-1] // 2
    frequency = rope_base ** (-(jnp.arange(half_dim, dtype=jnp.float32) * 2.0) / tensor.shape[-1])
    angles = token_position.astype(jnp.float32)[:, None] * frequency[None, :]
    cosine_table = jnp.cos(angles)[:, None, :]
    sine_table = jnp.sin(angles)[:, None, :]
    first_half = tensor[..., :half_dim]
    second_half = tensor[..., half_dim:]
    return jnp.concatenate(
        [
            first_half * cosine_table - second_half * sine_table,
            second_half * cosine_table + first_half * sine_table,
        ],
        axis=-1,
    )


def doc_lookup(ids_row, token_index, block):
    block_count = ids_row.shape[0]
    start_block = jnp.sum((ids_row[None, :] < ids_row[:, None]).astype(jnp.int32), axis=1)
    block_of = jnp.clip(token_index // block, 0, block_count - 1)
    onehot = (block_of[:, None] == jnp.arange(block_count, dtype=jnp.int32)[None, :]).astype(
        jnp.int32
    )
    start_of = jnp.sum(onehot * start_block[None, :], axis=1)
    doc_of = jnp.sum(onehot * ids_row[None, :], axis=1)
    return (token_index - start_of * block, doc_of)


def attention_rows(
    grouped_heads, key_matrix_rows, value_rows, query_index, query_doc, key_index, key_doc
):
    scores = (
        jnp.einsum(
            "qgrd,kgd->grqk", grouped_heads, key_matrix_rows, preferred_element_type=jnp.float32
        )
        * query_scale
    )
    allowed = (key_index[None, :] >= 0) & (key_index[None, :] <= query_index[:, None])
    allowed = (
        allowed
        & (query_index[:, None] - key_index[None, :] < WINDOW)
        & (key_doc[None, :] == query_doc[:, None])
    )
    scores = jnp.where(allowed[None, None], scores, -1e30)
    peak_score = jnp.max(scores, axis=-1, keepdims=True)
    raised = jnp.exp(scores - peak_score)
    weights = (raised / jnp.sum(raised, axis=-1, keepdims=True)).astype(jnp.bfloat16)
    layer_result = jnp.einsum(
        "grqk,kgd->qgrd", weights, value_rows, preferred_element_type=jnp.float32
    )
    return layer_result.astype(jnp.bfloat16).reshape(grouped_heads.shape[0], -1)


def local(x_in, norm_gain, w_query, w_key, value_projection, w_out, doc_ids):
    section_num = lax.axis_index("section")
    section_count = lax.axis_size("section")
    ctx_num = lax.axis_index("ctx")
    ctx_count = lax.axis_size("ctx")
    tp_count = lax.axis_size("tp")
    micro_count, half_rows, model_width = x_in.shape
    key_full, value_full, out_part = (
        lax.all_gather(w_key, "ctx", axis=1, tiled=True),
        lax.all_gather(value_projection, "ctx", axis=1, tiled=True),
        lax.all_gather(w_out, "ctx", axis=2, tiled=True),
    )
    query_weight = w_query[0]
    key_matrix = key_full[0]
    value_matrix = value_full[0]
    out_weight = out_part[0]
    tok_rows = half_rows * tp_count
    gain_row = norm_gain[0]
    query_heads = query_weight.shape[1] // HEAD_SIZE
    kv_heads = key_matrix.shape[1] // HEAD_SIZE
    group_size = query_heads // kv_heads
    reach_hops = min(-(-WINDOW // tok_rows), ctx_count - 1)
    token_index = ctx_num * tok_rows + jnp.arange(tok_rows, dtype=jnp.int32)
    key_index = (ctx_num - reach_hops) * tok_rows + jnp.arange(
        (reach_hops + 1) * tok_rows, dtype=jnp.int32
    )

    def project(operands):
        whole_rows, token_position = operands
        normalized_input = rms_normed(whole_rows, gain_row)
        query_matrix_rows = rotary_apply(
            jnp.dot(normalized_input, query_weight, preferred_element_type=jnp.float32).reshape(
                tok_rows, query_heads, HEAD_SIZE
            ),
            token_position,
        )
        key_matrix_rows = rotary_apply(
            jnp.dot(normalized_input, key_matrix, preferred_element_type=jnp.float32).reshape(
                tok_rows, kv_heads, HEAD_SIZE
            ),
            token_position,
        )
        value_rows = jnp.dot(
            normalized_input, value_matrix, preferred_element_type=jnp.float32
        ).astype(jnp.bfloat16)
        stacked = jnp.stack(
            [
                key_matrix_rows.astype(jnp.bfloat16).reshape(tok_rows, kv_heads * HEAD_SIZE),
                value_rows,
            ]
        )
        return (
            query_matrix_rows.astype(jnp.bfloat16).reshape(tok_rows, query_heads * HEAD_SIZE),
            stacked,
        )

    def skip_project(operands):
        return (
            jnp.zeros((tok_rows, query_heads * HEAD_SIZE), jnp.bfloat16),
            jnp.zeros((2, tok_rows, kv_heads * HEAD_SIZE), jnp.bfloat16),
        )

    def skip_attend(operands):
        return jnp.zeros((tok_rows, query_heads * HEAD_SIZE), jnp.bfloat16)

    def out_local(operands):
        return jnp.dot(operands, out_weight, preferred_element_type=jnp.float32)

    def skip_out(operands):
        return jnp.zeros((operands.shape[0], out_weight.shape[1]), jnp.float32)

    def step(step_num, carry):
        received, results = carry
        micro_num = step_num - section_num
        active = (micro_num >= 0) & (micro_num < micro_count)
        micro_at = jnp.clip(micro_num, 0, micro_count - 1)
        fresh_rows = lax.dynamic_index_in_dim(x_in, micro_at, 0, keepdims=False)
        current = jnp.where(section_num == 0, fresh_rows, received)
        whole_rows = lax.all_gather(current, "tp", axis=0, tiled=True)
        ids_row = lax.dynamic_index_in_dim(doc_ids, micro_at, 0, keepdims=False)
        token_position, query_doc = doc_lookup(ids_row, token_index, BLOCK)
        unused, key_doc = doc_lookup(ids_row, key_index, BLOCK)
        query_matrix_rows, stacked = lax.cond(
            active, project, skip_project, (whole_rows, token_position)
        )
        pieces = [shifted(stacked, "ctx", distance) for distance in range(reach_hops, 0, -1)]
        window_kv = jnp.concatenate(pieces + [stacked], axis=1)

        def attend(operands):
            query_part, window_part = operands
            grouped_heads = query_part.reshape(tok_rows, kv_heads, group_size, HEAD_SIZE)
            key_matrix_rows = window_part[0].reshape(-1, kv_heads, HEAD_SIZE)
            value_rows = window_part[1].reshape(-1, kv_heads, HEAD_SIZE)
            return attention_rows(
                grouped_heads,
                key_matrix_rows,
                value_rows,
                token_index,
                query_doc,
                key_index,
                key_doc,
            )

        attended = lax.cond(active, attend, skip_attend, (query_matrix_rows, window_kv))
        summed = lax.psum_scatter(
            lax.cond(active, out_local, skip_out, attended), "tp", scatter_dimension=0, tiled=True
        )
        updated = (current.astype(jnp.float32) + summed).astype(jnp.bfloat16)
        previous = lax.dynamic_index_in_dim(results, micro_at, 0, keepdims=False)
        results = lax.dynamic_update_index_in_dim(
            results, jnp.where(active, updated, previous), micro_at, 0
        )
        received = shifted(updated, "section", 1)
        return (received, results)

    start_carry = (
        jnp.zeros((half_rows, model_width), jnp.bfloat16),
        jnp.zeros((micro_count, half_rows, model_width), jnp.bfloat16),
    )
    unused_received, results = lax.fori_loop(0, micro_count + section_count - 1, step, start_carry)
    return results[None]


SECTION, CORE, TP, CHIP = range(4)


def swapped(shard, axis):
    return lax.ppermute(shard, axis, [(0, 1), (1, 0)])


def core_swapped(shard, ctx_count):
    return lax.ppermute(shard, "ctx", [(i, i ^ 1) for i in range(ctx_count)])


def chip_xor(shard, ctx_count, by):
    return lax.ppermute(shard, "ctx", [(i, i ^ (2 * by)) for i in range(ctx_count)])


def chip_shift(shard, ctx_count, by):
    return lax.ppermute(
        shard, "ctx", [(i, i + 2 * by) for i in range(ctx_count) if i + 2 * by < ctx_count]
    )


def columns(array, block, width):
    return lax.dynamic_slice_in_dim(array, block * width, width, 1)


def own_first(flag, own, other):
    return jnp.where(flag == 0, own, other), jnp.where(flag == 0, other, own)


def together(*values):
    return lax.optimization_barrier(values)


def call(kernel, scalars, operands, outputs, scratch=(), limit=16, in_hbm=False):
    vmem = pl.BlockSpec(memory_space=pltpu.VMEM)
    smem = pl.BlockSpec(memory_space=pltpu.SMEM)
    place = pl.BlockSpec(memory_space=pltpu.HBM) if in_hbm else vmem
    return list(
        pl.pallas_call(
            kernel,
            out_shape=[jax.ShapeDtypeStruct(shape, kind) for shape, kind in outputs],
            in_specs=[smem] * len(scalars) + [place] * len(operands),
            out_specs=[vmem] * len(outputs),
            scratch_shapes=list(scratch),
            compiler_params=pltpu.CompilerParams(vmem_limit_bytes=limit * 2**20),
            cost_estimate=pl.CostEstimate(flops=1024, bytes_accessed=1024, transcendentals=0),
        )(*scalars, *operands)
    )


def aligned(index, size):
    return pl.ds(pl.multiple_of(index * size, size), size)


def pick_kernel(place, key_ref, value_ref, mine_ref, theirs_ref, sems):
    core, copies = place[CORE], []
    for out_ref, which in ((mine_ref, core), (theirs_ref, 1 - core)):
        for sec in (0, 1):
            for kind, ref in enumerate((key_ref, value_ref)):
                at = (2 * sec + kind) * HEAD_SIZE
                copies.append(
                    pltpu.make_async_copy(
                        ref.at[:, aligned(2 * sec + which, HEAD_SIZE)],
                        out_ref.at[:, at : at + HEAD_SIZE],
                        sems.at[len(copies)],
                    )
                )
    for copy in copies:
        copy.start()
    for copy in copies:
        copy.wait()


def halve_kernel(place, mine_ref, theirs_ref, gain_ref, own_ref, other_ref):
    core, section = place[CORE], place[SECTION]
    rows, pair = mine_ref.shape[0], 2 * HEAD_SIZE
    for out_ref, sec in ((own_ref, section), (other_ref, 1 - section)):
        out_ref[aligned(core, rows), :] = mine_ref[:, aligned(sec, pair)]
        out_ref[aligned(1 - core, rows), :] = theirs_ref[:, aligned(sec, pair)]
    other_ref[2 * rows :, :] = gain_ref[...]


def layers_kernel(place, own_ref, other_ref, first_ref, second_ref):
    rows = own_ref.shape[0]
    for section in (0, 1):

        @pl.when(place[SECTION] == section)
        def _():
            out_refs = (first_ref, second_ref) if section == 0 else (second_ref, first_ref)
            out_refs[0][...] = own_ref[...]
            out_refs[1][...] = other_ref[:rows, :]


def query_columns_kernel(place, weight_ref, out_ref, sems):
    copies = []
    for sec in (0, 1):
        copies.append(
            pltpu.make_async_copy(
                weight_ref.at[:, aligned(2 * sec + place[CORE], 2 * HEAD_SIZE)],
                out_ref.at[:, 2 * sec * HEAD_SIZE : (2 * sec + 2) * HEAD_SIZE],
                sems.at[sec],
            )
        )
    for copy in copies:
        copy.start()
    for copy in copies:
        copy.wait()


def late_kernel(gain_ref, query_ref, kv_ref, gain_out, query_out, kv_out):
    rows = kv_ref.shape[0] // 4
    gain = jnp.broadcast_to(gain_ref[...].astype(jnp.float32), (BLOCK, gain_ref.shape[1])).T
    for block in range(4):
        query = []
        for chip in range(4):
            at = slice((4 * chip + block) * rows, (4 * chip + block + 1) * rows)
            gain_out[block, chip * rows : (chip + 1) * rows, :] = gain[at]
            query.append(query_ref[at, :].astype(jnp.float32))
        query_out[block, :, :] = jnp.concatenate(query, axis=0).astype(jnp.bfloat16)
        lanes = slice(block * 2 * HEAD_SIZE, (block + 1) * 2 * HEAD_SIZE)
        kv_out[:, lanes] = kv_ref[block * rows : (block + 1) * rows, :]


def residual_kernel(place, own, core_, out_ref, wide):
    me = 2 * place[SECTION] + place[CORE]
    rows = out_ref.shape[1] // 4
    for micro in range(own.shape[0]):
        for by, ref in enumerate((own, core_)):
            wide[...] = ref[micro].astype(jnp.float32).T
            for chip in range(4):
                at = pl.multiple_of((4 * chip + me) * rows, 8)
                out_ref[micro, chip * rows : (chip + 1) * rows, aligned(place[CORE] ^ by, BLOCK)] = (
                    wide[pl.ds(at, rows), :]
                )


def turned(array, cosine, sine):
    return array * cosine + pltpu.roll(array, HEAD_SIZE // 2, 1) * sine


def rope_tables(inside, tables):
    row_cos, row_sin, block_cos, block_sin = tables
    cosine, sine = [], []
    count = inside.shape[0]
    for at in range(count):
        block = pl.ds(inside[at], 1)
        first, second = block_cos[block, :], block_sin[block, :]
        cosine.append(first * row_cos[...] - second * row_sin[...])
        sine.append(second * row_cos[...] + first * row_sin[...])
    lane = lax.broadcasted_iota(jnp.int32, (count * BLOCK, HEAD_SIZE), 1)
    sine = jnp.concatenate(sine, axis=0)
    return jnp.concatenate(cosine, axis=0), jnp.where(lane < HEAD_SIZE // 2, -sine, sine)


def host_tables(block_count):
    lane = np.arange(HEAD_SIZE) % (HEAD_SIZE // 2)
    frequency = rope_base ** (-(lane * 2.0) / HEAD_SIZE)
    rows = np.arange(BLOCK)[:, None] * frequency
    blocks = np.arange(block_count)[:, None] * (BLOCK * frequency)
    angles = (np.cos(rows), np.sin(rows), np.cos(blocks), np.sin(blocks))
    return [jnp.asarray(one, jnp.float32) for one in angles]


def store_queries(place, query, rope, own_ref, other_ref, row=0):
    heads = [
        turned(query[:, at : at + HEAD_SIZE], *rope).astype(jnp.bfloat16)
        for at in range(0, query.shape[1], HEAD_SIZE)
    ]
    rows = slice(row, row + query.shape[0])
    for sec in (0, 1):

        @pl.when(place[SECTION] == sec)
        def _():
            for out_ref, first in ((own_ref, 2 * sec), (other_ref, 2 - 2 * sec)):
                out_ref[rows, :HEAD_SIZE] = heads[first]
                out_ref[rows, HEAD_SIZE:] = heads[first + 1]


def store_keys(key_value, rope, out_ref, far_ref):
    size = HEAD_SIZE
    key = turned(key_value[:, :size], *rope).astype(jnp.bfloat16)
    value = key_value[:, size:].astype(jnp.bfloat16)
    out_ref[:, :size] = key
    out_ref[:, size:] = value
    for micro in range(far_ref.shape[0] // BLOCK):
        last = slice((4 * micro + 3) * BLOCK, (4 * micro + 4) * BLOCK)
        far_ref[micro * BLOCK : (micro + 1) * BLOCK, :size] = key[last]
        far_ref[micro * BLOCK : (micro + 1) * BLOCK, size:] = value[last]


def first_query_kernel(micro, place, inside, *refs):
    pieces, tables, (gain, weight), refs = refs[:4], refs[4:8], refs[8:10], refs[10:]
    normed_ref, own_ref, other_ref = refs[-3:]
    step = 16
    for by, ref in enumerate(pieces):
        at = 2 * (place[TP] ^ (by & 1)) + (place[CORE] ^ (by >> 1))
        for row in range(0, BLOCK, step):
            rows = ref[micro, row : row + step, :].astype(jnp.float32)
            mean_square = jnp.mean(rows * rows, axis=-1, keepdims=True)
            rows = rows * lax.rsqrt(mean_square + 1e-06) * gain[...].astype(jnp.float32)
            where = pl.ds(pl.multiple_of(at * BLOCK + row, step), step)
            normed_ref[where, :] = rows.astype(jnp.bfloat16)
    query = jnp.dot(normed_ref[...], weight[...], preferred_element_type=jnp.float32)
    row = micro * normed_ref.shape[0]
    if micro > 0:
        own_ref[:row, :], other_ref[:row, :] = refs[0][:row, :], refs[1][:row, :]
    store_queries(place, query, rope_tables(inside, tables), own_ref, other_ref, row)


def first_keys_kernel(place, inside, first, second, *refs):
    parts, tables, (out_ref, far_ref, weight) = refs[:4], refs[4:8], refs[8:]
    for by, ref in enumerate(parts):
        weight[aligned(place[CHIP] ^ by, ref.shape[0]), :] = ref[...]
    key_value = jnp.concatenate(
        [
            jnp.dot(one[...], weight[...], preferred_element_type=jnp.float32)
            for one in (first, second)
        ],
        axis=0,
    )
    store_keys(key_value, rope_tables(inside, tables), out_ref, far_ref)


def tn(left, right):
    return lax.dot_general(
        left, right, (((0,), (0,)), ((), ())), preferred_element_type=jnp.float32
    )


def keys_kernel(place, inside, *refs):
    pieces, tables, (gain, weight, out_ref, far_ref, normed) = refs[:8], refs[8:12], refs[12:]
    me = 2 * place[SECTION] + place[CORE]
    width, step = 4 * pieces[0].shape[0], 56
    for by_tp in (0, 1):
        for half in (0, 1):
            lanes = slice(half * BLOCK, (half + 1) * BLOCK)
            total = jnp.zeros((8, BLOCK), jnp.float32)
            for block in range(4):
                for row in range(0, width // 4, step):
                    one = pieces[2 * block + by_tp][row : row + step, lanes].astype(jnp.float32)
                    total = total + jnp.sum((one * one).reshape(-1, 8, BLOCK), axis=0)
            total = jnp.sum(total, axis=0, keepdims=True)
            scale = lax.rsqrt(total / width + 1e-06)
            at = 2 * (place[TP] ^ by_tp) + half
            for block in range(4):
                one = pieces[2 * block + by_tp][:, lanes].astype(jnp.float32)
                normed[block, :, aligned(at, BLOCK)] = (one * scale * gain[me ^ block]).astype(
                    jnp.bfloat16
                )
    key_value = sum(
        tn(normed[block], weight[:, aligned(me ^ block, 2 * HEAD_SIZE)]) for block in range(4)
    )
    store_keys(key_value, rope_tables(inside, tables), out_ref, far_ref)


def query_kernel(place, inside, normed, weight, *refs):
    tables, (own_ref, other_ref) = refs[:4], refs[4:]
    me = 2 * place[SECTION] + place[CORE]
    query = sum(tn(normed[block], weight[me ^ block]) for block in range(4))
    store_queries(place, query, rope_tables(inside, tables), own_ref, other_ref)


def attention_kernel(
    layer, place, low_ref, kept_ref, sent_ref, far_ref, near_ref, own_ref, out_ref, window_ref
):
    size = HEAD_SIZE
    span = 6 * BLOCK
    row = lax.broadcasted_iota(jnp.int32, (2 * BLOCK, span), 0) % BLOCK
    col = lax.broadcasted_iota(jnp.int32, (2 * BLOCK, span), 1)
    causal = col - 5 * BLOCK <= row
    home = place[SECTION] == layer
    for micro in range(own_ref.shape[0] // (4 * BLOCK)):
        window_ref[micro, 0:BLOCK, :] = far_ref[micro * BLOCK : (micro + 1) * BLOCK, :]
        places = [(4 * micro + at) * BLOCK for at in (0, 2, 1, 3)]
        for block, at in enumerate(places):
            window_ref[micro, (1 + block) * BLOCK : (2 + block) * BLOCK, :] = near_ref[at : at + BLOCK, :]
            window_ref[micro, (5 + block) * BLOCK : (6 + block) * BLOCK, :] = own_ref[at : at + BLOCK, :]
        for block, at in enumerate(places):
            rows = slice(block * BLOCK, (block + 6) * BLOCK)
            query = jnp.where(home, kept_ref[at : at + BLOCK, :], sent_ref[at : at + BLOCK, :])
            query = jnp.concatenate([query[:, :size], query[:, size:]], axis=0)
            scores = lax.dot_general(
                query,
                window_ref[micro, rows, 0:size],
                (((1,), (1,)), ((), ())),
                preferred_element_type=jnp.float32,
            )
            allowed = causal & (col >= low_ref[4 * micro + block] * BLOCK)
            scores = jnp.where(allowed, scores * query_scale, -1e30)
            raised = jnp.exp(scores - jnp.max(scores, axis=-1, keepdims=True))
            total = jnp.sum(raised, axis=-1, keepdims=True)
            mixed = jnp.dot(
                raised.astype(jnp.bfloat16),
                window_ref[micro, rows, size : 2 * size],
                preferred_element_type=jnp.float32,
            )
            mixed = (mixed / total).astype(jnp.bfloat16)
            out_ref[at : at + BLOCK, 0:size] = mixed[0:BLOCK]
            out_ref[at : at + BLOCK, size : 2 * size] = mixed[BLOCK:]


def gather_kernel(place, *refs):
    parts, (out_ref, wide) = refs[:4], refs[4:]
    for by, ref in enumerate(parts):
        wide[aligned(place[CHIP] ^ by, ref.shape[0]), :] = ref[...].astype(jnp.float32)
    out_ref[...] = wide[...].astype(out_ref.dtype)


def gather_near_kernel(place, own, across, below, above, far, out_ref, wide):
    chip = place[CHIP]
    one = jnp.where(chip % 2 == 0, above[...], below[...])
    three = jnp.where(chip == 1, above[...], jnp.where(chip == 2, below[...], far[...]))
    for by, rows in enumerate((own[...], one, across[...], three)):
        wide[aligned(chip ^ by, own.shape[0]), :] = rows.astype(jnp.float32)
    out_ref[...] = wide[...].astype(out_ref.dtype)


def mix_kernel(layer, place, own, core_, across, both, home, away, *out_refs):
    me = 2 * place[SECTION] + place[CORE]
    at_home = place[SECTION] == layer
    weights = []
    for by in range(4):
        lanes = aligned(me ^ by, 2 * HEAD_SIZE)
        weights.append(jnp.where(at_home, home[:, lanes], away[:, lanes]))
    for at, out_ref in enumerate(out_refs):
        half = out_ref.shape[1]
        tp = place[TP] if at % 2 == 0 else 1 - place[TP]
        total = sum(
            lax.dot_general(
                weights[by],
                ref[aligned(2 * (at // 2) + tp, half), :],
                (((1,), (1,)), ((), ())),
                preferred_element_type=jnp.float32,
            )
            for by, ref in enumerate((own, core_, across, both))
        )
        out_ref[...] = total.astype(out_ref.dtype)


def add_kernel(residual, keep, arrived, out_ref):
    total = residual[...].astype(jnp.float32) + keep[...] + arrived[...].astype(jnp.float32)
    out_ref[...] = total.astype(out_ref.dtype)


def split_heads(x_in, norm_gain, w_query, w_key, value_projection, w_out, doc_ids):
    section = lax.axis_index("section")
    ctx = lax.axis_index("ctx")
    tp = lax.axis_index("tp")
    ctx_count = lax.axis_size("ctx")
    chips = ctx_count // 2
    chip, core = ctx // 2, ctx % 2
    place = jnp.stack([section, core, tp, chip]).astype(jnp.int32)
    micro_count, half_rows, width = x_in.shape
    tokens = 4 * half_rows
    slab = width // ctx_count
    head, pair = HEAD_SIZE, 2 * HEAD_SIZE
    block_rows = width // 4
    micros = range(micro_count)
    b16, f32 = jnp.bfloat16, jnp.float32

    def up(shard):
        return chip_shift(shard, ctx_count, 1)

    def down(shard):
        return lax.ppermute(shard, "ctx", [(i, i - 2) for i in range(2, ctx_count)])

    def across_chips(shard):
        return [chip_xor(shard, ctx_count, 2), up(shard), down(shard)]

    def onward(shard):
        return lax.ppermute(shard, "ctx", [(2, 0), (3, 1), (4, 6), (5, 7)])

    def whole(kernel, parts, at=place):
        rows, columns = parts[0].shape
        return call(
            kernel,
            [at],
            parts,
            [((chips * rows, columns), b16)],
            [pltpu.VMEM((chips * rows, columns), f32)],
        )[0]

    x_tp = swapped(x_in, "tp")
    x_core = core_swapped(x_in, ctx_count)

    out_t = w_out[0].T
    kept = lax.dynamic_slice_in_dim(out_t, core * (slab // 2), slab // 2, 0)
    sent = lax.dynamic_slice_in_dim(out_t, (1 - core) * (slab // 2), slab // 2, 0)
    sent = core_swapped(sent, ctx_count)
    at_home = core == section
    own_half, cross_half = jnp.where(at_home, kept, sent), jnp.where(at_home, sent, kept)
    own_half, later = together(own_half, place)
    own_parts = across_chips(own_half)

    mine, theirs = call(
        pick_kernel,
        [later],
        [w_key[0], value_projection[0]],
        [((slab, 2 * pair), b16)] * 2,
        [pltpu.SemaphoreType.DMA((8,))],
        in_hbm=True,
    )
    theirs = core_swapped(theirs, ctx_count)
    gain_rows = jnp.pad(norm_gain[0], (0, 16 * pair - width)).reshape(16, pair)
    kv_own, kv_other = call(
        halve_kernel,
        [place],
        [mine, theirs, gain_rows],
        [((2 * slab, pair), b16), ((2 * slab + 16, pair), b16)],
    )
    kv_other = swapped(kv_other, "section")

    *own_parts, kv_other = together(*own_parts, kv_other)
    own_far = onward(own_parts[0])
    gain_other = kv_other[2 * slab :].reshape(-1)[:width]
    gains = own_first(section, norm_gain[0], gain_other)
    kv_shards = call(
        layers_kernel, [place], [kv_own, kv_other], [((2 * slab, pair), b16)] * 2
    )
    kv_parts = [chip_xor(kv_shards[0], ctx_count, by) for by in range(1, chips)]

    start = jnp.sum((doc_ids[:, None, :] < doc_ids[:, :, None]).astype(jnp.int32), axis=2)
    chip_start = lax.dynamic_slice_in_dim(start, chip * 4, 4, 1)
    inside = chip * 4 + jnp.arange(4, dtype=jnp.int32)[None, :] - chip_start
    lows = 5 - inside
    order = inside.reshape(micro_count, 2, 2).transpose(0, 2, 1).reshape(micro_count, 4)
    tables = host_tables(doc_ids.shape[1])

    def by_block(weight):
        columns = weight.shape[1]
        weight = weight.reshape(chips, 4, slab // 2, columns).transpose(1, 0, 2, 3)
        return weight.reshape(4, block_rows, columns)

    def shifted(key_value, far):
        return chip_shift(key_value, ctx_count, 1), chip_shift(far, ctx_count, 2)

    def attend(layer, low, query, key_value, window):
        own, other = query
        sent = lax.ppermute(other, "section", [(layer, 1 - layer)])
        near, far = window
        return call(
            functools.partial(attention_kernel, layer),
            [place, low],
            [own, sent, far, near, key_value],
            [(own.shape, b16)],
            [pltpu.VMEM((own.shape[0] // tokens, 9 * BLOCK, pair), b16)],
        )[0]

    def mix(layer, attended, across):
        shape = (block_rows, tokens // 2)
        return call(
            functools.partial(mix_kernel, layer),
            [place],
            [
                attended,
                core_swapped(attended, ctx_count),
                across,
                core_swapped(across, ctx_count),
                home_out,
                away_out,
            ],
            [(shape, f32), (shape, b16)] * (attended.shape[0] // tokens),
            )

    def add(residual, keep, send):
        return call(add_kernel, [], [residual, keep, swapped(send, "tp")], [(send.shape, b16)])[0]

    def spread(piece):
        over_tp, over_section = swapped(piece, "tp"), swapped(piece, "section")
        over_both = lax.ppermute(piece, ("section", "tp"), [(i, 3 - i) for i in range(4)])
        return [piece, over_tp, over_section, over_both]

    def both_cores(pieces):
        over = [core_swapped(one, ctx_count) for one in pieces]
        return pieces[:2] + over[:2] + pieces[2:] + over[2:]

    def in_order(blocks):
        by_section = [own_first(core, blocks[0], blocks[1]), own_first(core, blocks[2], blocks[3])]
        low = own_first(section, by_section[0][0], by_section[1][0])
        high = own_first(section, by_section[0][1], by_section[1][1])
        whole = jnp.stack([low[0], high[0], low[1], high[1]])
        count = whole.shape[-1]
        whole = whole.reshape(4, chips, slab // 2, count).transpose(1, 0, 2, 3)
        return whole.reshape(width, count)

    cross_half, kv_shard = together(cross_half, kv_shards[1])
    cross_half = swapped(cross_half, "section")
    x_tp, kv_shard, later = together(x_tp, kv_shard, place)
    query_weight = call(
        query_columns_kernel,
        [later],
        [w_query[0]],
        [((width, 2 * pair), b16)],
        [pltpu.SemaphoreType.DMA((2,))],
        in_hbm=True,
    )[0]
    x_both = core_swapped(x_tp, ctx_count)
    rows = (micro_count * tokens, pair)
    normed, query = [], []
    for micro in micros:
        one, *query = call(
            functools.partial(first_query_kernel, micro),
            [place, order[micro]],
            [x_in, x_tp, x_core, x_both, *tables, gains[0][None], query_weight, *query],
            [((tokens, width), b16), (rows, b16), (rows, b16)],
        )
        normed.append(one)
    (residuals,) = call(
        residual_kernel,
        [place],
        [x_in, x_core],
        [((micro_count, block_rows, tokens // 2), f32)],
        [pltpu.VMEM((width, BLOCK), f32)],
    )
    *kv_parts, cross_half, normed[0], normed[1], residuals = together(
        *kv_parts, cross_half, *normed, residuals
    )
    key, far = call(
        first_keys_kernel,
        [place, order.reshape(-1)],
        [*normed, kv_shards[0], *kv_parts, *tables],
        [(rows, b16), ((micro_count * BLOCK, pair), b16)],
        [pltpu.VMEM((width, pair), b16)],
    )
    window = shifted(key, far)

    key, cross_half, later, own_far = together(key, cross_half, place, own_far)
    other_parts = [chip_xor(cross_half, ctx_count, by) for by in range(1, chips)]
    home_out = whole(gather_near_kernel, [own_half, *own_parts, own_far], later)
    other_parts[1], low = together(other_parts[1], lows.reshape(-1))
    attended = attend(0, low, query, key, window)
    across = swapped(attended, "section")
    *other_parts, across = together(*other_parts, across)
    away_out = whole(gather_kernel, [cross_half, *other_parts])
    late_gain, late_query_weight, kv_shard = call(
        late_kernel,
        [],
        [gains[1][None], query_weight, kv_shard],
        [
            ((4, block_rows, BLOCK), f32),
            ((4, block_rows, 2 * pair), b16),
            ((slab // 2, 4 * pair), b16),
        ],
    )
    mixed = mix(0, attended, across)
    mixed[1], mixed[3], kv_shard = together(mixed[1], mixed[3], kv_shard)
    kv_parts = [chip_xor(kv_shard, ctx_count, by) for by in range(1, chips)]
    halves = [add(residuals[m], *mixed[2 * m : 2 * m + 2]) for m in micros]
    spreads = [spread(one) for one in halves]
    spreads[0][1:], kv_parts = (lambda got: (got[:3], got[3:]))(
        together(*spreads[0][1:], *kv_parts)
    )

    next_kv = whole(gather_kernel, [kv_shard, *kv_parts])
    pieces, queries, keys, windows = [], [], [], []
    for micro in micros:
        pieces.append(both_cores(spreads[micro]))
        key_value, far, normed = call(
            keys_kernel,
            [place, order[micro]],
            [*pieces[micro], *tables, late_gain, next_kv],
            [((tokens, pair), b16), ((BLOCK, pair), b16), ((4, block_rows, tokens), b16)],
        )
        windows.append(shifted(key_value, far))
        normed, key_value = together(normed, key_value)
        query = call(
            query_kernel,
            [place, order[micro]],
            [normed, late_query_weight, *tables],
            [((tokens, pair), b16)] * 2,
        )
        queries.append(query)
        keys.append(key_value)
        if micro == 0:
            query[0], *spreads[1] = together(query[0], *spreads[1])
    queries[1][0], keys[0] = together(queries[1][0], keys[0])
    attended = [attend(1, lows[m], queries[m], keys[m], windows[m]) for m in micros]
    across = [swapped(one, "section") for one in attended]
    mixed = [mix(1, attended[0], across[0])]
    mixed[0][0], across[1] = together(mixed[0][0], across[1])
    mixed.append(mix(1, attended[1], across[1]))
    results = [
        jnp.stack(
            [in_order([columns(one[2 * i], core, BLOCK) for i in range(4)]).T for one in pieces]
        )
    ]
    last = []
    for micro in micros:
        piece = add(halves[micro], *mixed[micro])
        blocks = []
        for one in (piece, lax.ppermute(piece, "section", [(0, 1)])):
            kept, passed = own_first(core, one[:, :BLOCK], one[:, BLOCK:])
            blocks += [kept, core_swapped(passed, ctx_count)]
        last.append(in_order(blocks).T)
    results.append(jnp.stack(last))
    return jnp.where(section == 0, results[0], results[1])[None]


def solution(mesh):
    in_specs = (
        P(None, ("ctx", "tp"), None),
        P("section", None),
        P("section", None, "tp"),
        P("section", "ctx", "tp"),
        P("section", "ctx", "tp"),
        P("section", "tp", "ctx"),
        P(),
    )
    out_specs = P("section", None, ("ctx", "tp"), None)
    sizes = mesh.shape
    fits = sizes["section"] == 2 and sizes["tp"] == 2 and sizes["ctx"] == 8
    body = split_heads if fits else local
    return jax.shard_map(body, mesh=mesh, in_specs=in_specs, out_specs=out_specs, check_vma=False)
```

```python
import functools

import numpy as np
import jax
import jax.numpy as jnp
from jax import lax
from jax.experimental import pallas as pl
from jax.experimental.pallas import tpu as pltpu
from jax.sharding import PartitionSpec as P

HEAD_SIZE = 128
WINDOW = 1024
BLOCK = 128


query_scale = 168.0 ** (-0.5)
rope_base = 10000.0


def shifted(shard, axis, by):
    count = lax.axis_size(axis)
    pairs = [(i, i + by) for i in range(count) if 0 <= i + by < count]
    return lax.ppermute(shard, axis, pairs)


def rms_normed(hidden, gain_row):
    widened = hidden.astype(jnp.float32)
    mean_square = jnp.mean(widened * widened, axis=-1, keepdims=True)
    return (widened * lax.rsqrt(mean_square + 1e-06) * gain_row.astype(jnp.float32)).astype(
        jnp.bfloat16
    )


def rotary_apply(tensor, token_position):
    half_dim = tensor.shape[-1] // 2
    frequency = rope_base ** (-(jnp.arange(half_dim, dtype=jnp.float32) * 2.0) / tensor.shape[-1])
    angles = token_position.astype(jnp.float32)[:, None] * frequency[None, :]
    cosine_table = jnp.cos(angles)[:, None, :]
    sine_table = jnp.sin(angles)[:, None, :]
    first_half = tensor[..., :half_dim]
    second_half = tensor[..., half_dim:]
    return jnp.concatenate(
        [
            first_half * cosine_table - second_half * sine_table,
            second_half * cosine_table + first_half * sine_table,
        ],
        axis=-1,
    )


def doc_lookup(ids_row, token_index, block):
    block_count = ids_row.shape[0]
    start_block = jnp.sum((ids_row[None, :] < ids_row[:, None]).astype(jnp.int32), axis=1)
    block_of = jnp.clip(token_index // block, 0, block_count - 1)
    onehot = (block_of[:, None] == jnp.arange(block_count, dtype=jnp.int32)[None, :]).astype(
        jnp.int32
    )
    start_of = jnp.sum(onehot * start_block[None, :], axis=1)
    doc_of = jnp.sum(onehot * ids_row[None, :], axis=1)
    return (token_index - start_of * block, doc_of)


def attention_rows(
    grouped_heads, key_matrix_rows, value_rows, query_index, query_doc, key_index, key_doc
):
    scores = (
        jnp.einsum(
            "qgrd,kgd->grqk", grouped_heads, key_matrix_rows, preferred_element_type=jnp.float32
        )
        * query_scale
    )
    allowed = (key_index[None, :] >= 0) & (key_index[None, :] <= query_index[:, None])
    allowed = (
        allowed
        & (query_index[:, None] - key_index[None, :] < WINDOW)
        & (key_doc[None, :] == query_doc[:, None])
    )
    scores = jnp.where(allowed[None, None], scores, -1e30)
    peak_score = jnp.max(scores, axis=-1, keepdims=True)
    raised = jnp.exp(scores - peak_score)
    weights = (raised / jnp.sum(raised, axis=-1, keepdims=True)).astype(jnp.bfloat16)
    layer_result = jnp.einsum(
        "grqk,kgd->qgrd", weights, value_rows, preferred_element_type=jnp.float32
    )
    return layer_result.astype(jnp.bfloat16).reshape(grouped_heads.shape[0], -1)


def local(x_in, norm_gain, w_query, w_key, value_projection, w_out, doc_ids):
    section_num = lax.axis_index("section")
    section_count = lax.axis_size("section")
    ctx_num = lax.axis_index("ctx")
    ctx_count = lax.axis_size("ctx")
    tp_count = lax.axis_size("tp")
    micro_count, half_rows, model_width = x_in.shape
    key_full, value_full, out_part = (
        lax.all_gather(w_key, "ctx", axis=1, tiled=True),
        lax.all_gather(value_projection, "ctx", axis=1, tiled=True),
        lax.all_gather(w_out, "ctx", axis=2, tiled=True),
    )
    query_weight = w_query[0]
    key_matrix = key_full[0]
    value_matrix = value_full[0]
    out_weight = out_part[0]
    tok_rows = half_rows * tp_count
    gain_row = norm_gain[0]
    query_heads = query_weight.shape[1] // HEAD_SIZE
    kv_heads = key_matrix.shape[1] // HEAD_SIZE
    group_size = query_heads // kv_heads
    reach_hops = min(-(-WINDOW // tok_rows), ctx_count - 1)
    token_index = ctx_num * tok_rows + jnp.arange(tok_rows, dtype=jnp.int32)
    key_index = (ctx_num - reach_hops) * tok_rows + jnp.arange(
        (reach_hops + 1) * tok_rows, dtype=jnp.int32
    )

    def project(operands):
        whole_rows, token_position = operands
        normalized_input = rms_normed(whole_rows, gain_row)
        query_matrix_rows = rotary_apply(
            jnp.dot(normalized_input, query_weight, preferred_element_type=jnp.float32).reshape(
                tok_rows, query_heads, HEAD_SIZE
            ),
            token_position,
        )
        key_matrix_rows = rotary_apply(
            jnp.dot(normalized_input, key_matrix, preferred_element_type=jnp.float32).reshape(
                tok_rows, kv_heads, HEAD_SIZE
            ),
            token_position,
        )
        value_rows = jnp.dot(
            normalized_input, value_matrix, preferred_element_type=jnp.float32
        ).astype(jnp.bfloat16)
        stacked = jnp.stack(
            [
                key_matrix_rows.astype(jnp.bfloat16).reshape(tok_rows, kv_heads * HEAD_SIZE),
                value_rows,
            ]
        )
        return (
            query_matrix_rows.astype(jnp.bfloat16).reshape(tok_rows, query_heads * HEAD_SIZE),
            stacked,
        )

    def skip_project(operands):
        return (
            jnp.zeros((tok_rows, query_heads * HEAD_SIZE), jnp.bfloat16),
            jnp.zeros((2, tok_rows, kv_heads * HEAD_SIZE), jnp.bfloat16),
        )

    def skip_attend(operands):
        return jnp.zeros((tok_rows, query_heads * HEAD_SIZE), jnp.bfloat16)

    def out_local(operands):
        return jnp.dot(operands, out_weight, preferred_element_type=jnp.float32)

    def skip_out(operands):
        return jnp.zeros((operands.shape[0], out_weight.shape[1]), jnp.float32)

    def step(step_num, carry):
        received, results = carry
        micro_num = step_num - section_num
        active = (micro_num >= 0) & (micro_num < micro_count)
        micro_at = jnp.clip(micro_num, 0, micro_count - 1)
        fresh_rows = lax.dynamic_index_in_dim(x_in, micro_at, 0, keepdims=False)
        current = jnp.where(section_num == 0, fresh_rows, received)
        whole_rows = lax.all_gather(current, "tp", axis=0, tiled=True)
        ids_row = lax.dynamic_index_in_dim(doc_ids, micro_at, 0, keepdims=False)
        token_position, query_doc = doc_lookup(ids_row, token_index, BLOCK)
        unused, key_doc = doc_lookup(ids_row, key_index, BLOCK)
        query_matrix_rows, stacked = lax.cond(
            active, project, skip_project, (whole_rows, token_position)
        )
        pieces = [shifted(stacked, "ctx", distance) for distance in range(reach_hops, 0, -1)]
        window_kv = jnp.concatenate(pieces + [stacked], axis=1)

        def attend(operands):
            query_part, window_part = operands
            grouped_heads = query_part.reshape(tok_rows, kv_heads, group_size, HEAD_SIZE)
            key_matrix_rows = window_part[0].reshape(-1, kv_heads, HEAD_SIZE)
            value_rows = window_part[1].reshape(-1, kv_heads, HEAD_SIZE)
            return attention_rows(
                grouped_heads,
                key_matrix_rows,
                value_rows,
                token_index,
                query_doc,
                key_index,
                key_doc,
            )

        attended = lax.cond(active, attend, skip_attend, (query_matrix_rows, window_kv))
        summed = lax.psum_scatter(
            lax.cond(active, out_local, skip_out, attended), "tp", scatter_dimension=0, tiled=True
        )
        updated = (current.astype(jnp.float32) + summed).astype(jnp.bfloat16)
        previous = lax.dynamic_index_in_dim(results, micro_at, 0, keepdims=False)
        results = lax.dynamic_update_index_in_dim(
            results, jnp.where(active, updated, previous), micro_at, 0
        )
        received = shifted(updated, "section", 1)
        return (received, results)

    start_carry = (
        jnp.zeros((half_rows, model_width), jnp.bfloat16),
        jnp.zeros((micro_count, half_rows, model_width), jnp.bfloat16),
    )
    unused_received, results = lax.fori_loop(0, micro_count + section_count - 1, step, start_carry)
    return results[None]


SECTION, CORE, TP, CHIP = range(4)


def swapped(shard, axis):
    return lax.ppermute(shard, axis, [(0, 1), (1, 0)])


def core_swapped(shard, ctx_count):
    return lax.ppermute(shard, "ctx", [(i, i ^ 1) for i in range(ctx_count)])


def chip_xor(shard, ctx_count, by):
    return lax.ppermute(shard, "ctx", [(i, i ^ (2 * by)) for i in range(ctx_count)])


def chip_shift(shard, ctx_count, by):
    return lax.ppermute(
        shard, "ctx", [(i, i + 2 * by) for i in range(ctx_count) if i + 2 * by < ctx_count]
    )


def columns(array, block, width):
    return lax.dynamic_slice_in_dim(array, block * width, width, 1)


def own_first(flag, own, other):
    return jnp.where(flag == 0, own, other), jnp.where(flag == 0, other, own)


def together(*values):
    return lax.optimization_barrier(values)


def call(kernel, scalars, operands, outputs, scratch=(), limit=16, in_hbm=False):
    vmem = pl.BlockSpec(memory_space=pltpu.VMEM)
    smem = pl.BlockSpec(memory_space=pltpu.SMEM)
    place = pl.BlockSpec(memory_space=pltpu.HBM) if in_hbm else vmem
    return list(
        pl.pallas_call(
            kernel,
            out_shape=[jax.ShapeDtypeStruct(shape, kind) for shape, kind in outputs],
            in_specs=[smem] * len(scalars) + [place] * len(operands),
            out_specs=[vmem] * len(outputs),
            scratch_shapes=list(scratch),
            compiler_params=pltpu.CompilerParams(vmem_limit_bytes=limit * 2**20),
            cost_estimate=pl.CostEstimate(flops=1024, bytes_accessed=1024, transcendentals=0),
        )(*scalars, *operands)
    )


def aligned(index, size):
    return pl.ds(pl.multiple_of(index * size, size), size)


def pick_kernel(place, key_ref, value_ref, mine_ref, theirs_ref, sems):
    core, copies = place[CORE], []
    for out_ref, which in ((mine_ref, core), (theirs_ref, 1 - core)):
        for sec in (0, 1):
            for kind, ref in enumerate((key_ref, value_ref)):
                at = (2 * sec + kind) * HEAD_SIZE
                copies.append(
                    pltpu.make_async_copy(
                        ref.at[:, aligned(2 * sec + which, HEAD_SIZE)],
                        out_ref.at[:, at : at + HEAD_SIZE],
                        sems.at[len(copies)],
                    )
                )
    for copy in copies:
        copy.start()
    for copy in copies:
        copy.wait()


def halve_kernel(place, mine_ref, theirs_ref, gain_ref, own_ref, other_ref):
    core, section = place[CORE], place[SECTION]
    rows, pair = mine_ref.shape[0], 2 * HEAD_SIZE
    for out_ref, sec in ((own_ref, section), (other_ref, 1 - section)):
        out_ref[aligned(core, rows), :] = mine_ref[:, aligned(sec, pair)]
        out_ref[aligned(1 - core, rows), :] = theirs_ref[:, aligned(sec, pair)]
    other_ref[2 * rows :, :] = gain_ref[...]


def layers_kernel(place, own_ref, other_ref, first_ref, second_ref):
    rows = own_ref.shape[0]
    for section in (0, 1):

        @pl.when(place[SECTION] == section)
        def _():
            out_refs = (first_ref, second_ref) if section == 0 else (second_ref, first_ref)
            out_refs[0][...] = own_ref[...]
            out_refs[1][...] = other_ref[:rows, :]


def query_columns_kernel(place, weight_ref, out_ref, sems):
    copies = []
    for sec in (0, 1):
        copies.append(
            pltpu.make_async_copy(
                weight_ref.at[:, aligned(2 * sec + place[CORE], 2 * HEAD_SIZE)],
                out_ref.at[:, 2 * sec * HEAD_SIZE : (2 * sec + 2) * HEAD_SIZE],
                sems.at[sec],
            )
        )
    for copy in copies:
        copy.start()
    for copy in copies:
        copy.wait()


def late_kernel(place, gain_ref, query_ref, *refs):
    home, away, (gain_out, query_out, kv_out, wide) = refs[:5], refs[5:9], refs[9:]
    rows = home[0].shape[0] // 4
    at_home = place[SECTION] == 1
    gain = jnp.broadcast_to(gain_ref[...].astype(jnp.float32), (BLOCK, gain_ref.shape[1])).T
    for by, part in enumerate(by_chip(place, home)):
        part = jnp.where(at_home, part, away[by][...]).astype(jnp.float32)
        for block in range(4):
            lanes = slice(block * 2 * HEAD_SIZE, (block + 1) * 2 * HEAD_SIZE)
            wide[aligned(place[CHIP] ^ by, rows), lanes] = part[block * rows : (block + 1) * rows]
    kv_out[...] = wide[...].astype(jnp.bfloat16)
    for block in range(4):
        query = []
        for chip in range(4):
            at = slice((4 * chip + block) * rows, (4 * chip + block + 1) * rows)
            gain_out[block, chip * rows : (chip + 1) * rows, :] = gain[at]
            query.append(query_ref[at, :].astype(jnp.float32))
        query_out[block, :, :] = jnp.concatenate(query, axis=0).astype(jnp.bfloat16)


def residual_kernel(place, own, tp_, core_, both, out_ref, wide):
    me = 2 * place[SECTION] + place[TP]
    rows = out_ref.shape[1] // 4
    at_home = place[CORE] == place[TP]
    for micro in range(own.shape[0]):
        for by, refs in enumerate(((own, tp_), (core_, both))):
            piece = jnp.where(at_home, refs[0][micro], refs[1][micro])
            wide[...] = piece.astype(jnp.float32).T
            for chip in range(4):
                at = pl.multiple_of((4 * chip + me) * rows, 8)
                out_ref[micro, chip * rows : (chip + 1) * rows, aligned(place[CORE] ^ by, BLOCK)] = (
                    wide[pl.ds(at, rows), :]
                )


def heads_kernel(place, slab_ref, kept_ref, sent_ref):
    pair = 2 * HEAD_SIZE
    for ref, core in ((kept_ref, place[CORE]), (sent_ref, 1 - place[CORE])):
        for sec in (0, 1):
            ref[:, sec * pair : (sec + 1) * pair] = slab_ref[:, aligned(2 * sec + core, pair)]


def halves_kernel(place, own_ref, other_ref, kept_ref, sent_ref, wide):
    rows = kept_ref.shape[1]
    for slab, ref in enumerate((own_ref, other_ref)):
        wide[...] = ref[...].astype(jnp.float32)
        for out_ref, tp in ((kept_ref, place[TP]), (sent_ref, 1 - place[TP])):
            out_ref[slab] = wide[pl.ds(pl.multiple_of(tp * rows, 8), rows), :].astype(out_ref.dtype)


def join_kernel(place, kept_ref, got_ref, home_ref, cross_ref):
    lanes = kept_ref.shape[2]
    slab = place[CORE] ^ place[SECTION]
    for ref, which in ((home_ref, slab), (cross_ref, 1 - slab)):
        ref[:, aligned(place[TP], lanes)] = kept_ref[which]
        ref[:, aligned(1 - place[TP], lanes)] = got_ref[which]


def turned(array, cosine, sine):
    return array * cosine + pltpu.roll(array, HEAD_SIZE // 2, 1) * sine


def rope_tables(inside, tables):
    row_cos, row_sin, block_cos, block_sin = tables
    cosine, sine = [], []
    count = inside.shape[0]
    for at in range(count):
        block = pl.ds(inside[at], 1)
        first, second = block_cos[block, :], block_sin[block, :]
        cosine.append(first * row_cos[...] - second * row_sin[...])
        sine.append(second * row_cos[...] + first * row_sin[...])
    lane = lax.broadcasted_iota(jnp.int32, (count * BLOCK, HEAD_SIZE), 1)
    sine = jnp.concatenate(sine, axis=0)
    return jnp.concatenate(cosine, axis=0), jnp.where(lane < HEAD_SIZE // 2, -sine, sine)


def host_tables(block_count):
    lane = np.arange(HEAD_SIZE) % (HEAD_SIZE // 2)
    frequency = rope_base ** (-(lane * 2.0) / HEAD_SIZE)
    rows = np.arange(BLOCK)[:, None] * frequency
    blocks = np.arange(block_count)[:, None] * (BLOCK * frequency)
    angles = (np.cos(rows), np.sin(rows), np.cos(blocks), np.sin(blocks))
    return [jnp.asarray(one, jnp.float32) for one in angles]


def store_queries(place, query, rope, own_ref, other_ref, row=0):
    heads = [
        turned(query[:, at : at + HEAD_SIZE], *rope).astype(jnp.bfloat16)
        for at in range(0, query.shape[1], HEAD_SIZE)
    ]
    rows = slice(row, row + query.shape[0])
    for sec in (0, 1):

        @pl.when(place[SECTION] == sec)
        def _():
            for out_ref, first in ((own_ref, 2 * sec), (other_ref, 2 - 2 * sec)):
                out_ref[rows, :HEAD_SIZE] = heads[first]
                out_ref[rows, HEAD_SIZE:] = heads[first + 1]


def store_keys(key_value, rope, out_ref, far_ref):
    size = HEAD_SIZE
    key = turned(key_value[:, :size], *rope).astype(jnp.bfloat16)
    value = key_value[:, size:].astype(jnp.bfloat16)
    out_ref[:, :size] = key
    out_ref[:, size:] = value
    for micro in range(far_ref.shape[0] // BLOCK):
        last = slice((4 * micro + 3) * BLOCK, (4 * micro + 4) * BLOCK)
        far_ref[micro * BLOCK : (micro + 1) * BLOCK, :size] = key[last]
        far_ref[micro * BLOCK : (micro + 1) * BLOCK, size:] = value[last]


def first_query_kernel(micro, place, inside, *refs):
    pieces, tables, (gain, weight), refs = refs[:4], refs[4:8], refs[8:10], refs[10:]
    normed_ref, own_ref, other_ref = refs[-3:]
    step = 16
    for by, ref in enumerate(pieces):
        at = 2 * (place[TP] ^ (by & 1)) + (place[CORE] ^ (by >> 1))
        for row in range(0, BLOCK, step):
            rows = ref[micro, row : row + step, :].astype(jnp.float32)
            mean_square = jnp.mean(rows * rows, axis=-1, keepdims=True)
            rows = rows * lax.rsqrt(mean_square + 1e-06) * gain[...].astype(jnp.float32)
            where = pl.ds(pl.multiple_of(at * BLOCK + row, step), step)
            normed_ref[where, :] = rows.astype(jnp.bfloat16)
    query = jnp.dot(normed_ref[...], weight[...], preferred_element_type=jnp.float32)
    row = micro * normed_ref.shape[0]
    if micro > 0:
        own_ref[:row, :], other_ref[:row, :] = refs[0][:row, :], refs[1][:row, :]
    store_queries(place, query, rope_tables(inside, tables), own_ref, other_ref, row)


def by_chip(place, refs):
    own, across, below, above, far = [ref[...] for ref in refs]
    chip = place[CHIP]
    one = jnp.where(chip % 2 == 0, above, below)
    three = jnp.where(chip == 1, above, jnp.where(chip == 2, below, far))
    return own, one, across, three


def first_keys_kernel(place, inside, first, second, *refs):
    home, away, tables, (out_ref, far_ref, weight) = refs[:5], refs[5:9], refs[9:13], refs[13:]
    at_home = place[SECTION] == 0
    for by, rows in enumerate(by_chip(place, home)):
        rows = jnp.where(at_home, rows, away[by][...])
        weight[aligned(place[CHIP] ^ by, rows.shape[0]), :] = rows
    key_value = jnp.concatenate(
        [
            jnp.dot(one[...], weight[...], preferred_element_type=jnp.float32)
            for one in (first, second)
        ],
        axis=0,
    )
    store_keys(key_value, rope_tables(inside, tables), out_ref, far_ref)


def tn(left, right):
    return lax.dot_general(
        left, right, (((0,), (0,)), ((), ())), preferred_element_type=jnp.float32
    )


def keys_kernel(place, inside, *refs):
    pieces, tables, (gain, weight, out_ref, far_ref, normed) = refs[:8], refs[8:12], refs[12:]
    me = 2 * place[SECTION] + place[TP]
    width, step = 4 * pieces[0].shape[0], 56
    for by_core in (0, 1):
        for half in (0, 1):
            lanes = slice(half * BLOCK, (half + 1) * BLOCK)
            total = jnp.zeros((8, BLOCK), jnp.float32)
            for block in range(4):
                for row in range(0, width // 4, step):
                    one = pieces[2 * block + by_core][row : row + step, lanes].astype(jnp.float32)
                    total = total + jnp.sum((one * one).reshape(-1, 8, BLOCK), axis=0)
            total = jnp.sum(total, axis=0, keepdims=True)
            scale = lax.rsqrt(total / width + 1e-06)
            at = 2 * (place[CORE] ^ by_core) + half
            for block in range(4):
                one = pieces[2 * block + by_core][:, lanes].astype(jnp.float32)
                normed[block, :, aligned(at, BLOCK)] = (one * scale * gain[me ^ block]).astype(
                    jnp.bfloat16
                )
    key_value = sum(
        tn(normed[block], weight[:, aligned(me ^ block, 2 * HEAD_SIZE)]) for block in range(4)
    )
    store_keys(key_value, rope_tables(inside, tables), out_ref, far_ref)


def query_kernel(place, inside, normed, weight, *refs):
    tables, (own_ref, other_ref) = refs[:4], refs[4:]
    me = 2 * place[SECTION] + place[TP]
    query = sum(tn(normed[block], weight[me ^ block]) for block in range(4))
    store_queries(place, query, rope_tables(inside, tables), own_ref, other_ref)


def attention_kernel(
    layer, place, low_ref, kept_ref, sent_ref, far_ref, near_ref, own_ref, out_ref, window_ref
):
    size = HEAD_SIZE
    span = 6 * BLOCK
    row = lax.broadcasted_iota(jnp.int32, (2 * BLOCK, span), 0) % BLOCK
    col = lax.broadcasted_iota(jnp.int32, (2 * BLOCK, span), 1)
    causal = col - 5 * BLOCK <= row
    home = place[SECTION] == layer
    for micro in range(own_ref.shape[0] // (4 * BLOCK)):
        window_ref[micro, 0:BLOCK, :] = far_ref[micro * BLOCK : (micro + 1) * BLOCK, :]
        places = [(4 * micro + at) * BLOCK for at in (0, 2, 1, 3)]
        for block, at in enumerate(places):
            window_ref[micro, (1 + block) * BLOCK : (2 + block) * BLOCK, :] = near_ref[at : at + BLOCK, :]
            window_ref[micro, (5 + block) * BLOCK : (6 + block) * BLOCK, :] = own_ref[at : at + BLOCK, :]
        for block, at in enumerate(places):
            rows = slice(block * BLOCK, (block + 6) * BLOCK)
            query = jnp.where(home, kept_ref[at : at + BLOCK, :], sent_ref[at : at + BLOCK, :])
            query = jnp.concatenate([query[:, :size], query[:, size:]], axis=0)
            scores = lax.dot_general(
                query,
                window_ref[micro, rows, 0:size],
                (((1,), (1,)), ((), ())),
                preferred_element_type=jnp.float32,
            )
            allowed = causal & (col >= low_ref[4 * micro + block] * BLOCK)
            scores = jnp.where(allowed, scores * query_scale, -1e30)
            raised = jnp.exp(scores - jnp.max(scores, axis=-1, keepdims=True))
            total = jnp.sum(raised, axis=-1, keepdims=True)
            mixed = jnp.dot(
                raised.astype(jnp.bfloat16),
                window_ref[micro, rows, size : 2 * size],
                preferred_element_type=jnp.float32,
            )
            mixed = (mixed / total).astype(jnp.bfloat16)
            out_ref[at : at + BLOCK, 0:size] = mixed[0:BLOCK]
            out_ref[at : at + BLOCK, size : 2 * size] = mixed[BLOCK:]


def gather_kernel(place, *refs):
    parts, (out_ref, wide) = refs[:4], refs[4:]
    for by, ref in enumerate(parts):
        wide[aligned(place[CHIP] ^ by, ref.shape[0]), :] = ref[...].astype(jnp.float32)
    out_ref[...] = wide[...].astype(out_ref.dtype)


def mix_kernel(place, own, section_, tp_, both, weight, *out_refs):
    me = 2 * place[TP] + place[SECTION]
    weights = [weight[:, aligned(me ^ by, 2 * HEAD_SIZE)] for by in range(4)]
    for at, out_ref in enumerate(out_refs):
        half = out_ref.shape[1]
        core = place[CORE] if at % 2 == 0 else 1 - place[CORE]
        total = sum(
            lax.dot_general(
                weights[by],
                ref[aligned(2 * (at // 2) + core, half), :],
                (((1,), (1,)), ((), ())),
                preferred_element_type=jnp.float32,
            )
            for by, ref in enumerate((own, section_, tp_, both))
        )
        out_ref[...] = total.astype(out_ref.dtype)


def add_kernel(residual, keep, arrived, out_ref):
    total = residual[...].astype(jnp.float32) + keep[...] + arrived[...].astype(jnp.float32)
    out_ref[...] = total.astype(out_ref.dtype)


def split_heads(x_in, norm_gain, w_query, w_key, value_projection, w_out, doc_ids):
    section = lax.axis_index("section")
    ctx = lax.axis_index("ctx")
    tp = lax.axis_index("tp")
    ctx_count = lax.axis_size("ctx")
    chips = ctx_count // 2
    chip, core = ctx // 2, ctx % 2
    place = jnp.stack([section, core, tp, chip]).astype(jnp.int32)
    micro_count, half_rows, width = x_in.shape
    tokens = 4 * half_rows
    slab = width // ctx_count
    head, pair = HEAD_SIZE, 2 * HEAD_SIZE
    block_rows = width // 4
    micros = range(micro_count)
    b16, f32 = jnp.bfloat16, jnp.float32

    def across_chips(shard):
        return [chip_xor(shard, ctx_count, by) for by in range(1, chips)]

    def whole(parts):
        rows, columns = parts[0].shape
        return call(
            gather_kernel,
            [place],
            parts,
            [((chips * rows, columns), b16)],
            [pltpu.VMEM((chips * rows, columns), f32)],
        )[0]

    x_tp = swapped(x_in, "tp")
    x_core = core_swapped(x_in, ctx_count)

    mine, theirs = call(
        pick_kernel,
        [place],
        [w_key[0], value_projection[0]],
        [((slab, 2 * pair), b16)] * 2,
        [pltpu.SemaphoreType.DMA((8,))],
        in_hbm=True,
    )
    theirs = core_swapped(theirs, ctx_count)
    gain_rows = jnp.pad(norm_gain[0], (0, 16 * pair - width)).reshape(16, pair)
    kv_own, kv_other = call(
        halve_kernel,
        [place],
        [mine, theirs, gain_rows],
        [((2 * slab, pair), b16), ((2 * slab + 16, pair), b16)],
    )
    kv_other = swapped(kv_other, "section")

    home_parts = [
        chip_xor(kv_own, ctx_count, 2),
        chip_shift(kv_own, ctx_count, 1),
        lax.ppermute(kv_own, "ctx", [(i, i - 2) for i in range(2, ctx_count)]),
    ]
    *home_parts, kv_other, later = together(*home_parts, kv_other, place)
    home_parts.append(
        lax.ppermute(home_parts[0], "ctx", [(2, 0), (3, 1), (4, 6), (5, 7)])
    )
    gain_other = kv_other[2 * slab :].reshape(-1)[:width]
    gains = own_first(section, norm_gain[0], gain_other)
    kv_other = kv_other[: 2 * slab]
    away_parts = across_chips(kv_other)

    start = jnp.sum((doc_ids[:, None, :] < doc_ids[:, :, None]).astype(jnp.int32), axis=2)
    chip_start = lax.dynamic_slice_in_dim(start, chip * 4, 4, 1)
    inside = chip * 4 + jnp.arange(4, dtype=jnp.int32)[None, :] - chip_start
    lows = 5 - inside
    order = inside.reshape(micro_count, 2, 2).transpose(0, 2, 1).reshape(micro_count, 4)
    tables = host_tables(doc_ids.shape[1])

    def by_block(weight):
        columns = weight.shape[1]
        weight = weight.reshape(chips, 4, slab // 2, columns).transpose(1, 0, 2, 3)
        return weight.reshape(4, block_rows, columns)

    def shifted(key_value, far):
        return chip_shift(key_value, ctx_count, 1), chip_shift(far, ctx_count, 2)

    def attend(layer, low, query, key_value, window):
        own, other = query
        sent = lax.ppermute(other, "section", [(layer, 1 - layer)])
        near, far = window
        return call(
            functools.partial(attention_kernel, layer),
            [place, low],
            [own, sent, far, near, key_value],
            [(own.shape, b16)],
            [pltpu.VMEM((own.shape[0] // tokens, 9 * BLOCK, pair), b16)],
        )[0]

    def to_peers(shard):
        over_both = lax.ppermute(shard, ("section", "tp"), [(i, 3 - i) for i in range(4)])
        return [swapped(shard, "section"), swapped(shard, "tp"), over_both]

    def mix(attended, across, out_weight):
        shape = (block_rows, tokens // 2)
        return call(
            mix_kernel,
            [place],
            [attended, *across, out_weight],
            [(shape, f32), (shape, b16)] * (attended.shape[0] // tokens),
        )

    def add(residual, keep, send):
        arrived = core_swapped(send, ctx_count)
        return call(add_kernel, [], [residual, keep, arrived], [(send.shape, b16)])[0]

    def both_cores(pieces):
        pieces = [pieces[0], pieces[2], pieces[1], pieces[3]]
        return [one for piece in pieces for one in (piece, core_swapped(piece, ctx_count))]

    def in_order(blocks):
        by_section = [own_first(tp, blocks[0], blocks[1]), own_first(tp, blocks[2], blocks[3])]
        low = own_first(section, by_section[0][0], by_section[1][0])
        high = own_first(section, by_section[0][1], by_section[1][1])
        whole = jnp.stack([low[0], high[0], low[1], high[1]])
        count = whole.shape[-1]
        whole = whole.reshape(4, chips, slab // 2, count).transpose(1, 0, 2, 3)
        return whole.reshape(width, count)

    heads = ((slab, 2 * pair), b16)
    kept, sent = call(heads_kernel, [later], [w_out[0].T], [heads] * 2)
    both_halves = ((2, slab // 2, 2 * pair), b16)
    kept, sent = call(
        halves_kernel,
        [place],
        [kept, core_swapped(sent, ctx_count)],
        [both_halves] * 2,
        [pltpu.VMEM((slab, 2 * pair), f32)],
    )
    x_tp, sent, later = together(x_tp, sent, later)
    own_half, cross_half = call(
        join_kernel,
        [place],
        [kept, swapped(sent, "tp")],
        [((slab // 2, 4 * pair), b16)] * 2,
    )
    cross_half = swapped(cross_half, "section")
    query_weight = call(
        query_columns_kernel,
        [later],
        [w_query[0]],
        [((width, 2 * pair), b16)],
        [pltpu.SemaphoreType.DMA((2,))],
        in_hbm=True,
    )[0]
    x_both = core_swapped(x_tp, ctx_count)
    rows = (micro_count * tokens, pair)
    normed, query = [], []
    for micro in micros:
        one, *query = call(
            functools.partial(first_query_kernel, micro),
            [place, order[micro]],
            [x_in, x_tp, x_core, x_both, *tables, gains[0][None], query_weight, *query],
            [((tokens, width), b16), (rows, b16), (rows, b16)],
        )
        normed.append(one)
    (residuals,) = call(
        residual_kernel,
        [place],
        [x_in, x_tp, x_core, x_both],
        [((micro_count, block_rows, tokens // 2), f32)],
        [pltpu.VMEM((width, BLOCK), f32)],
    )
    *away_parts, home_parts[3], cross_half, normed[0], normed[1], residuals = together(
        *away_parts, home_parts[3], cross_half, *normed, residuals
    )
    home_parts, away_parts = [kv_own, *home_parts], [kv_other, *away_parts]
    out_halves = call(layers_kernel, [place], [own_half, cross_half], [(own_half.shape, b16)] * 2)
    key, far = call(
        first_keys_kernel,
        [place, order.reshape(-1)],
        [*normed, *home_parts, *away_parts, *tables],
        [(rows, b16), ((micro_count * BLOCK, pair), b16)],
        [pltpu.VMEM((width, pair), b16)],
    )
    window = shifted(key, far)

    key, out_half, later = together(key, out_halves[0], place)
    out_parts = across_chips(out_half)
    attended = attend(0, lows.reshape(-1), query, key, window)
    across = to_peers(attended)
    late_gain, late_query_weight, next_kv = call(
        late_kernel,
        [later],
        [gains[1][None], query_weight, *home_parts, *away_parts],
        [
            ((4, block_rows, BLOCK), f32),
            ((4, block_rows, 2 * pair), b16),
            ((block_rows, 4 * pair), b16),
        ],
        [pltpu.VMEM((block_rows, 4 * pair), f32)],
    )
    *out_parts, across[0], across[1], across[2], next_kv = together(*out_parts, *across, next_kv)
    out_weight = whole([out_half, *out_parts])
    mixed = mix(attended, across, out_weight)
    mixed[1], mixed[3], out_half = together(mixed[1], mixed[3], out_halves[1])
    out_parts = across_chips(out_half)
    halves = [add(residuals[m], *mixed[2 * m : 2 * m + 2]) for m in micros]
    spreads = [[one, *to_peers(one)] for one in halves]
    *spreads[0][1:], halves[1], out_parts[0], out_parts[1], out_parts[2] = together(
        *spreads[0][1:], halves[1], *out_parts
    )

    pieces, queries, keys, windows = [], [], [], []
    for micro in micros:
        pieces.append(both_cores(spreads[micro]))
        key_value, far, normed = call(
            keys_kernel,
            [place, order[micro]],
            [*pieces[micro], *tables, late_gain, next_kv],
            [((tokens, pair), b16), ((BLOCK, pair), b16), ((4, block_rows, tokens), b16)],
        )
        windows.append(shifted(key_value, far))
        normed, key_value = together(normed, key_value)
        query = call(
            query_kernel,
            [place, order[micro]],
            [normed, late_query_weight, *tables],
            [((tokens, pair), b16)] * 2,
        )
        queries.append(query)
        keys.append(key_value)
        if micro == 0:
            query[0], *spreads[1] = together(query[0], *spreads[1])
    queries[1][0], keys[0] = together(queries[1][0], keys[0])
    out_weight = whole([out_half, *out_parts])
    attended = [attend(1, lows[m], queries[m], keys[m], windows[m]) for m in micros]
    across = [to_peers(one) for one in attended]
    mixed = [mix(attended[0], across[0], out_weight)]
    mixed[0][0], *across[1] = together(mixed[0][0], *across[1])
    mixed.append(mix(attended[1], across[1], out_weight))
    at_home = core == tp

    def own_tokens(pieces):
        pairs = zip(pieces[::2], pieces[1::2])
        return [columns(jnp.where(at_home, here, there), core, BLOCK) for here, there in pairs]

    results = [jnp.stack([in_order(own_tokens(one)).T for one in pieces])]
    last = []
    for micro in micros:
        piece = add(halves[micro], *mixed[micro])
        goal = [(1, i, i % 2) for i in range(ctx_count)]
        moves = [(0, 1), (1, 0), (1, 1)]
        got = [
            lax.ppermute(
                piece,
                ("section", "ctx", "tp"),
                [
                    (
                        ((sec ^ by_sec) * ctx_count + i) * 2 + (t ^ by_tp),
                        (sec * ctx_count + i) * 2 + t,
                    )
                    for sec, i, t in goal
                ],
            )
            for by_sec, by_tp in moves
        ]
        blocks = []
        for one in (piece, got[0], got[1], got[2]):
            kept, passed = own_first(core, one[:, :BLOCK], one[:, BLOCK:])
            blocks.append((kept, core_swapped(passed, ctx_count)))
        first = [jnp.where(at_home, kept, arrived) for kept, arrived in blocks]
        last.append(in_order(first).T)
    results.append(jnp.stack(last))
    return jnp.where(section == 0, results[0], results[1])[None]


def solution(mesh):
    in_specs = (
        P(None, ("ctx", "tp"), None),
        P("section", None),
        P("section", None, "tp"),
        P("section", "ctx", "tp"),
        P("section", "ctx", "tp"),
        P("section", "tp", "ctx"),
        P(),
    )
    out_specs = P("section", None, ("ctx", "tp"), None)
    sizes = mesh.shape
    fits = sizes["section"] == 2 and sizes["tp"] == 2 and sizes["ctx"] == 8
    body = split_heads if fits else local
    return jax.shard_map(body, mesh=mesh, in_specs=in_specs, out_specs=out_specs, check_vma=False)
```

```python
import functools

import numpy as np
import jax
import jax.numpy as jnp
from jax import lax
from jax.experimental import pallas as pl
from jax.experimental.pallas import tpu as pltpu
from jax.sharding import PartitionSpec as P

HEAD_SIZE = 128
WINDOW = 1024
BLOCK = 128


query_scale = 168.0 ** (-0.5)
rope_base = 10000.0


def shifted(shard, axis, by):
    count = lax.axis_size(axis)
    pairs = [(i, i + by) for i in range(count) if 0 <= i + by < count]
    return lax.ppermute(shard, axis, pairs)


def rms_normed(hidden, gain_row):
    widened = hidden.astype(jnp.float32)
    mean_square = jnp.mean(widened * widened, axis=-1, keepdims=True)
    return (widened * lax.rsqrt(mean_square + 1e-06) * gain_row.astype(jnp.float32)).astype(
        jnp.bfloat16
    )


def rotary_apply(tensor, token_position):
    half_dim = tensor.shape[-1] // 2
    frequency = rope_base ** (-(jnp.arange(half_dim, dtype=jnp.float32) * 2.0) / tensor.shape[-1])
    angles = token_position.astype(jnp.float32)[:, None] * frequency[None, :]
    cosine_table = jnp.cos(angles)[:, None, :]
    sine_table = jnp.sin(angles)[:, None, :]
    first_half = tensor[..., :half_dim]
    second_half = tensor[..., half_dim:]
    return jnp.concatenate(
        [
            first_half * cosine_table - second_half * sine_table,
            second_half * cosine_table + first_half * sine_table,
        ],
        axis=-1,
    )


def doc_lookup(ids_row, token_index, block):
    block_count = ids_row.shape[0]
    start_block = jnp.sum((ids_row[None, :] < ids_row[:, None]).astype(jnp.int32), axis=1)
    block_of = jnp.clip(token_index // block, 0, block_count - 1)
    onehot = (block_of[:, None] == jnp.arange(block_count, dtype=jnp.int32)[None, :]).astype(
        jnp.int32
    )
    start_of = jnp.sum(onehot * start_block[None, :], axis=1)
    doc_of = jnp.sum(onehot * ids_row[None, :], axis=1)
    return (token_index - start_of * block, doc_of)


def attention_rows(
    grouped_heads, key_matrix_rows, value_rows, query_index, query_doc, key_index, key_doc
):
    scores = (
        jnp.einsum(
            "qgrd,kgd->grqk", grouped_heads, key_matrix_rows, preferred_element_type=jnp.float32
        )
        * query_scale
    )
    allowed = (key_index[None, :] >= 0) & (key_index[None, :] <= query_index[:, None])
    allowed = (
        allowed
        & (query_index[:, None] - key_index[None, :] < WINDOW)
        & (key_doc[None, :] == query_doc[:, None])
    )
    scores = jnp.where(allowed[None, None], scores, -1e30)
    peak_score = jnp.max(scores, axis=-1, keepdims=True)
    raised = jnp.exp(scores - peak_score)
    weights = (raised / jnp.sum(raised, axis=-1, keepdims=True)).astype(jnp.bfloat16)
    layer_result = jnp.einsum(
        "grqk,kgd->qgrd", weights, value_rows, preferred_element_type=jnp.float32
    )
    return layer_result.astype(jnp.bfloat16).reshape(grouped_heads.shape[0], -1)


def local(x_in, norm_gain, w_query, w_key, value_projection, w_out, doc_ids):
    section_num = lax.axis_index("section")
    section_count = lax.axis_size("section")
    ctx_num = lax.axis_index("ctx")
    ctx_count = lax.axis_size("ctx")
    tp_count = lax.axis_size("tp")
    micro_count, half_rows, model_width = x_in.shape
    key_full, value_full, out_part = (
        lax.all_gather(w_key, "ctx", axis=1, tiled=True),
        lax.all_gather(value_projection, "ctx", axis=1, tiled=True),
        lax.all_gather(w_out, "ctx", axis=2, tiled=True),
    )
    query_weight = w_query[0]
    key_matrix = key_full[0]
    value_matrix = value_full[0]
    out_weight = out_part[0]
    tok_rows = half_rows * tp_count
    gain_row = norm_gain[0]
    query_heads = query_weight.shape[1] // HEAD_SIZE
    kv_heads = key_matrix.shape[1] // HEAD_SIZE
    group_size = query_heads // kv_heads
    reach_hops = min(-(-WINDOW // tok_rows), ctx_count - 1)
    token_index = ctx_num * tok_rows + jnp.arange(tok_rows, dtype=jnp.int32)
    key_index = (ctx_num - reach_hops) * tok_rows + jnp.arange(
        (reach_hops + 1) * tok_rows, dtype=jnp.int32
    )

    def project(operands):
        whole_rows, token_position = operands
        normalized_input = rms_normed(whole_rows, gain_row)
        query_matrix_rows = rotary_apply(
            jnp.dot(normalized_input, query_weight, preferred_element_type=jnp.float32).reshape(
                tok_rows, query_heads, HEAD_SIZE
            ),
            token_position,
        )
        key_matrix_rows = rotary_apply(
            jnp.dot(normalized_input, key_matrix, preferred_element_type=jnp.float32).reshape(
                tok_rows, kv_heads, HEAD_SIZE
            ),
            token_position,
        )
        value_rows = jnp.dot(
            normalized_input, value_matrix, preferred_element_type=jnp.float32
        ).astype(jnp.bfloat16)
        stacked = jnp.stack(
            [
                key_matrix_rows.astype(jnp.bfloat16).reshape(tok_rows, kv_heads * HEAD_SIZE),
                value_rows,
            ]
        )
        return (
            query_matrix_rows.astype(jnp.bfloat16).reshape(tok_rows, query_heads * HEAD_SIZE),
            stacked,
        )

    def skip_project(operands):
        return (
            jnp.zeros((tok_rows, query_heads * HEAD_SIZE), jnp.bfloat16),
            jnp.zeros((2, tok_rows, kv_heads * HEAD_SIZE), jnp.bfloat16),
        )

    def skip_attend(operands):
        return jnp.zeros((tok_rows, query_heads * HEAD_SIZE), jnp.bfloat16)

    def out_local(operands):
        return jnp.dot(operands, out_weight, preferred_element_type=jnp.float32)

    def skip_out(operands):
        return jnp.zeros((operands.shape[0], out_weight.shape[1]), jnp.float32)

    def step(step_num, carry):
        received, results = carry
        micro_num = step_num - section_num
        active = (micro_num >= 0) & (micro_num < micro_count)
        micro_at = jnp.clip(micro_num, 0, micro_count - 1)
        fresh_rows = lax.dynamic_index_in_dim(x_in, micro_at, 0, keepdims=False)
        current = jnp.where(section_num == 0, fresh_rows, received)
        whole_rows = lax.all_gather(current, "tp", axis=0, tiled=True)
        ids_row = lax.dynamic_index_in_dim(doc_ids, micro_at, 0, keepdims=False)
        token_position, query_doc = doc_lookup(ids_row, token_index, BLOCK)
        unused, key_doc = doc_lookup(ids_row, key_index, BLOCK)
        query_matrix_rows, stacked = lax.cond(
            active, project, skip_project, (whole_rows, token_position)
        )
        pieces = [shifted(stacked, "ctx", distance) for distance in range(reach_hops, 0, -1)]
        window_kv = jnp.concatenate(pieces + [stacked], axis=1)

        def attend(operands):
            query_part, window_part = operands
            grouped_heads = query_part.reshape(tok_rows, kv_heads, group_size, HEAD_SIZE)
            key_matrix_rows = window_part[0].reshape(-1, kv_heads, HEAD_SIZE)
            value_rows = window_part[1].reshape(-1, kv_heads, HEAD_SIZE)
            return attention_rows(
                grouped_heads,
                key_matrix_rows,
                value_rows,
                token_index,
                query_doc,
                key_index,
                key_doc,
            )

        attended = lax.cond(active, attend, skip_attend, (query_matrix_rows, window_kv))
        summed = lax.psum_scatter(
            lax.cond(active, out_local, skip_out, attended), "tp", scatter_dimension=0, tiled=True
        )
        updated = (current.astype(jnp.float32) + summed).astype(jnp.bfloat16)
        previous = lax.dynamic_index_in_dim(results, micro_at, 0, keepdims=False)
        results = lax.dynamic_update_index_in_dim(
            results, jnp.where(active, updated, previous), micro_at, 0
        )
        received = shifted(updated, "section", 1)
        return (received, results)

    start_carry = (
        jnp.zeros((half_rows, model_width), jnp.bfloat16),
        jnp.zeros((micro_count, half_rows, model_width), jnp.bfloat16),
    )
    unused_received, results = lax.fori_loop(0, micro_count + section_count - 1, step, start_carry)
    return results[None]


SECTION, CORE, TP, CHIP = range(4)


def swapped(shard, axis):
    return lax.ppermute(shard, axis, [(0, 1), (1, 0)])


def core_swapped(shard, ctx_count):
    return lax.ppermute(shard, "ctx", [(i, i ^ 1) for i in range(ctx_count)])


def chip_xor(shard, ctx_count, by):
    return lax.ppermute(shard, "ctx", [(i, i ^ (2 * by)) for i in range(ctx_count)])


def chip_shift(shard, ctx_count, by):
    return lax.ppermute(
        shard, "ctx", [(i, i + 2 * by) for i in range(ctx_count) if i + 2 * by < ctx_count]
    )


def columns(array, block, width):
    return lax.dynamic_slice_in_dim(array, block * width, width, 1)


def own_first(flag, own, other):
    return jnp.where(flag == 0, own, other), jnp.where(flag == 0, other, own)


def together(*values):
    return lax.optimization_barrier(values)


def call(kernel, scalars, operands, outputs, scratch=(), limit=16, in_hbm=False):
    vmem = pl.BlockSpec(memory_space=pltpu.VMEM)
    smem = pl.BlockSpec(memory_space=pltpu.SMEM)
    place = pl.BlockSpec(memory_space=pltpu.HBM) if in_hbm else vmem
    return list(
        pl.pallas_call(
            kernel,
            out_shape=[jax.ShapeDtypeStruct(shape, kind) for shape, kind in outputs],
            in_specs=[smem] * len(scalars) + [place] * len(operands),
            out_specs=[vmem] * len(outputs),
            scratch_shapes=list(scratch),
            compiler_params=pltpu.CompilerParams(vmem_limit_bytes=limit * 2**20),
            cost_estimate=pl.CostEstimate(flops=1024, bytes_accessed=1024, transcendentals=0),
        )(*scalars, *operands)
    )


def aligned(index, size):
    return pl.ds(pl.multiple_of(index * size, size), size)


def pick_kernel(place, key_ref, value_ref, mine_ref, theirs_ref, sems):
    core, copies = place[CORE], []
    for out_ref, which in ((mine_ref, core), (theirs_ref, 1 - core)):
        for sec in (0, 1):
            for kind, ref in enumerate((key_ref, value_ref)):
                at = (2 * sec + kind) * HEAD_SIZE
                copies.append(
                    pltpu.make_async_copy(
                        ref.at[:, aligned(2 * sec + which, HEAD_SIZE)],
                        out_ref.at[:, at : at + HEAD_SIZE],
                        sems.at[len(copies)],
                    )
                )
    for copy in copies:
        copy.start()
    for copy in copies:
        copy.wait()


def halve_kernel(place, mine_ref, theirs_ref, gain_ref, own_ref, other_ref):
    core, section = place[CORE], place[SECTION]
    rows, pair = mine_ref.shape[0], 2 * HEAD_SIZE
    for out_ref, sec in ((own_ref, section), (other_ref, 1 - section)):
        out_ref[aligned(core, rows), :] = mine_ref[:, aligned(sec, pair)]
        out_ref[aligned(1 - core, rows), :] = theirs_ref[:, aligned(sec, pair)]
    other_ref[2 * rows :, :] = gain_ref[...]


def layers_kernel(place, own_ref, other_ref, first_ref, second_ref):
    rows = own_ref.shape[0]
    for section in (0, 1):

        @pl.when(place[SECTION] == section)
        def _():
            out_refs = (first_ref, second_ref) if section == 0 else (second_ref, first_ref)
            out_refs[0][...] = own_ref[...]
            out_refs[1][...] = other_ref[:rows, :]


def query_columns_kernel(place, weight_ref, out_ref, sems):
    copies = []
    for sec in (0, 1):
        copies.append(
            pltpu.make_async_copy(
                weight_ref.at[:, aligned(2 * sec + place[CORE], 2 * HEAD_SIZE)],
                out_ref.at[:, 2 * sec * HEAD_SIZE : (2 * sec + 2) * HEAD_SIZE],
                sems.at[sec],
            )
        )
    for copy in copies:
        copy.start()
    for copy in copies:
        copy.wait()


def late_kernel(place, gain_ref, query_ref, *refs):
    home, away, (gain_out, query_out, kv_out, wide) = refs[:5], refs[5:9], refs[9:]
    rows = home[0].shape[0] // 4
    at_home = place[SECTION] == 1
    gain = jnp.broadcast_to(gain_ref[...].astype(jnp.float32), (BLOCK, gain_ref.shape[1])).T
    for by, part in enumerate(by_chip(place, home)):
        part = jnp.where(at_home, part, away[by][: 4 * rows, :]).astype(jnp.float32)
        for block in range(4):
            lanes = slice(block * 2 * HEAD_SIZE, (block + 1) * 2 * HEAD_SIZE)
            wide[aligned(place[CHIP] ^ by, rows), lanes] = part[block * rows : (block + 1) * rows]
    kv_out[...] = wide[...].astype(jnp.bfloat16)
    for block in range(4):
        query = []
        for chip in range(4):
            at = slice((4 * chip + block) * rows, (4 * chip + block + 1) * rows)
            gain_out[block, chip * rows : (chip + 1) * rows, :] = gain[at]
            query.append(query_ref[at, :].astype(jnp.float32))
        query_out[block, :, :] = jnp.concatenate(query, axis=0).astype(jnp.bfloat16)


def split_kernel(place, slab_ref, kept_ref, sent_ref, wide):
    rows = kept_ref.shape[0]
    wide[...] = slab_ref[...].astype(jnp.float32)
    for ref, core in ((kept_ref, place[CORE]), (sent_ref, 1 - place[CORE])):
        ref[...] = wide[pl.ds(pl.multiple_of(core * rows, 8), rows), :].astype(ref.dtype)


def sort_kernel(place, kept_ref, got_ref, home_ref, cross_ref):
    for at_home in (False, True):

        @pl.when((place[CORE] == place[SECTION]) == at_home)
        def _():
            home_ref[...] = kept_ref[...] if at_home else got_ref[...]
            cross_ref[...] = got_ref[...] if at_home else kept_ref[...]


def residual_kernel(place, own, core_, out_ref, wide):
    me = 2 * place[SECTION] + place[CORE]
    rows = out_ref.shape[1] // 4
    for micro in range(own.shape[0]):
        for by, ref in enumerate((own, core_)):
            wide[...] = ref[micro].astype(jnp.float32).T
            for chip in range(4):
                at = pl.multiple_of((4 * chip + me) * rows, 8)
                out_ref[micro, chip * rows : (chip + 1) * rows, aligned(place[CORE] ^ by, BLOCK)] = (
                    wide[pl.ds(at, rows), :]
                )


def turned(array, cosine, sine):
    return array * cosine + pltpu.roll(array, HEAD_SIZE // 2, 1) * sine


def rope_tables(inside, tables):
    row_cos, row_sin, block_cos, block_sin = tables
    cosine, sine = [], []
    count = inside.shape[0]
    for at in range(count):
        block = pl.ds(inside[at], 1)
        first, second = block_cos[block, :], block_sin[block, :]
        cosine.append(first * row_cos[...] - second * row_sin[...])
        sine.append(second * row_cos[...] + first * row_sin[...])
    lane = lax.broadcasted_iota(jnp.int32, (count * BLOCK, HEAD_SIZE), 1)
    sine = jnp.concatenate(sine, axis=0)
    return jnp.concatenate(cosine, axis=0), jnp.where(lane < HEAD_SIZE // 2, -sine, sine)


def host_tables(block_count):
    lane = np.arange(HEAD_SIZE) % (HEAD_SIZE // 2)
    frequency = rope_base ** (-(lane * 2.0) / HEAD_SIZE)
    rows = np.arange(BLOCK)[:, None] * frequency
    blocks = np.arange(block_count)[:, None] * (BLOCK * frequency)
    angles = (np.cos(rows), np.sin(rows), np.cos(blocks), np.sin(blocks))
    return [jnp.asarray(one, jnp.float32) for one in angles]


def store_queries(place, query, rope, own_ref, other_ref, row=0):
    heads = [
        turned(query[:, at : at + HEAD_SIZE], *rope).astype(jnp.bfloat16)
        for at in range(0, query.shape[1], HEAD_SIZE)
    ]
    rows = slice(row, row + query.shape[0])
    for sec in (0, 1):

        @pl.when(place[SECTION] == sec)
        def _():
            for out_ref, first in ((own_ref, 2 * sec), (other_ref, 2 - 2 * sec)):
                out_ref[rows, :HEAD_SIZE] = heads[first]
                out_ref[rows, HEAD_SIZE:] = heads[first + 1]


def store_keys(key_value, rope, out_ref, far_ref, rows=(0, 0)):
    size = HEAD_SIZE
    key = turned(key_value[:, :size], *rope).astype(jnp.bfloat16)
    value = key_value[:, size:].astype(jnp.bfloat16)
    out_ref[rows[0] : rows[0] + key.shape[0], :size] = key
    out_ref[rows[0] : rows[0] + key.shape[0], size:] = value
    for micro in range(key.shape[0] // (4 * BLOCK)):
        last = slice((4 * micro + 3) * BLOCK, (4 * micro + 4) * BLOCK)
        to = slice(rows[1] + micro * BLOCK, rows[1] + (micro + 1) * BLOCK)
        far_ref[to, :size] = key[last]
        far_ref[to, size:] = value[last]


def first_query_kernel(micro, place, inside, *refs):
    pieces, tables, (gain, weight), refs = refs[:4], refs[4:8], refs[8:10], refs[10:]
    normed_ref, own_ref, other_ref = refs[-3:]
    step = 16
    for by, ref in enumerate(pieces):
        at = 2 * (place[TP] ^ (by & 1)) + (place[CORE] ^ (by >> 1))
        for row in range(0, BLOCK, step):
            rows = ref[micro, row : row + step, :].astype(jnp.float32)
            mean_square = jnp.mean(rows * rows, axis=-1, keepdims=True)
            rows = rows * lax.rsqrt(mean_square + 1e-06) * gain[...].astype(jnp.float32)
            where = pl.ds(pl.multiple_of(at * BLOCK + row, step), step)
            normed_ref[where, :] = rows.astype(jnp.bfloat16)
    query = jnp.dot(normed_ref[...], weight[...], preferred_element_type=jnp.float32)
    row = micro * normed_ref.shape[0]
    if micro > 0:
        own_ref[:row, :], other_ref[:row, :] = refs[0][:row, :], refs[1][:row, :]
    store_queries(place, query, rope_tables(inside, tables), own_ref, other_ref, row)


def by_chip(place, refs):
    own, across, below, above, far = [ref[...] for ref in refs]
    chip = place[CHIP]
    one = jnp.where(chip % 2 == 0, above, below)
    three = jnp.where(chip == 1, above, jnp.where(chip == 2, below, far))
    return own, one, across, three


def first_keys_kernel(place, inside, first, second, *refs):
    home, away, tables, (out_ref, far_ref, weight) = refs[:5], refs[5:9], refs[9:13], refs[13:]
    at_home = place[SECTION] == 0
    for by, rows in enumerate(by_chip(place, home)):
        rows = jnp.where(at_home, rows, away[by][: rows.shape[0], :])
        weight[aligned(place[CHIP] ^ by, rows.shape[0]), :] = rows
    key_value = jnp.concatenate(
        [
            jnp.dot(one[...], weight[...], preferred_element_type=jnp.float32)
            for one in (first, second)
        ],
        axis=0,
    )
    store_keys(key_value, rope_tables(inside, tables), out_ref, far_ref)


def tn(left, right):
    return lax.dot_general(
        left, right, (((0,), (0,)), ((), ())), preferred_element_type=jnp.float32
    )


def keys_kernel(place, inside, *refs):
    pieces, tables, (gain, weight), refs = refs[:8], refs[8:12], refs[12:14], refs[14:]
    out_ref, far_ref, normed = refs[-3:]
    for ref, before in zip((out_ref, far_ref), refs[:-3]):
        ref[: before.shape[0], :] = before[...]
    me = 2 * place[SECTION] + place[CORE]
    width, step = 4 * pieces[0].shape[0], 56
    for by_tp in (0, 1):
        for half in (0, 1):
            lanes = slice(half * BLOCK, (half + 1) * BLOCK)
            total = jnp.zeros((8, BLOCK), jnp.float32)
            for block in range(4):
                for row in range(0, width // 4, step):
                    one = pieces[2 * block + by_tp][row : row + step, lanes].astype(jnp.float32)
                    total = total + jnp.sum((one * one).reshape(-1, 8, BLOCK), axis=0)
            total = jnp.sum(total, axis=0, keepdims=True)
            scale = lax.rsqrt(total / width + 1e-06)
            at = 2 * (place[TP] ^ by_tp) + half
            for block in range(4):
                one = pieces[2 * block + by_tp][:, lanes].astype(jnp.float32)
                normed[block, :, aligned(at, BLOCK)] = (one * scale * gain[me ^ block]).astype(
                    jnp.bfloat16
                )
    key_value = sum(
        tn(normed[block], weight[:, aligned(me ^ block, 2 * HEAD_SIZE)]) for block in range(4)
    )
    rows = (refs[0].shape[0], refs[1].shape[0]) if len(refs) > 3 else (0, 0)
    store_keys(key_value, rope_tables(inside, tables), out_ref, far_ref, rows)


def query_kernel(place, inside, normed, weight, *refs):
    tables, (own_ref, other_ref) = refs[:4], refs[4:]
    me = 2 * place[SECTION] + place[CORE]
    query = sum(tn(normed[block], weight[me ^ block]) for block in range(4))
    store_queries(place, query, rope_tables(inside, tables), own_ref, other_ref)


def attention_kernel(
    layer, micros, place, low_ref, kept_ref, sent_ref, far_ref, near_ref, own_ref, out_ref, window_ref
):
    size = HEAD_SIZE
    span = 6 * BLOCK
    row = lax.broadcasted_iota(jnp.int32, (2 * BLOCK, span), 0) % BLOCK
    col = lax.broadcasted_iota(jnp.int32, (2 * BLOCK, span), 1)
    causal = col - 5 * BLOCK <= row
    home = place[SECTION] == layer
    for micro in micros:
        window_ref[micro, 0:BLOCK, :] = far_ref[micro * BLOCK : (micro + 1) * BLOCK, :]
        places = [(4 * micro + at) * BLOCK for at in (0, 2, 1, 3)]
        for block, at in enumerate(places):
            window_ref[micro, (1 + block) * BLOCK : (2 + block) * BLOCK, :] = near_ref[at : at + BLOCK, :]
            window_ref[micro, (5 + block) * BLOCK : (6 + block) * BLOCK, :] = own_ref[at : at + BLOCK, :]
        for block, at in enumerate(places):
            rows = slice(block * BLOCK, (block + 6) * BLOCK)
            to = at - 4 * micros[0] * BLOCK
            query = jnp.where(home, kept_ref[to : to + BLOCK, :], sent_ref[to : to + BLOCK, :])
            query = jnp.concatenate([query[:, :size], query[:, size:]], axis=0)
            scores = lax.dot_general(
                query,
                window_ref[micro, rows, 0:size],
                (((1,), (1,)), ((), ())),
                preferred_element_type=jnp.float32,
            )
            allowed = causal & (col >= low_ref[4 * micro + block] * BLOCK)
            scores = jnp.where(allowed, scores * query_scale, -1e30)
            raised = jnp.exp(scores - jnp.max(scores, axis=-1, keepdims=True))
            total = jnp.sum(raised, axis=-1, keepdims=True)
            mixed = jnp.dot(
                raised.astype(jnp.bfloat16),
                window_ref[micro, rows, size : 2 * size],
                preferred_element_type=jnp.float32,
            )
            mixed = (mixed / total).astype(jnp.bfloat16)
            out_ref[to : to + BLOCK, 0:size] = mixed[0:BLOCK]
            out_ref[to : to + BLOCK, size : 2 * size] = mixed[BLOCK:]


def gather_kernel(place, *refs):
    parts, (out_ref, wide) = refs[:4], refs[4:]
    for by, ref in enumerate(parts):
        wide[aligned(place[CHIP] ^ by, ref.shape[0]), :] = ref[...].astype(jnp.float32)
    out_ref[...] = wide[...].astype(out_ref.dtype)


def mix_kernel(place, own, core_, across, both, weight, *out_refs):
    me = 2 * place[SECTION] + place[CORE]
    weights = [weight[:, aligned(me ^ by, 2 * HEAD_SIZE)] for by in range(4)]
    for at, out_ref in enumerate(out_refs):
        half = out_ref.shape[1]
        tp = place[TP] if at % 2 == 0 else 1 - place[TP]
        total = sum(
            lax.dot_general(
                weights[by],
                ref[aligned(2 * (at // 2) + tp, half), :],
                (((1,), (1,)), ((), ())),
                preferred_element_type=jnp.float32,
            )
            for by, ref in enumerate((own, core_, across, both))
        )
        out_ref[...] = total.astype(out_ref.dtype)


def add_kernel(residual, keep, arrived, out_ref):
    total = residual[...].astype(jnp.float32) + keep[...] + arrived[...].astype(jnp.float32)
    out_ref[...] = total.astype(out_ref.dtype)


def split_heads(x_in, norm_gain, w_query, w_key, value_projection, w_out, doc_ids):
    section = lax.axis_index("section")
    ctx = lax.axis_index("ctx")
    tp = lax.axis_index("tp")
    ctx_count = lax.axis_size("ctx")
    chips = ctx_count // 2
    chip, core = ctx // 2, ctx % 2
    place = jnp.stack([section, core, tp, chip]).astype(jnp.int32)
    micro_count, half_rows, width = x_in.shape
    tokens = 4 * half_rows
    slab = width // ctx_count
    head, pair = HEAD_SIZE, 2 * HEAD_SIZE
    block_rows = width // 4
    micros = range(micro_count)
    b16, f32 = jnp.bfloat16, jnp.float32

    def across_chips(shard):
        return [chip_xor(shard, ctx_count, by) for by in range(1, chips)]

    def whole(parts):
        rows, columns = parts[0].shape
        return call(
            gather_kernel,
            [place],
            parts,
            [((chips * rows, columns), b16)],
            [pltpu.VMEM((chips * rows, columns), f32)],
        )[0]

    x_tp = swapped(x_in, "tp")
    x_core = core_swapped(x_in, ctx_count)

    mine, theirs = call(
        pick_kernel,
        [place],
        [w_key[0], value_projection[0]],
        [((slab, 2 * pair), b16)] * 2,
        [pltpu.SemaphoreType.DMA((8,))],
        in_hbm=True,
    )
    theirs = core_swapped(theirs, ctx_count)
    gain_rows = jnp.pad(norm_gain[0], (0, 16 * pair - width)).reshape(16, pair)
    kv_own, kv_other = call(
        halve_kernel,
        [place],
        [mine, theirs, gain_rows],
        [((2 * slab, pair), b16), ((2 * slab + 16, pair), b16)],
    )
    kv_other = swapped(kv_other, "section")

    home_parts = [
        chip_xor(kv_own, ctx_count, 2),
        chip_shift(kv_own, ctx_count, 1),
        lax.ppermute(kv_own, "ctx", [(i, i - 2) for i in range(2, ctx_count)]),
    ]
    home_parts[1], later = together(home_parts[1], place)
    query_weight = call(
        query_columns_kernel,
        [later],
        [w_query[0]],
        [((width, 2 * pair), b16)],
        [pltpu.SemaphoreType.DMA((2,))],
        in_hbm=True,
    )[0]
    *home_parts, kv_other, query_weight, later = together(
        *home_parts, kv_other, query_weight, place
    )
    home_parts.append(
        lax.ppermute(home_parts[0], "ctx", [(2, 0), (3, 1), (4, 6), (5, 7)])
    )
    gain_other = kv_other[2 * slab :].reshape(-1)[:width]
    gains = own_first(section, norm_gain[0], gain_other)
    away_parts = across_chips(kv_other)

    start = jnp.sum((doc_ids[:, None, :] < doc_ids[:, :, None]).astype(jnp.int32), axis=2)
    chip_start = lax.dynamic_slice_in_dim(start, chip * 4, 4, 1)
    inside = chip * 4 + jnp.arange(4, dtype=jnp.int32)[None, :] - chip_start
    lows = 5 - inside
    order = inside.reshape(micro_count, 2, 2).transpose(0, 2, 1).reshape(micro_count, 4)
    tables = host_tables(doc_ids.shape[1])

    def by_block(weight):
        columns = weight.shape[1]
        weight = weight.reshape(chips, 4, slab // 2, columns).transpose(1, 0, 2, 3)
        return weight.reshape(4, block_rows, columns)

    def shifted(key_value, far):
        return chip_shift(key_value, ctx_count, 1), chip_shift(far, ctx_count, 2)

    def sent_over(layer, queries):
        return lax.ppermute(queries, "section", [(layer, 1 - layer)])

    def attend(layer, which, low, query, key_value, window):
        own, sent = query
        near, far = window
        return call(
            functools.partial(attention_kernel, layer, which),
            [place, low],
            [own, sent, far, near, key_value],
            [(own.shape, b16)],
            [pltpu.VMEM((micro_count, 9 * BLOCK, pair), b16)],
        )[0]

    def mix(attended, across, out_weight):
        shape = (block_rows, tokens // 2)
        return call(
            mix_kernel,
            [place],
            [
                attended,
                core_swapped(attended, ctx_count),
                across,
                core_swapped(across, ctx_count),
                out_weight,
            ],
            [(shape, f32), (shape, b16)] * (attended.shape[0] // tokens),
            )

    def add(residual, keep, send):
        return call(add_kernel, [], [residual, keep, swapped(send, "tp")], [(send.shape, b16)])[0]

    def spread(piece, direct):
        over_tp, over_section = swapped(piece, "tp"), swapped(piece, "section")
        if direct:
            over_both = lax.ppermute(piece, ("section", "tp"), [(i, 3 - i) for i in range(4)])
        else:
            over_both = swapped(over_tp, "section")
        return [piece, over_tp, over_section, over_both]

    def both_cores(pieces):
        over = [core_swapped(one, ctx_count) for one in pieces]
        return pieces[:2] + over[:2] + pieces[2:] + over[2:]

    def in_order(blocks):
        by_section = [own_first(core, blocks[0], blocks[1]), own_first(core, blocks[2], blocks[3])]
        low = own_first(section, by_section[0][0], by_section[1][0])
        high = own_first(section, by_section[0][1], by_section[1][1])
        whole = jnp.stack([low[0], high[0], low[1], high[1]])
        count = whole.shape[-1]
        whole = whole.reshape(4, chips, slab // 2, count).transpose(1, 0, 2, 3)
        return whole.reshape(width, count)

    half_shape = ((slab // 2, w_out.shape[1]), b16)
    kept, sent = call(
        split_kernel,
        [later],
        [w_out[0].T],
        [half_shape] * 2,
        [pltpu.VMEM((slab, w_out.shape[1]), f32)],
    )
    own_half, cross_half = call(
        sort_kernel, [place], [kept, core_swapped(sent, ctx_count)], [half_shape] * 2
    )
    cross_half = swapped(cross_half, "section")
    x_tp, later = together(x_tp, later)
    x_both = core_swapped(x_tp, ctx_count)
    rows = (micro_count * tokens, pair)
    normed, query = [], []
    for micro in micros:
        one, *query = call(
            functools.partial(first_query_kernel, micro),
            [place, order[micro]],
            [x_in, x_tp, x_core, x_both, *tables, gains[0][None], query_weight, *query],
            [((tokens, width), b16), (rows, b16), (rows, b16)],
        )
        normed.append(one)
    *away_parts, home_parts[3], cross_half, normed[0], normed[1] = together(
        *away_parts, home_parts[3], cross_half, *normed
    )
    home_parts, away_parts = [kv_own, *home_parts], [kv_other, *away_parts]
    out_halves = call(layers_kernel, [place], [own_half, cross_half], [(own_half.shape, b16)] * 2)
    key, far = call(
        first_keys_kernel,
        [place, order.reshape(-1)],
        [*normed, *home_parts, *away_parts, *tables],
        [(rows, b16), ((micro_count * BLOCK, pair), b16)],
        [pltpu.VMEM((width, pair), b16)],
    )
    window = shifted(key, far)

    key, out_half, later = together(key, out_halves[0], place)
    out_parts = across_chips(out_half)
    query = query[0], sent_over(0, query[1])
    attended = attend(0, micros, lows.reshape(-1), query, key, window)
    across = swapped(attended, "section")
    (residuals,) = call(
        residual_kernel,
        [later],
        [x_in, x_core],
        [((micro_count, block_rows, tokens // 2), f32)],
        [pltpu.VMEM((width, BLOCK), f32)],
    )
    late_gain, late_query_weight, next_kv = call(
        late_kernel,
        [later],
        [gains[1][None], query_weight, *home_parts, *away_parts],
        [
            ((4, block_rows, BLOCK), f32),
            ((4, block_rows, 2 * pair), b16),
            ((block_rows, 4 * pair), b16),
        ],
        [pltpu.VMEM((block_rows, 4 * pair), f32)],
    )
    *out_parts, across, next_kv, residuals = together(*out_parts, across, next_kv, residuals)
    out_weight = whole([out_half, *out_parts])
    mixed = mix(attended, across, out_weight)
    mixed[1], mixed[3], out_half = together(mixed[1], mixed[3], out_halves[1])
    out_parts = across_chips(out_half)
    halves = [add(residuals[m], *mixed[2 * m : 2 * m + 2]) for m in micros]
    spreads = [spread(halves[0], True)]
    halves[1], spreads[0][1], spreads[0][2], out_parts[1] = together(
        halves[1], *spreads[0][1:3], out_parts[1]
    )
    spreads.append(spread(halves[1], False))
    *spreads[0][1:], spreads[1][1], spreads[1][2] = together(*spreads[0][1:], *spreads[1][1:3])
    *spreads[0][1:], out_parts[0], out_parts[2] = together(
        *spreads[0][1:], out_parts[0], out_parts[2]
    )
    next_out = whole([out_half, *out_parts])

    pieces, queries, before = [], [], []
    for micro in micros:
        pieces.append(both_cores(spreads[micro]))
        *before, normed = call(
            keys_kernel,
            [place, order[micro]],
            [*pieces[micro], *tables, late_gain, next_kv, *before],
            [
                (((micro + 1) * tokens, pair), b16),
                (((micro + 1) * BLOCK, pair), b16),
                ((4, block_rows, tokens), b16),
            ],
        )
        normed, before[0] = together(normed, before[0])
        query = call(
            query_kernel,
            [place, order[micro]],
            [normed, late_query_weight, *tables],
            [((tokens, pair), b16)] * 2,
        )
        queries.append(query)
        if micro == 0:
            query[0], *spreads[1] = together(query[0], *spreads[1])
    key, far = before
    window = shifted(key, far)
    queries = [(own, sent_over(1, other)) for own, other in queries]
    near, far, first, second, next_out = together(
        *window, *[sent for _, sent in queries], next_out
    )
    queries = [(queries[0][0], first), (queries[1][0], second)]
    attended = [attend(1, (m,), lows.reshape(-1), queries[m], key, (near, far)) for m in micros]
    across = [swapped(one, "section") for one in attended]
    across[0], attended[1] = together(across[0], attended[1])
    mixed = [mix(attended[0], across[0], next_out)]
    mixed[0][0], across[1] = together(mixed[0][0], across[1])
    mixed.append(mix(attended[1], across[1], next_out))
    results = [
        jnp.stack(
            [in_order([columns(one[2 * i], core, BLOCK) for i in range(4)]).T for one in pieces]
        )
    ]
    last = []
    for micro in micros:
        piece = add(halves[micro], *mixed[micro])
        blocks = []
        for one in (piece, lax.ppermute(piece, "section", [(0, 1)])):
            kept, passed = own_first(core, one[:, :BLOCK], one[:, BLOCK:])
            blocks += [kept, core_swapped(passed, ctx_count)]
        last.append(in_order(blocks).T)
    results.append(jnp.stack(last))
    return jnp.where(section == 0, results[0], results[1])[None]


def solution(mesh):
    in_specs = (
        P(None, ("ctx", "tp"), None),
        P("section", None),
        P("section", None, "tp"),
        P("section", "ctx", "tp"),
        P("section", "ctx", "tp"),
        P("section", "tp", "ctx"),
        P(),
    )
    out_specs = P("section", None, ("ctx", "tp"), None)
    sizes = mesh.shape
    fits = sizes["section"] == 2 and sizes["tp"] == 2 and sizes["ctx"] == 8
    body = split_heads if fits else local
    return jax.shard_map(body, mesh=mesh, in_specs=in_specs, out_specs=out_specs, check_vma=False)
```

```python
import functools

import numpy as np
import jax
import jax.numpy as jnp
from jax import lax
from jax.experimental import pallas as pl
from jax.experimental.pallas import tpu as pltpu
from jax.sharding import PartitionSpec as P

HEAD_SIZE = 128
WINDOW = 1024
BLOCK = 128


query_scale = 168.0 ** (-0.5)
rope_base = 10000.0


def shifted(shard, axis, by):
    count = lax.axis_size(axis)
    pairs = [(i, i + by) for i in range(count) if 0 <= i + by < count]
    return lax.ppermute(shard, axis, pairs)


def rms_normed(hidden, gain_row):
    widened = hidden.astype(jnp.float32)
    mean_square = jnp.mean(widened * widened, axis=-1, keepdims=True)
    return (widened * lax.rsqrt(mean_square + 1e-06) * gain_row.astype(jnp.float32)).astype(
        jnp.bfloat16
    )


def rotary_apply(tensor, token_position):
    half_dim = tensor.shape[-1] // 2
    frequency = rope_base ** (-(jnp.arange(half_dim, dtype=jnp.float32) * 2.0) / tensor.shape[-1])
    angles = token_position.astype(jnp.float32)[:, None] * frequency[None, :]
    cosine_table = jnp.cos(angles)[:, None, :]
    sine_table = jnp.sin(angles)[:, None, :]
    first_half = tensor[..., :half_dim]
    second_half = tensor[..., half_dim:]
    return jnp.concatenate(
        [
            first_half * cosine_table - second_half * sine_table,
            second_half * cosine_table + first_half * sine_table,
        ],
        axis=-1,
    )


def doc_lookup(ids_row, token_index, block):
    block_count = ids_row.shape[0]
    start_block = jnp.sum((ids_row[None, :] < ids_row[:, None]).astype(jnp.int32), axis=1)
    block_of = jnp.clip(token_index // block, 0, block_count - 1)
    onehot = (block_of[:, None] == jnp.arange(block_count, dtype=jnp.int32)[None, :]).astype(
        jnp.int32
    )
    start_of = jnp.sum(onehot * start_block[None, :], axis=1)
    doc_of = jnp.sum(onehot * ids_row[None, :], axis=1)
    return (token_index - start_of * block, doc_of)


def attention_rows(
    grouped_heads, key_matrix_rows, value_rows, query_index, query_doc, key_index, key_doc
):
    scores = (
        jnp.einsum(
            "qgrd,kgd->grqk", grouped_heads, key_matrix_rows, preferred_element_type=jnp.float32
        )
        * query_scale
    )
    allowed = (key_index[None, :] >= 0) & (key_index[None, :] <= query_index[:, None])
    allowed = (
        allowed
        & (query_index[:, None] - key_index[None, :] < WINDOW)
        & (key_doc[None, :] == query_doc[:, None])
    )
    scores = jnp.where(allowed[None, None], scores, -1e30)
    peak_score = jnp.max(scores, axis=-1, keepdims=True)
    raised = jnp.exp(scores - peak_score)
    weights = (raised / jnp.sum(raised, axis=-1, keepdims=True)).astype(jnp.bfloat16)
    layer_result = jnp.einsum(
        "grqk,kgd->qgrd", weights, value_rows, preferred_element_type=jnp.float32
    )
    return layer_result.astype(jnp.bfloat16).reshape(grouped_heads.shape[0], -1)


def local(x_in, norm_gain, w_query, w_key, value_projection, w_out, doc_ids):
    section_num = lax.axis_index("section")
    section_count = lax.axis_size("section")
    ctx_num = lax.axis_index("ctx")
    ctx_count = lax.axis_size("ctx")
    tp_count = lax.axis_size("tp")
    micro_count, half_rows, model_width = x_in.shape
    key_full, value_full, out_part = (
        lax.all_gather(w_key, "ctx", axis=1, tiled=True),
        lax.all_gather(value_projection, "ctx", axis=1, tiled=True),
        lax.all_gather(w_out, "ctx", axis=2, tiled=True),
    )
    query_weight = w_query[0]
    key_matrix = key_full[0]
    value_matrix = value_full[0]
    out_weight = out_part[0]
    tok_rows = half_rows * tp_count
    gain_row = norm_gain[0]
    query_heads = query_weight.shape[1] // HEAD_SIZE
    kv_heads = key_matrix.shape[1] // HEAD_SIZE
    group_size = query_heads // kv_heads
    reach_hops = min(-(-WINDOW // tok_rows), ctx_count - 1)
    token_index = ctx_num * tok_rows + jnp.arange(tok_rows, dtype=jnp.int32)
    key_index = (ctx_num - reach_hops) * tok_rows + jnp.arange(
        (reach_hops + 1) * tok_rows, dtype=jnp.int32
    )

    def project(operands):
        whole_rows, token_position = operands
        normalized_input = rms_normed(whole_rows, gain_row)
        query_matrix_rows = rotary_apply(
            jnp.dot(normalized_input, query_weight, preferred_element_type=jnp.float32).reshape(
                tok_rows, query_heads, HEAD_SIZE
            ),
            token_position,
        )
        key_matrix_rows = rotary_apply(
            jnp.dot(normalized_input, key_matrix, preferred_element_type=jnp.float32).reshape(
                tok_rows, kv_heads, HEAD_SIZE
            ),
            token_position,
        )
        value_rows = jnp.dot(
            normalized_input, value_matrix, preferred_element_type=jnp.float32
        ).astype(jnp.bfloat16)
        stacked = jnp.stack(
            [
                key_matrix_rows.astype(jnp.bfloat16).reshape(tok_rows, kv_heads * HEAD_SIZE),
                value_rows,
            ]
        )
        return (
            query_matrix_rows.astype(jnp.bfloat16).reshape(tok_rows, query_heads * HEAD_SIZE),
            stacked,
        )

    def skip_project(operands):
        return (
            jnp.zeros((tok_rows, query_heads * HEAD_SIZE), jnp.bfloat16),
            jnp.zeros((2, tok_rows, kv_heads * HEAD_SIZE), jnp.bfloat16),
        )

    def skip_attend(operands):
        return jnp.zeros((tok_rows, query_heads * HEAD_SIZE), jnp.bfloat16)

    def out_local(operands):
        return jnp.dot(operands, out_weight, preferred_element_type=jnp.float32)

    def skip_out(operands):
        return jnp.zeros((operands.shape[0], out_weight.shape[1]), jnp.float32)

    def step(step_num, carry):
        received, results = carry
        micro_num = step_num - section_num
        active = (micro_num >= 0) & (micro_num < micro_count)
        micro_at = jnp.clip(micro_num, 0, micro_count - 1)
        fresh_rows = lax.dynamic_index_in_dim(x_in, micro_at, 0, keepdims=False)
        current = jnp.where(section_num == 0, fresh_rows, received)
        whole_rows = lax.all_gather(current, "tp", axis=0, tiled=True)
        ids_row = lax.dynamic_index_in_dim(doc_ids, micro_at, 0, keepdims=False)
        token_position, query_doc = doc_lookup(ids_row, token_index, BLOCK)
        unused, key_doc = doc_lookup(ids_row, key_index, BLOCK)
        query_matrix_rows, stacked = lax.cond(
            active, project, skip_project, (whole_rows, token_position)
        )
        pieces = [shifted(stacked, "ctx", distance) for distance in range(reach_hops, 0, -1)]
        window_kv = jnp.concatenate(pieces + [stacked], axis=1)

        def attend(operands):
            query_part, window_part = operands
            grouped_heads = query_part.reshape(tok_rows, kv_heads, group_size, HEAD_SIZE)
            key_matrix_rows = window_part[0].reshape(-1, kv_heads, HEAD_SIZE)
            value_rows = window_part[1].reshape(-1, kv_heads, HEAD_SIZE)
            return attention_rows(
                grouped_heads,
                key_matrix_rows,
                value_rows,
                token_index,
                query_doc,
                key_index,
                key_doc,
            )

        attended = lax.cond(active, attend, skip_attend, (query_matrix_rows, window_kv))
        summed = lax.psum_scatter(
            lax.cond(active, out_local, skip_out, attended), "tp", scatter_dimension=0, tiled=True
        )
        updated = (current.astype(jnp.float32) + summed).astype(jnp.bfloat16)
        previous = lax.dynamic_index_in_dim(results, micro_at, 0, keepdims=False)
        results = lax.dynamic_update_index_in_dim(
            results, jnp.where(active, updated, previous), micro_at, 0
        )
        received = shifted(updated, "section", 1)
        return (received, results)

    start_carry = (
        jnp.zeros((half_rows, model_width), jnp.bfloat16),
        jnp.zeros((micro_count, half_rows, model_width), jnp.bfloat16),
    )
    unused_received, results = lax.fori_loop(0, micro_count + section_count - 1, step, start_carry)
    return results[None]


SECTION, CORE, TP, CHIP = range(4)


def swapped(shard, axis):
    return lax.ppermute(shard, axis, [(0, 1), (1, 0)])


def core_swapped(shard, ctx_count):
    return lax.ppermute(shard, "ctx", [(i, i ^ 1) for i in range(ctx_count)])


def chip_xor(shard, ctx_count, by):
    return lax.ppermute(shard, "ctx", [(i, i ^ (2 * by)) for i in range(ctx_count)])


def chip_shift(shard, ctx_count, by):
    return lax.ppermute(
        shard, "ctx", [(i, i + 2 * by) for i in range(ctx_count) if i + 2 * by < ctx_count]
    )


def columns(array, block, width):
    return lax.dynamic_slice_in_dim(array, block * width, width, 1)


def own_first(flag, own, other):
    return jnp.where(flag == 0, own, other), jnp.where(flag == 0, other, own)


def together(*values):
    return lax.optimization_barrier(values)


def call(kernel, scalars, operands, outputs, scratch=(), limit=16, in_hbm=False):
    vmem = pl.BlockSpec(memory_space=pltpu.VMEM)
    smem = pl.BlockSpec(memory_space=pltpu.SMEM)
    place = pl.BlockSpec(memory_space=pltpu.HBM) if in_hbm else vmem
    return list(
        pl.pallas_call(
            kernel,
            out_shape=[jax.ShapeDtypeStruct(shape, kind) for shape, kind in outputs],
            in_specs=[smem] * len(scalars) + [place] * len(operands),
            out_specs=[vmem] * len(outputs),
            scratch_shapes=list(scratch),
            compiler_params=pltpu.CompilerParams(vmem_limit_bytes=limit * 2**20),
            cost_estimate=pl.CostEstimate(flops=1024, bytes_accessed=1024, transcendentals=0),
        )(*scalars, *operands)
    )


def aligned(index, size):
    return pl.ds(pl.multiple_of(index * size, size), size)


def pick_kernel(place, key_ref, value_ref, mine_ref, theirs_ref, sems):
    core, copies = place[CORE], []
    for out_ref, which in ((mine_ref, core), (theirs_ref, 1 - core)):
        for sec in (0, 1):
            for kind, ref in enumerate((key_ref, value_ref)):
                at = (2 * sec + kind) * HEAD_SIZE
                copies.append(
                    pltpu.make_async_copy(
                        ref.at[:, aligned(2 * sec + which, HEAD_SIZE)],
                        out_ref.at[:, at : at + HEAD_SIZE],
                        sems.at[len(copies)],
                    )
                )
    for copy in copies:
        copy.start()
    for copy in copies:
        copy.wait()


def halve_kernel(place, mine_ref, theirs_ref, gain_ref, own_ref, other_ref):
    core, section = place[CORE], place[SECTION]
    rows, pair = mine_ref.shape[0], 2 * HEAD_SIZE
    for out_ref, sec in ((own_ref, section), (other_ref, 1 - section)):
        out_ref[aligned(core, rows), :] = mine_ref[:, aligned(sec, pair)]
        out_ref[aligned(1 - core, rows), :] = theirs_ref[:, aligned(sec, pair)]
    other_ref[2 * rows :, :] = gain_ref[...]


def layers_kernel(place, own_ref, other_ref, first_ref, second_ref):
    rows = own_ref.shape[0]
    for section in (0, 1):

        @pl.when(place[SECTION] == section)
        def _():
            out_refs = (first_ref, second_ref) if section == 0 else (second_ref, first_ref)
            out_refs[0][...] = own_ref[...]
            out_refs[1][...] = other_ref[:rows, :]


def query_columns_kernel(place, weight_ref, out_ref, sems):
    copies = []
    for sec in (0, 1):
        copies.append(
            pltpu.make_async_copy(
                weight_ref.at[:, aligned(2 * sec + place[CORE], 2 * HEAD_SIZE)],
                out_ref.at[:, 2 * sec * HEAD_SIZE : (2 * sec + 2) * HEAD_SIZE],
                sems.at[sec],
            )
        )
    for copy in copies:
        copy.start()
    for copy in copies:
        copy.wait()


def late_kernel(place, gain_ref, query_ref, *refs):
    home, away, (gain_out, query_out, kv_out, wide) = refs[:5], refs[5:9], refs[9:]
    rows = home[0].shape[0] // 4
    at_home = place[SECTION] == 1
    gain = jnp.broadcast_to(gain_ref[...].astype(jnp.float32), (BLOCK, gain_ref.shape[1])).T
    for by, part in enumerate(by_chip(place, home)):
        part = jnp.where(at_home, part, away[by][: 4 * rows, :]).astype(jnp.float32)
        for block in range(4):
            lanes = slice(block * 2 * HEAD_SIZE, (block + 1) * 2 * HEAD_SIZE)
            wide[aligned(place[CHIP] ^ by, rows), lanes] = part[block * rows : (block + 1) * rows]
    kv_out[...] = wide[...].astype(jnp.bfloat16)
    for block in range(4):
        query = []
        for chip in range(4):
            at = slice((4 * chip + block) * rows, (4 * chip + block + 1) * rows)
            gain_out[block, chip * rows : (chip + 1) * rows, :] = gain[at]
            query.append(query_ref[at, :].astype(jnp.float32))
        query_out[block, :, :] = jnp.concatenate(query, axis=0).astype(jnp.bfloat16)


def split_kernel(place, slab_ref, kept_ref, sent_ref, wide):
    rows = kept_ref.shape[0]
    wide[...] = slab_ref[...].astype(jnp.float32)
    for ref, core in ((kept_ref, place[CORE]), (sent_ref, 1 - place[CORE])):
        ref[...] = wide[pl.ds(pl.multiple_of(core * rows, 8), rows), :].astype(ref.dtype)


def sort_kernel(place, kept_ref, got_ref, home_ref, cross_ref):
    for at_home in (False, True):

        @pl.when((place[CORE] == place[SECTION]) == at_home)
        def _():
            home_ref[...] = kept_ref[...] if at_home else got_ref[...]
            cross_ref[...] = got_ref[...] if at_home else kept_ref[...]


def residual_kernel(place, own, core_, out_ref, wide):
    me = 2 * place[SECTION] + place[CORE]
    rows = out_ref.shape[1] // 4
    for micro in range(own.shape[0]):
        for by, ref in enumerate((own, core_)):
            wide[...] = ref[micro].astype(jnp.float32).T
            for chip in range(4):
                at = pl.multiple_of((4 * chip + me) * rows, 8)
                out_ref[micro, chip * rows : (chip + 1) * rows, aligned(place[CORE] ^ by, BLOCK)] = (
                    wide[pl.ds(at, rows), :]
                )


def turned(array, cosine, sine):
    return array * cosine + pltpu.roll(array, HEAD_SIZE // 2, 1) * sine


def rope_tables(inside, tables):
    row_cos, row_sin, block_cos, block_sin = tables
    cosine, sine = [], []
    count = inside.shape[0]
    for at in range(count):
        block = pl.ds(inside[at], 1)
        first, second = block_cos[block, :], block_sin[block, :]
        cosine.append(first * row_cos[...] - second * row_sin[...])
        sine.append(second * row_cos[...] + first * row_sin[...])
    lane = lax.broadcasted_iota(jnp.int32, (count * BLOCK, HEAD_SIZE), 1)
    sine = jnp.concatenate(sine, axis=0)
    return jnp.concatenate(cosine, axis=0), jnp.where(lane < HEAD_SIZE // 2, -sine, sine)


def host_tables(block_count):
    lane = np.arange(HEAD_SIZE) % (HEAD_SIZE // 2)
    frequency = rope_base ** (-(lane * 2.0) / HEAD_SIZE)
    rows = np.arange(BLOCK)[:, None] * frequency
    blocks = np.arange(block_count)[:, None] * (BLOCK * frequency)
    angles = (np.cos(rows), np.sin(rows), np.cos(blocks), np.sin(blocks))
    return [jnp.asarray(one, jnp.float32) for one in angles]


def store_queries(place, query, rope, own_ref, other_ref, row=0):
    heads = [
        turned(query[:, at : at + HEAD_SIZE], *rope).astype(jnp.bfloat16)
        for at in range(0, query.shape[1], HEAD_SIZE)
    ]
    rows = slice(row, row + query.shape[0])
    for sec in (0, 1):

        @pl.when(place[SECTION] == sec)
        def _():
            for out_ref, first in ((own_ref, 2 * sec), (other_ref, 2 - 2 * sec)):
                out_ref[rows, :HEAD_SIZE] = heads[first]
                out_ref[rows, HEAD_SIZE:] = heads[first + 1]


def store_keys(key_value, rope, out_ref, far_ref, rows=(0, 0)):
    size = HEAD_SIZE
    key = turned(key_value[:, :size], *rope).astype(jnp.bfloat16)
    value = key_value[:, size:].astype(jnp.bfloat16)
    out_ref[rows[0] : rows[0] + key.shape[0], :size] = key
    out_ref[rows[0] : rows[0] + key.shape[0], size:] = value
    for micro in range(key.shape[0] // (4 * BLOCK)):
        last = slice((4 * micro + 3) * BLOCK, (4 * micro + 4) * BLOCK)
        to = slice(rows[1] + micro * BLOCK, rows[1] + (micro + 1) * BLOCK)
        far_ref[to, :size] = key[last]
        far_ref[to, size:] = value[last]


def first_query_kernel(micro, place, inside, *refs):
    pieces, tables, (gain, weight), refs = refs[:4], refs[4:8], refs[8:10], refs[10:]
    normed_ref, own_ref, other_ref = refs[-3:]
    step = 16
    for by, ref in enumerate(pieces):
        at = 2 * (place[TP] ^ (by & 1)) + (place[CORE] ^ (by >> 1))
        for row in range(0, BLOCK, step):
            rows = ref[micro, row : row + step, :].astype(jnp.float32)
            mean_square = jnp.mean(rows * rows, axis=-1, keepdims=True)
            rows = rows * lax.rsqrt(mean_square + 1e-06) * gain[...].astype(jnp.float32)
            where = pl.ds(pl.multiple_of(at * BLOCK + row, step), step)
            normed_ref[where, :] = rows.astype(jnp.bfloat16)
    query = jnp.dot(normed_ref[...], weight[...], preferred_element_type=jnp.float32)
    row = micro * normed_ref.shape[0]
    if micro > 0:
        own_ref[:row, :], other_ref[:row, :] = refs[0][:row, :], refs[1][:row, :]
    store_queries(place, query, rope_tables(inside, tables), own_ref, other_ref, row)


def by_chip(place, refs):
    own, across, below, above, far = [ref[...] for ref in refs]
    chip = place[CHIP]
    one = jnp.where(chip % 2 == 0, above, below)
    three = jnp.where(chip == 1, above, jnp.where(chip == 2, below, far))
    return own, one, across, three


def first_keys_kernel(place, inside, first, second, *refs):
    home, away, tables, (out_ref, far_ref, weight) = refs[:5], refs[5:9], refs[9:13], refs[13:]
    at_home = place[SECTION] == 0
    for by, rows in enumerate(by_chip(place, home)):
        rows = jnp.where(at_home, rows, away[by][: rows.shape[0], :])
        weight[aligned(place[CHIP] ^ by, rows.shape[0]), :] = rows
    key_value = jnp.concatenate(
        [
            jnp.dot(one[...], weight[...], preferred_element_type=jnp.float32)
            for one in (first, second)
        ],
        axis=0,
    )
    store_keys(key_value, rope_tables(inside, tables), out_ref, far_ref)


def tn(left, right):
    return lax.dot_general(
        left, right, (((0,), (0,)), ((), ())), preferred_element_type=jnp.float32
    )


def keys_kernel(place, inside, *refs):
    pieces, tables, (gain, weight), refs = refs[:8], refs[8:12], refs[12:14], refs[14:]
    out_ref, far_ref, normed = refs[-3:]
    for ref, before in zip((out_ref, far_ref), refs[:-3]):
        ref[: before.shape[0], :] = before[...]
    me = 2 * place[SECTION] + place[CORE]
    width, step = 4 * pieces[0].shape[0], 56
    for by_tp in (0, 1):
        for half in (0, 1):
            lanes = slice(half * BLOCK, (half + 1) * BLOCK)
            total = jnp.zeros((8, BLOCK), jnp.float32)
            for block in range(4):
                for row in range(0, width // 4, step):
                    one = pieces[2 * block + by_tp][row : row + step, lanes].astype(jnp.float32)
                    total = total + jnp.sum((one * one).reshape(-1, 8, BLOCK), axis=0)
            total = jnp.sum(total, axis=0, keepdims=True)
            scale = lax.rsqrt(total / width + 1e-06)
            at = 2 * (place[TP] ^ by_tp) + half
            for block in range(4):
                one = pieces[2 * block + by_tp][:, lanes].astype(jnp.float32)
                normed[block, :, aligned(at, BLOCK)] = (one * scale * gain[me ^ block]).astype(
                    jnp.bfloat16
                )
    key_value = sum(
        tn(normed[block], weight[:, aligned(me ^ block, 2 * HEAD_SIZE)]) for block in range(4)
    )
    rows = (refs[0].shape[0], refs[1].shape[0]) if len(refs) > 3 else (0, 0)
    store_keys(key_value, rope_tables(inside, tables), out_ref, far_ref, rows)


def query_kernel(place, inside, normed, weight, *refs):
    tables, (own_ref, other_ref) = refs[:4], refs[4:]
    me = 2 * place[SECTION] + place[CORE]
    query = sum(tn(normed[block], weight[me ^ block]) for block in range(4))
    store_queries(place, query, rope_tables(inside, tables), own_ref, other_ref)


def attention_kernel(
    layer, micros, place, low_ref, kept_ref, sent_ref, far_ref, near_ref, own_ref, out_ref, window_ref
):
    size = HEAD_SIZE
    span = 6 * BLOCK
    row = lax.broadcasted_iota(jnp.int32, (2 * BLOCK, span), 0) % BLOCK
    col = lax.broadcasted_iota(jnp.int32, (2 * BLOCK, span), 1)
    back = 5 * BLOCK + row - col
    causal = (back >= 0) & (back < WINDOW)
    home = place[SECTION] == layer
    for micro in micros:
        window_ref[micro, 0:BLOCK, :] = far_ref[micro * BLOCK : (micro + 1) * BLOCK, :]
        places = [(4 * micro + at) * BLOCK for at in (0, 2, 1, 3)]
        for block, at in enumerate(places):
            window_ref[micro, (1 + block) * BLOCK : (2 + block) * BLOCK, :] = near_ref[at : at + BLOCK, :]
            window_ref[micro, (5 + block) * BLOCK : (6 + block) * BLOCK, :] = own_ref[at : at + BLOCK, :]
        for block, at in enumerate(places):
            rows = slice(block * BLOCK, (block + 6) * BLOCK)
            to = at - 4 * micros[0] * BLOCK
            query = jnp.where(home, kept_ref[to : to + BLOCK, :], sent_ref[to : to + BLOCK, :])
            query = jnp.concatenate([query[:, :size], query[:, size:]], axis=0)
            scores = lax.dot_general(
                query,
                window_ref[micro, rows, 0:size],
                (((1,), (1,)), ((), ())),
                preferred_element_type=jnp.float32,
            )
            allowed = causal & (col >= low_ref[4 * micro + block] * BLOCK)
            scores = jnp.where(allowed, scores * query_scale, -1e30)
            raised = jnp.exp(scores - jnp.max(scores, axis=-1, keepdims=True))
            total = jnp.sum(raised, axis=-1, keepdims=True)
            mixed = jnp.dot(
                raised.astype(jnp.bfloat16),
                window_ref[micro, rows, size : 2 * size],
                preferred_element_type=jnp.float32,
            )
            mixed = (mixed / total).astype(jnp.bfloat16)
            out_ref[to : to + BLOCK, 0:size] = mixed[0:BLOCK]
            out_ref[to : to + BLOCK, size : 2 * size] = mixed[BLOCK:]


def gather_kernel(place, *refs):
    parts, (out_ref, wide) = refs[:4], refs[4:]
    for by, ref in enumerate(parts):
        wide[aligned(place[CHIP] ^ by, ref.shape[0]), :] = ref[...].astype(jnp.float32)
    out_ref[...] = wide[...].astype(out_ref.dtype)


def mix_kernel(place, own, core_, across, both, weight, *out_refs):
    me = 2 * place[SECTION] + place[CORE]
    weights = [weight[:, aligned(me ^ by, 2 * HEAD_SIZE)] for by in range(4)]
    for at, out_ref in enumerate(out_refs):
        half = out_ref.shape[1]
        tp = place[TP] if at % 2 == 0 else 1 - place[TP]
        total = sum(
            lax.dot_general(
                weights[by],
                ref[aligned(2 * (at // 2) + tp, half), :],
                (((1,), (1,)), ((), ())),
                preferred_element_type=jnp.float32,
            )
            for by, ref in enumerate((own, core_, across, both))
        )
        out_ref[...] = total.astype(out_ref.dtype)


def add_kernel(residual, keep, arrived, out_ref):
    total = residual[...].astype(jnp.float32) + keep[...] + arrived[...].astype(jnp.float32)
    out_ref[...] = total.astype(out_ref.dtype)


def split_heads(x_in, norm_gain, w_query, w_key, value_projection, w_out, doc_ids):
    section = lax.axis_index("section")
    ctx = lax.axis_index("ctx")
    tp = lax.axis_index("tp")
    ctx_count = lax.axis_size("ctx")
    chips = ctx_count // 2
    chip, core = ctx // 2, ctx % 2
    place = jnp.stack([section, core, tp, chip]).astype(jnp.int32)
    micro_count, half_rows, width = x_in.shape
    tokens = 4 * half_rows
    slab = width // ctx_count
    head, pair = HEAD_SIZE, 2 * HEAD_SIZE
    block_rows = width // 4
    micros = range(micro_count)
    b16, f32 = jnp.bfloat16, jnp.float32

    def across_chips(shard):
        return [chip_xor(shard, ctx_count, by) for by in range(1, chips)]

    def whole(parts):
        rows, columns = parts[0].shape
        return call(
            gather_kernel,
            [place],
            parts,
            [((chips * rows, columns), b16)],
            [pltpu.VMEM((chips * rows, columns), f32)],
        )[0]

    x_tp = swapped(x_in, "tp")
    x_core = core_swapped(x_in, ctx_count)

    mine, theirs = call(
        pick_kernel,
        [place],
        [w_key[0], value_projection[0]],
        [((slab, 2 * pair), b16)] * 2,
        [pltpu.SemaphoreType.DMA((8,))],
        in_hbm=True,
    )
    theirs = core_swapped(theirs, ctx_count)
    gain_rows = jnp.pad(norm_gain[0], (0, 16 * pair - width)).reshape(16, pair)
    kv_own, kv_other = call(
        halve_kernel,
        [place],
        [mine, theirs, gain_rows],
        [((2 * slab, pair), b16), ((2 * slab + 16, pair), b16)],
    )
    kv_other = swapped(kv_other, "section")

    home_parts = [
        chip_xor(kv_own, ctx_count, 2),
        chip_shift(kv_own, ctx_count, 1),
        lax.ppermute(kv_own, "ctx", [(i, i - 2) for i in range(2, ctx_count)]),
    ]
    home_parts[1], later = together(home_parts[1], place)
    query_weight = call(
        query_columns_kernel,
        [later],
        [w_query[0]],
        [((width, 2 * pair), b16)],
        [pltpu.SemaphoreType.DMA((2,))],
        in_hbm=True,
    )[0]
    *home_parts, kv_other, query_weight, later = together(
        *home_parts, kv_other, query_weight, place
    )
    home_parts.append(
        lax.ppermute(home_parts[0], "ctx", [(2, 0), (3, 1), (4, 6), (5, 7)])
    )
    gain_other = kv_other[2 * slab :].reshape(-1)[:width]
    gains = own_first(section, norm_gain[0], gain_other)
    away_parts = across_chips(kv_other)

    start = jnp.sum((doc_ids[:, None, :] < doc_ids[:, :, None]).astype(jnp.int32), axis=2)
    chip_start = lax.dynamic_slice_in_dim(start, chip * 4, 4, 1)
    inside = chip * 4 + jnp.arange(4, dtype=jnp.int32)[None, :] - chip_start
    lows = 5 - inside
    order = inside.reshape(micro_count, 2, 2).transpose(0, 2, 1).reshape(micro_count, 4)
    tables = host_tables(doc_ids.shape[1])

    def by_block(weight):
        columns = weight.shape[1]
        weight = weight.reshape(chips, 4, slab // 2, columns).transpose(1, 0, 2, 3)
        return weight.reshape(4, block_rows, columns)

    def shifted(key_value, far):
        return chip_shift(key_value, ctx_count, 1), chip_shift(far, ctx_count, 2)

    def sent_over(layer, queries):
        return lax.ppermute(queries, "section", [(layer, 1 - layer)])

    def attend(layer, which, low, query, key_value, window):
        own, sent = query
        near, far = window
        return call(
            functools.partial(attention_kernel, layer, which),
            [place, low],
            [own, sent, far, near, key_value],
            [(own.shape, b16)],
            [pltpu.VMEM((micro_count, 9 * BLOCK, pair), b16)],
        )[0]

    def mix(attended, across, out_weight):
        shape = (block_rows, tokens // 2)
        return call(
            mix_kernel,
            [place],
            [
                attended,
                core_swapped(attended, ctx_count),
                across,
                core_swapped(across, ctx_count),
                out_weight,
            ],
            [(shape, f32), (shape, b16)] * (attended.shape[0] // tokens),
            )

    def add(residual, keep, send):
        return call(add_kernel, [], [residual, keep, swapped(send, "tp")], [(send.shape, b16)])[0]

    def spread(piece, direct):
        over_tp, over_section = swapped(piece, "tp"), swapped(piece, "section")
        if direct:
            over_both = lax.ppermute(piece, ("section", "tp"), [(i, 3 - i) for i in range(4)])
        else:
            over_both = swapped(over_tp, "section")
        return [piece, over_tp, over_section, over_both]

    def both_cores(pieces):
        over = [core_swapped(one, ctx_count) for one in pieces]
        return pieces[:2] + over[:2] + pieces[2:] + over[2:]

    def in_order(blocks):
        by_section = [own_first(core, blocks[0], blocks[1]), own_first(core, blocks[2], blocks[3])]
        low = own_first(section, by_section[0][0], by_section[1][0])
        high = own_first(section, by_section[0][1], by_section[1][1])
        whole = jnp.stack([low[0], high[0], low[1], high[1]])
        count = whole.shape[-1]
        whole = whole.reshape(4, chips, slab // 2, count).transpose(1, 0, 2, 3)
        return whole.reshape(width, count)

    half_shape = ((slab // 2, w_out.shape[1]), b16)
    kept, sent = call(
        split_kernel,
        [later],
        [w_out[0].T],
        [half_shape] * 2,
        [pltpu.VMEM((slab, w_out.shape[1]), f32)],
    )
    own_half, cross_half = call(
        sort_kernel, [place], [kept, core_swapped(sent, ctx_count)], [half_shape] * 2
    )
    cross_half = swapped(cross_half, "section")
    x_tp, later = together(x_tp, later)
    x_both = core_swapped(x_tp, ctx_count)
    rows = (micro_count * tokens, pair)
    normed, query = [], []
    for micro in micros:
        one, *query = call(
            functools.partial(first_query_kernel, micro),
            [place, order[micro]],
            [x_in, x_tp, x_core, x_both, *tables, gains[0][None], query_weight, *query],
            [((tokens, width), b16), (rows, b16), (rows, b16)],
        )
        normed.append(one)
    *away_parts, home_parts[3], cross_half, normed[0], normed[1] = together(
        *away_parts, home_parts[3], cross_half, *normed
    )
    home_parts, away_parts = [kv_own, *home_parts], [kv_other, *away_parts]
    out_halves = call(layers_kernel, [place], [own_half, cross_half], [(own_half.shape, b16)] * 2)
    key, far = call(
        first_keys_kernel,
        [place, order.reshape(-1)],
        [*normed, *home_parts, *away_parts, *tables],
        [(rows, b16), ((micro_count * BLOCK, pair), b16)],
        [pltpu.VMEM((width, pair), b16)],
    )
    window = shifted(key, far)

    key, out_half, later = together(key, out_halves[0], place)
    out_parts = across_chips(out_half)
    query = query[0], sent_over(0, query[1])
    attended = attend(0, micros, lows.reshape(-1), query, key, window)
    across = swapped(attended, "section")
    (residuals,) = call(
        residual_kernel,
        [later],
        [x_in, x_core],
        [((micro_count, block_rows, tokens // 2), f32)],
        [pltpu.VMEM((width, BLOCK), f32)],
    )
    late_gain, late_query_weight, next_kv = call(
        late_kernel,
        [later],
        [gains[1][None], query_weight, *home_parts, *away_parts],
        [
            ((4, block_rows, BLOCK), f32),
            ((4, block_rows, 2 * pair), b16),
            ((block_rows, 4 * pair), b16),
        ],
        [pltpu.VMEM((block_rows, 4 * pair), f32)],
    )
    *out_parts, across, next_kv, residuals = together(*out_parts, across, next_kv, residuals)
    out_weight = whole([out_half, *out_parts])
    mixed = mix(attended, across, out_weight)
    mixed[1], mixed[3], out_half = together(mixed[1], mixed[3], out_halves[1])
    out_parts = across_chips(out_half)
    halves = [add(residuals[m], *mixed[2 * m : 2 * m + 2]) for m in micros]
    spreads = [spread(halves[0], True)]
    halves[1], spreads[0][1], spreads[0][2], out_parts[0], out_parts[1] = together(
        halves[1], *spreads[0][1:3], *out_parts[:2]
    )
    spreads.append(spread(halves[1], False))
    *spreads[0][1:], spreads[1][1], spreads[1][2] = together(*spreads[0][1:], *spreads[1][1:3])
    *spreads[0][1:], out_parts[2] = together(*spreads[0][1:], out_parts[2])
    next_out = whole([out_half, *out_parts])

    pieces, queries, before = [], [], []
    for micro in micros:
        pieces.append(both_cores(spreads[micro]))
        *before, normed = call(
            keys_kernel,
            [place, order[micro]],
            [*pieces[micro], *tables, late_gain, next_kv, *before],
            [
                (((micro + 1) * tokens, pair), b16),
                (((micro + 1) * BLOCK, pair), b16),
                ((4, block_rows, tokens), b16),
            ],
        )
        normed, before[0] = together(normed, before[0])
        query = call(
            query_kernel,
            [place, order[micro]],
            [normed, late_query_weight, *tables],
            [((tokens, pair), b16)] * 2,
        )
        queries.append(query)
        if micro == 0:
            query[0], *spreads[1] = together(query[0], *spreads[1])
    key, far = before
    window = shifted(key, far)
    queries = [(own, sent_over(1, other)) for own, other in queries]
    near, far, first, second, next_out = together(
        *window, *[sent for _, sent in queries], next_out
    )
    queries = [(queries[0][0], first), (queries[1][0], second)]
    attended = [attend(1, (m,), lows.reshape(-1), queries[m], key, (near, far)) for m in micros]
    across = [swapped(one, "section") for one in attended]
    across[0], attended[1] = together(across[0], attended[1])
    mixed = [mix(attended[0], across[0], next_out)]
    mixed[0][0], across[1] = together(mixed[0][0], across[1])
    mixed.append(mix(attended[1], across[1], next_out))
    results = [
        jnp.stack(
            [in_order([columns(one[2 * i], core, BLOCK) for i in range(4)]).T for one in pieces]
        )
    ]
    last = []
    for micro in micros:
        piece = add(halves[micro], *mixed[micro])
        blocks = []
        for one in (piece, lax.ppermute(piece, "section", [(0, 1)])):
            kept, passed = own_first(core, one[:, :BLOCK], one[:, BLOCK:])
            blocks += [kept, core_swapped(passed, ctx_count)]
        last.append(in_order(blocks).T)
    results.append(jnp.stack(last))
    return jnp.where(section == 0, results[0], results[1])[None]


def solution(mesh):
    in_specs = (
        P(None, ("ctx", "tp"), None),
        P("section", None),
        P("section", None, "tp"),
        P("section", "ctx", "tp"),
        P("section", "ctx", "tp"),
        P("section", "tp", "ctx"),
        P(),
    )
    out_specs = P("section", None, ("ctx", "tp"), None)
    sizes = mesh.shape
    fits = sizes["section"] == 2 and sizes["tp"] == 2 and sizes["ctx"] == 8
    body = split_heads if fits else local
    return jax.shard_map(body, mesh=mesh, in_specs=in_specs, out_specs=out_specs, check_vma=False)
```

```python
import functools

import numpy as np
import jax
import jax.numpy as jnp
from jax import lax
from jax.experimental import pallas as pl
from jax.experimental.pallas import tpu as pltpu
from jax.sharding import PartitionSpec as P

HEAD_SIZE = 128
WINDOW = 1024
BLOCK = 128


query_scale = 168.0 ** (-0.5)
rope_base = 10000.0


def shifted(shard, axis, by):
    count = lax.axis_size(axis)
    pairs = [(i, i + by) for i in range(count) if 0 <= i + by < count]
    return lax.ppermute(shard, axis, pairs)


def rms_normed(hidden, gain_row):
    widened = hidden.astype(jnp.float32)
    mean_square = jnp.mean(widened * widened, axis=-1, keepdims=True)
    return (widened * lax.rsqrt(mean_square + 1e-06) * gain_row.astype(jnp.float32)).astype(
        jnp.bfloat16
    )


def rotary_apply(tensor, token_position):
    half_dim = tensor.shape[-1] // 2
    frequency = rope_base ** (-(jnp.arange(half_dim, dtype=jnp.float32) * 2.0) / tensor.shape[-1])
    angles = token_position.astype(jnp.float32)[:, None] * frequency[None, :]
    cosine_table = jnp.cos(angles)[:, None, :]
    sine_table = jnp.sin(angles)[:, None, :]
    first_half = tensor[..., :half_dim]
    second_half = tensor[..., half_dim:]
    return jnp.concatenate(
        [
            first_half * cosine_table - second_half * sine_table,
            second_half * cosine_table + first_half * sine_table,
        ],
        axis=-1,
    )


def doc_lookup(ids_row, token_index, block):
    block_count = ids_row.shape[0]
    start_block = jnp.sum((ids_row[None, :] < ids_row[:, None]).astype(jnp.int32), axis=1)
    block_of = jnp.clip(token_index // block, 0, block_count - 1)
    onehot = (block_of[:, None] == jnp.arange(block_count, dtype=jnp.int32)[None, :]).astype(
        jnp.int32
    )
    start_of = jnp.sum(onehot * start_block[None, :], axis=1)
    doc_of = jnp.sum(onehot * ids_row[None, :], axis=1)
    return (token_index - start_of * block, doc_of)


def attention_rows(
    grouped_heads, key_matrix_rows, value_rows, query_index, query_doc, key_index, key_doc
):
    scores = (
        jnp.einsum(
            "qgrd,kgd->grqk", grouped_heads, key_matrix_rows, preferred_element_type=jnp.float32
        )
        * query_scale
    )
    allowed = (key_index[None, :] >= 0) & (key_index[None, :] <= query_index[:, None])
    allowed = (
        allowed
        & (query_index[:, None] - key_index[None, :] < WINDOW)
        & (key_doc[None, :] == query_doc[:, None])
    )
    scores = jnp.where(allowed[None, None], scores, -1e30)
    peak_score = jnp.max(scores, axis=-1, keepdims=True)
    raised = jnp.exp(scores - peak_score)
    weights = (raised / jnp.sum(raised, axis=-1, keepdims=True)).astype(jnp.bfloat16)
    layer_result = jnp.einsum(
        "grqk,kgd->qgrd", weights, value_rows, preferred_element_type=jnp.float32
    )
    return layer_result.astype(jnp.bfloat16).reshape(grouped_heads.shape[0], -1)


def local(x_in, norm_gain, w_query, w_key, value_projection, w_out, doc_ids):
    section_num = lax.axis_index("section")
    section_count = lax.axis_size("section")
    ctx_num = lax.axis_index("ctx")
    ctx_count = lax.axis_size("ctx")
    tp_count = lax.axis_size("tp")
    micro_count, half_rows, model_width = x_in.shape
    key_full, value_full, out_part = (
        lax.all_gather(w_key, "ctx", axis=1, tiled=True),
        lax.all_gather(value_projection, "ctx", axis=1, tiled=True),
        lax.all_gather(w_out, "ctx", axis=2, tiled=True),
    )
    query_weight = w_query[0]
    key_matrix = key_full[0]
    value_matrix = value_full[0]
    out_weight = out_part[0]
    tok_rows = half_rows * tp_count
    gain_row = norm_gain[0]
    query_heads = query_weight.shape[1] // HEAD_SIZE
    kv_heads = key_matrix.shape[1] // HEAD_SIZE
    group_size = query_heads // kv_heads
    reach_hops = min(-(-WINDOW // tok_rows), ctx_count - 1)
    token_index = ctx_num * tok_rows + jnp.arange(tok_rows, dtype=jnp.int32)
    key_index = (ctx_num - reach_hops) * tok_rows + jnp.arange(
        (reach_hops + 1) * tok_rows, dtype=jnp.int32
    )

    def project(operands):
        whole_rows, token_position = operands
        normalized_input = rms_normed(whole_rows, gain_row)
        query_matrix_rows = rotary_apply(
            jnp.dot(normalized_input, query_weight, preferred_element_type=jnp.float32).reshape(
                tok_rows, query_heads, HEAD_SIZE
            ),
            token_position,
        )
        key_matrix_rows = rotary_apply(
            jnp.dot(normalized_input, key_matrix, preferred_element_type=jnp.float32).reshape(
                tok_rows, kv_heads, HEAD_SIZE
            ),
            token_position,
        )
        value_rows = jnp.dot(
            normalized_input, value_matrix, preferred_element_type=jnp.float32
        ).astype(jnp.bfloat16)
        stacked = jnp.stack(
            [
                key_matrix_rows.astype(jnp.bfloat16).reshape(tok_rows, kv_heads * HEAD_SIZE),
                value_rows,
            ]
        )
        return (
            query_matrix_rows.astype(jnp.bfloat16).reshape(tok_rows, query_heads * HEAD_SIZE),
            stacked,
        )

    def skip_project(operands):
        return (
            jnp.zeros((tok_rows, query_heads * HEAD_SIZE), jnp.bfloat16),
            jnp.zeros((2, tok_rows, kv_heads * HEAD_SIZE), jnp.bfloat16),
        )

    def skip_attend(operands):
        return jnp.zeros((tok_rows, query_heads * HEAD_SIZE), jnp.bfloat16)

    def out_local(operands):
        return jnp.dot(operands, out_weight, preferred_element_type=jnp.float32)

    def skip_out(operands):
        return jnp.zeros((operands.shape[0], out_weight.shape[1]), jnp.float32)

    def step(step_num, carry):
        received, results = carry
        micro_num = step_num - section_num
        active = (micro_num >= 0) & (micro_num < micro_count)
        micro_at = jnp.clip(micro_num, 0, micro_count - 1)
        fresh_rows = lax.dynamic_index_in_dim(x_in, micro_at, 0, keepdims=False)
        current = jnp.where(section_num == 0, fresh_rows, received)
        whole_rows = lax.all_gather(current, "tp", axis=0, tiled=True)
        ids_row = lax.dynamic_index_in_dim(doc_ids, micro_at, 0, keepdims=False)
        token_position, query_doc = doc_lookup(ids_row, token_index, BLOCK)
        unused, key_doc = doc_lookup(ids_row, key_index, BLOCK)
        query_matrix_rows, stacked = lax.cond(
            active, project, skip_project, (whole_rows, token_position)
        )
        pieces = [shifted(stacked, "ctx", distance) for distance in range(reach_hops, 0, -1)]
        window_kv = jnp.concatenate(pieces + [stacked], axis=1)

        def attend(operands):
            query_part, window_part = operands
            grouped_heads = query_part.reshape(tok_rows, kv_heads, group_size, HEAD_SIZE)
            key_matrix_rows = window_part[0].reshape(-1, kv_heads, HEAD_SIZE)
            value_rows = window_part[1].reshape(-1, kv_heads, HEAD_SIZE)
            return attention_rows(
                grouped_heads,
                key_matrix_rows,
                value_rows,
                token_index,
                query_doc,
                key_index,
                key_doc,
            )

        attended = lax.cond(active, attend, skip_attend, (query_matrix_rows, window_kv))
        summed = lax.psum_scatter(
            lax.cond(active, out_local, skip_out, attended), "tp", scatter_dimension=0, tiled=True
        )
        updated = (current.astype(jnp.float32) + summed).astype(jnp.bfloat16)
        previous = lax.dynamic_index_in_dim(results, micro_at, 0, keepdims=False)
        results = lax.dynamic_update_index_in_dim(
            results, jnp.where(active, updated, previous), micro_at, 0
        )
        received = shifted(updated, "section", 1)
        return (received, results)

    start_carry = (
        jnp.zeros((half_rows, model_width), jnp.bfloat16),
        jnp.zeros((micro_count, half_rows, model_width), jnp.bfloat16),
    )
    unused_received, results = lax.fori_loop(0, micro_count + section_count - 1, step, start_carry)
    return results[None]


SECTION, CORE, TP, CHIP = range(4)


def swapped(shard, axis):
    return lax.ppermute(shard, axis, [(0, 1), (1, 0)])


def core_swapped(shard, ctx_count):
    return lax.ppermute(shard, "ctx", [(i, i ^ 1) for i in range(ctx_count)])


def chip_xor(shard, ctx_count, by):
    return lax.ppermute(shard, "ctx", [(i, i ^ (2 * by)) for i in range(ctx_count)])


def chip_shift(shard, ctx_count, by):
    return lax.ppermute(
        shard, "ctx", [(i, i + 2 * by) for i in range(ctx_count) if i + 2 * by < ctx_count]
    )


def columns(array, block, width):
    return lax.dynamic_slice_in_dim(array, block * width, width, 1)


def own_first(flag, own, other):
    return jnp.where(flag == 0, own, other), jnp.where(flag == 0, other, own)


def together(*values):
    return lax.optimization_barrier(values)


def call(kernel, scalars, operands, outputs, scratch=(), limit=16, in_hbm=False):
    vmem = pl.BlockSpec(memory_space=pltpu.VMEM)
    smem = pl.BlockSpec(memory_space=pltpu.SMEM)
    place = pl.BlockSpec(memory_space=pltpu.HBM) if in_hbm else vmem
    return list(
        pl.pallas_call(
            kernel,
            out_shape=[jax.ShapeDtypeStruct(shape, kind) for shape, kind in outputs],
            in_specs=[smem] * len(scalars) + [place] * len(operands),
            out_specs=[vmem] * len(outputs),
            scratch_shapes=list(scratch),
            compiler_params=pltpu.CompilerParams(vmem_limit_bytes=limit * 2**20),
            cost_estimate=pl.CostEstimate(flops=1024, bytes_accessed=1024, transcendentals=0),
        )(*scalars, *operands)
    )


def aligned(index, size):
    return pl.ds(pl.multiple_of(index * size, size), size)


def pick_kernel(place, key_ref, value_ref, mine_ref, theirs_ref, sems):
    core, copies = place[CORE], []
    for out_ref, which in ((mine_ref, core), (theirs_ref, 1 - core)):
        for sec in (0, 1):
            for kind, ref in enumerate((key_ref, value_ref)):
                at = (2 * sec + kind) * HEAD_SIZE
                copies.append(
                    pltpu.make_async_copy(
                        ref.at[:, aligned(2 * sec + which, HEAD_SIZE)],
                        out_ref.at[:, at : at + HEAD_SIZE],
                        sems.at[len(copies)],
                    )
                )
    for copy in copies:
        copy.start()
    for copy in copies:
        copy.wait()


def halve_kernel(place, mine_ref, theirs_ref, gain_ref, own_ref, other_ref):
    core, section = place[CORE], place[SECTION]
    rows, pair = mine_ref.shape[0], 2 * HEAD_SIZE
    for out_ref, sec in ((own_ref, section), (other_ref, 1 - section)):
        out_ref[aligned(core, rows), :] = mine_ref[:, aligned(sec, pair)]
        out_ref[aligned(1 - core, rows), :] = theirs_ref[:, aligned(sec, pair)]
    other_ref[2 * rows :, :] = gain_ref[...]


def layers_kernel(place, own_ref, other_ref, first_ref, second_ref):
    rows = own_ref.shape[0]
    for section in (0, 1):

        @pl.when(place[SECTION] == section)
        def _():
            out_refs = (first_ref, second_ref) if section == 0 else (second_ref, first_ref)
            out_refs[0][...] = own_ref[...]
            out_refs[1][...] = other_ref[:rows, :]


def query_columns_kernel(place, weight_ref, out_ref, sems):
    copies = []
    for sec in (0, 1):
        copies.append(
            pltpu.make_async_copy(
                weight_ref.at[:, aligned(2 * sec + place[CORE], 2 * HEAD_SIZE)],
                out_ref.at[:, 2 * sec * HEAD_SIZE : (2 * sec + 2) * HEAD_SIZE],
                sems.at[sec],
            )
        )
    for copy in copies:
        copy.start()
    for copy in copies:
        copy.wait()


def late_kernel(place, gain_ref, query_ref, *refs):
    home, away, (gain_out, query_out, kv_out, wide) = refs[:5], refs[5:9], refs[9:]
    rows = home[0].shape[0] // 4
    at_home = place[SECTION] == 1
    gain = jnp.broadcast_to(gain_ref[...].astype(jnp.float32), (BLOCK, gain_ref.shape[1])).T
    for by, part in enumerate(by_chip(place, home)):
        part = jnp.where(at_home, part, away[by][: 4 * rows, :]).astype(jnp.float32)
        for block in range(4):
            lanes = slice(block * 2 * HEAD_SIZE, (block + 1) * 2 * HEAD_SIZE)
            wide[aligned(place[CHIP] ^ by, rows), lanes] = part[block * rows : (block + 1) * rows]
    kv_out[...] = wide[...].astype(jnp.bfloat16)
    for block in range(4):
        query = []
        for chip in range(4):
            at = slice((4 * chip + block) * rows, (4 * chip + block + 1) * rows)
            gain_out[block, chip * rows : (chip + 1) * rows, :] = gain[at]
            query.append(query_ref[at, :].astype(jnp.float32))
        query_out[block, :, :] = jnp.concatenate(query, axis=0).astype(jnp.bfloat16)


def split_kernel(place, slab_ref, kept_ref, sent_ref, wide):
    rows = kept_ref.shape[0]
    wide[...] = slab_ref[...].astype(jnp.float32)
    for ref, core in ((kept_ref, place[CORE]), (sent_ref, 1 - place[CORE])):
        ref[...] = wide[pl.ds(pl.multiple_of(core * rows, 8), rows), :].astype(ref.dtype)


def sort_kernel(place, kept_ref, got_ref, home_ref, cross_ref):
    for at_home in (False, True):

        @pl.when((place[CORE] == place[SECTION]) == at_home)
        def _():
            home_ref[...] = kept_ref[...] if at_home else got_ref[...]
            cross_ref[...] = got_ref[...] if at_home else kept_ref[...]


def residual_kernel(place, own, core_, out_ref, wide):
    me = 2 * place[SECTION] + place[CORE]
    rows = out_ref.shape[1] // 4
    for micro in range(own.shape[0]):
        for by, ref in enumerate((own, core_)):
            wide[...] = ref[micro].astype(jnp.float32).T
            for chip in range(4):
                at = pl.multiple_of((4 * chip + me) * rows, 8)
                out_ref[micro, chip * rows : (chip + 1) * rows, aligned(place[CORE] ^ by, BLOCK)] = (
                    wide[pl.ds(at, rows), :]
                )


def turned(array, cosine, sine):
    return array * cosine + pltpu.roll(array, HEAD_SIZE // 2, 1) * sine


def rope_tables(inside, tables):
    row_cos, row_sin, block_cos, block_sin = tables
    cosine, sine = [], []
    count = inside.shape[0]
    for at in range(count):
        block = pl.ds(inside[at], 1)
        first, second = block_cos[block, :], block_sin[block, :]
        cosine.append(first * row_cos[...] - second * row_sin[...])
        sine.append(second * row_cos[...] + first * row_sin[...])
    lane = lax.broadcasted_iota(jnp.int32, (count * BLOCK, HEAD_SIZE), 1)
    sine = jnp.concatenate(sine, axis=0)
    return jnp.concatenate(cosine, axis=0), jnp.where(lane < HEAD_SIZE // 2, -sine, sine)


def host_tables(block_count):
    lane = np.arange(HEAD_SIZE) % (HEAD_SIZE // 2)
    frequency = rope_base ** (-(lane * 2.0) / HEAD_SIZE)
    rows = np.arange(BLOCK)[:, None] * frequency
    blocks = np.arange(block_count)[:, None] * (BLOCK * frequency)
    angles = (np.cos(rows), np.sin(rows), np.cos(blocks), np.sin(blocks))
    return [jnp.asarray(one, jnp.float32) for one in angles]


def store_queries(place, query, rope, own_ref, other_ref, row=0):
    heads = [
        turned(query[:, at : at + HEAD_SIZE], *rope).astype(jnp.bfloat16)
        for at in range(0, query.shape[1], HEAD_SIZE)
    ]
    rows = slice(row, row + query.shape[0])
    for sec in (0, 1):

        @pl.when(place[SECTION] == sec)
        def _():
            for out_ref, first in ((own_ref, 2 * sec), (other_ref, 2 - 2 * sec)):
                out_ref[rows, :HEAD_SIZE] = heads[first]
                out_ref[rows, HEAD_SIZE:] = heads[first + 1]


def store_keys(key_value, rope, out_ref, far_ref, rows=(0, 0)):
    size = HEAD_SIZE
    key = turned(key_value[:, :size], *rope).astype(jnp.bfloat16)
    value = key_value[:, size:].astype(jnp.bfloat16)
    out_ref[rows[0] : rows[0] + key.shape[0], :size] = key
    out_ref[rows[0] : rows[0] + key.shape[0], size:] = value
    for micro in range(key.shape[0] // (4 * BLOCK)):
        last = slice((4 * micro + 3) * BLOCK, (4 * micro + 4) * BLOCK)
        to = slice(rows[1] + micro * BLOCK, rows[1] + (micro + 1) * BLOCK)
        far_ref[to, :size] = key[last]
        far_ref[to, size:] = value[last]


def first_query_kernel(micro, place, inside, *refs):
    pieces, tables, (gain, weight), refs = refs[:4], refs[4:8], refs[8:10], refs[10:]
    normed_ref, own_ref, other_ref = refs[-3:]
    step = 16
    for by, ref in enumerate(pieces):
        at = 2 * (place[TP] ^ (by & 1)) + (place[CORE] ^ (by >> 1))
        for row in range(0, BLOCK, step):
            rows = ref[micro, row : row + step, :].astype(jnp.float32)
            mean_square = jnp.mean(rows * rows, axis=-1, keepdims=True)
            rows = rows * lax.rsqrt(mean_square + 1e-06) * gain[...].astype(jnp.float32)
            where = pl.ds(pl.multiple_of(at * BLOCK + row, step), step)
            normed_ref[where, :] = rows.astype(jnp.bfloat16)
    query = jnp.dot(normed_ref[...], weight[...], preferred_element_type=jnp.float32)
    row = micro * normed_ref.shape[0]
    if micro > 0:
        own_ref[:row, :], other_ref[:row, :] = refs[0][:row, :], refs[1][:row, :]
    store_queries(place, query, rope_tables(inside, tables), own_ref, other_ref, row)


def by_chip(place, refs):
    own, across, below, above, far = [ref[...] for ref in refs]
    chip = place[CHIP]
    one = jnp.where(chip % 2 == 0, above, below)
    three = jnp.where(chip == 1, above, jnp.where(chip == 2, below, far))
    return own, one, across, three


def first_keys_kernel(place, inside, first, second, *refs):
    home, away, tables, (out_ref, far_ref, weight) = refs[:5], refs[5:9], refs[9:13], refs[13:]
    at_home = place[SECTION] == 0
    for by, rows in enumerate(by_chip(place, home)):
        rows = jnp.where(at_home, rows, away[by][: rows.shape[0], :])
        weight[aligned(place[CHIP] ^ by, rows.shape[0]), :] = rows
    key_value = jnp.concatenate(
        [
            jnp.dot(one[...], weight[...], preferred_element_type=jnp.float32)
            for one in (first, second)
        ],
        axis=0,
    )
    store_keys(key_value, rope_tables(inside, tables), out_ref, far_ref)


def tn(left, right):
    return lax.dot_general(
        left, right, (((0,), (0,)), ((), ())), preferred_element_type=jnp.float32
    )


def keys_kernel(place, inside, *refs):
    pieces, tables, (gain, weight), refs = refs[:8], refs[8:12], refs[12:14], refs[14:]
    out_ref, far_ref, normed = refs[-3:]
    for ref, before in zip((out_ref, far_ref), refs[:-3]):
        ref[: before.shape[0], :] = before[...]
    me = 2 * place[SECTION] + place[CORE]
    width, step = 4 * pieces[0].shape[0], 56
    for by_tp in (0, 1):
        for half in (0, 1):
            lanes = slice(half * BLOCK, (half + 1) * BLOCK)
            total = jnp.zeros((8, BLOCK), jnp.float32)
            for block in range(4):
                for row in range(0, width // 4, step):
                    one = pieces[2 * block + by_tp][row : row + step, lanes].astype(jnp.float32)
                    total = total + jnp.sum((one * one).reshape(-1, 8, BLOCK), axis=0)
            total = jnp.sum(total, axis=0, keepdims=True)
            scale = lax.rsqrt(total / width + 1e-06)
            at = 2 * (place[TP] ^ by_tp) + half
            for block in range(4):
                one = pieces[2 * block + by_tp][:, lanes].astype(jnp.float32)
                normed[block, :, aligned(at, BLOCK)] = (one * scale * gain[me ^ block]).astype(
                    jnp.bfloat16
                )
    key_value = sum(
        tn(normed[block], weight[:, aligned(me ^ block, 2 * HEAD_SIZE)]) for block in range(4)
    )
    rows = (refs[0].shape[0], refs[1].shape[0]) if len(refs) > 3 else (0, 0)
    store_keys(key_value, rope_tables(inside, tables), out_ref, far_ref, rows)


def query_kernel(place, inside, normed, weight, *refs):
    tables, (own_ref, other_ref) = refs[:4], refs[4:]
    me = 2 * place[SECTION] + place[CORE]
    query = sum(tn(normed[block], weight[me ^ block]) for block in range(4))
    store_queries(place, query, rope_tables(inside, tables), own_ref, other_ref)


def attention_kernel(
    layer, micros, place, low_ref, kept_ref, sent_ref, far_ref, near_ref, own_ref, out_ref, window_ref
):
    size = HEAD_SIZE
    span = 6 * BLOCK
    row = lax.broadcasted_iota(jnp.int32, (2 * BLOCK, span), 0) % BLOCK
    col = lax.broadcasted_iota(jnp.int32, (2 * BLOCK, span), 1)
    back = 5 * BLOCK + row - col
    causal = (back >= 0) & (back < WINDOW)
    home = place[SECTION] == layer
    for micro in micros:
        window_ref[micro, 0:BLOCK, :] = far_ref[micro * BLOCK : (micro + 1) * BLOCK, :]
        places = [(4 * micro + at) * BLOCK for at in (0, 2, 1, 3)]
        for block, at in enumerate(places):
            window_ref[micro, (1 + block) * BLOCK : (2 + block) * BLOCK, :] = near_ref[at : at + BLOCK, :]
            window_ref[micro, (5 + block) * BLOCK : (6 + block) * BLOCK, :] = own_ref[at : at + BLOCK, :]
        for block, at in enumerate(places):
            rows = slice(block * BLOCK, (block + 6) * BLOCK)
            to = at - 4 * micros[0] * BLOCK
            query = jnp.where(home, kept_ref[to : to + BLOCK, :], sent_ref[to : to + BLOCK, :])
            query = jnp.concatenate([query[:, :size], query[:, size:]], axis=0)
            scores = lax.dot_general(
                query,
                window_ref[micro, rows, 0:size],
                (((1,), (1,)), ((), ())),
                preferred_element_type=jnp.float32,
            )
            allowed = causal & (col >= low_ref[4 * micro + block] * BLOCK)
            scores = jnp.where(allowed, scores, -1e30)
            peak = jnp.max(scores, axis=-1, keepdims=True)
            raised = jnp.exp2((scores - peak) * (query_scale * 1.4426950408889634))
            total = jnp.sum(raised, axis=-1, keepdims=True)
            mixed = jnp.dot(
                raised.astype(jnp.bfloat16),
                window_ref[micro, rows, size : 2 * size],
                preferred_element_type=jnp.float32,
            )
            mixed = (mixed / total).astype(jnp.bfloat16)
            out_ref[to : to + BLOCK, 0:size] = mixed[0:BLOCK]
            out_ref[to : to + BLOCK, size : 2 * size] = mixed[BLOCK:]


def gather_kernel(place, *refs):
    parts, (out_ref, wide) = refs[:4], refs[4:]
    for by, ref in enumerate(parts):
        wide[aligned(place[CHIP] ^ by, ref.shape[0]), :] = ref[...].astype(jnp.float32)
    out_ref[...] = wide[...].astype(out_ref.dtype)


def mix_kernel(place, own, core_, across, both, weight, *out_refs):
    me = 2 * place[SECTION] + place[CORE]
    weights = [weight[:, aligned(me ^ by, 2 * HEAD_SIZE)] for by in range(4)]
    for at, out_ref in enumerate(out_refs):
        half = out_ref.shape[1]
        tp = place[TP] if at % 2 == 0 else 1 - place[TP]
        total = sum(
            lax.dot_general(
                weights[by],
                ref[aligned(2 * (at // 2) + tp, half), :],
                (((1,), (1,)), ((), ())),
                preferred_element_type=jnp.float32,
            )
            for by, ref in enumerate((own, core_, across, both))
        )
        out_ref[...] = total.astype(out_ref.dtype)


def add_kernel(residual, keep, arrived, out_ref):
    total = residual[...].astype(jnp.float32) + keep[...] + arrived[...].astype(jnp.float32)
    out_ref[...] = total.astype(out_ref.dtype)


def split_heads(x_in, norm_gain, w_query, w_key, value_projection, w_out, doc_ids):
    section = lax.axis_index("section")
    ctx = lax.axis_index("ctx")
    tp = lax.axis_index("tp")
    ctx_count = lax.axis_size("ctx")
    chips = ctx_count // 2
    chip, core = ctx // 2, ctx % 2
    place = jnp.stack([section, core, tp, chip]).astype(jnp.int32)
    micro_count, half_rows, width = x_in.shape
    tokens = 4 * half_rows
    slab = width // ctx_count
    head, pair = HEAD_SIZE, 2 * HEAD_SIZE
    block_rows = width // 4
    micros = range(micro_count)
    b16, f32 = jnp.bfloat16, jnp.float32

    def across_chips(shard):
        return [chip_xor(shard, ctx_count, by) for by in range(1, chips)]

    def whole(parts):
        rows, columns = parts[0].shape
        return call(
            gather_kernel,
            [place],
            parts,
            [((chips * rows, columns), b16)],
            [pltpu.VMEM((chips * rows, columns), f32)],
        )[0]

    x_tp = swapped(x_in, "tp")
    x_core = core_swapped(x_in, ctx_count)

    mine, theirs = call(
        pick_kernel,
        [place],
        [w_key[0], value_projection[0]],
        [((slab, 2 * pair), b16)] * 2,
        [pltpu.SemaphoreType.DMA((8,))],
        in_hbm=True,
    )
    theirs = core_swapped(theirs, ctx_count)
    gain_rows = jnp.pad(norm_gain[0], (0, 16 * pair - width)).reshape(16, pair)
    kv_own, kv_other = call(
        halve_kernel,
        [place],
        [mine, theirs, gain_rows],
        [((2 * slab, pair), b16), ((2 * slab + 16, pair), b16)],
    )
    kv_other = swapped(kv_other, "section")

    home_parts = [
        chip_xor(kv_own, ctx_count, 2),
        chip_shift(kv_own, ctx_count, 1),
        lax.ppermute(kv_own, "ctx", [(i, i - 2) for i in range(2, ctx_count)]),
    ]
    home_parts[1], later = together(home_parts[1], place)
    query_weight = call(
        query_columns_kernel,
        [later],
        [w_query[0]],
        [((width, 2 * pair), b16)],
        [pltpu.SemaphoreType.DMA((2,))],
        in_hbm=True,
    )[0]
    *home_parts, kv_other, query_weight, later = together(
        *home_parts, kv_other, query_weight, place
    )
    home_parts.append(
        lax.ppermute(home_parts[0], "ctx", [(2, 0), (3, 1), (4, 6), (5, 7)])
    )
    gain_other = kv_other[2 * slab :].reshape(-1)[:width]
    gains = own_first(section, norm_gain[0], gain_other)
    away_parts = across_chips(kv_other)

    start = jnp.sum((doc_ids[:, None, :] < doc_ids[:, :, None]).astype(jnp.int32), axis=2)
    chip_start = lax.dynamic_slice_in_dim(start, chip * 4, 4, 1)
    inside = chip * 4 + jnp.arange(4, dtype=jnp.int32)[None, :] - chip_start
    lows = 5 - inside
    order = inside.reshape(micro_count, 2, 2).transpose(0, 2, 1).reshape(micro_count, 4)
    tables = host_tables(doc_ids.shape[1])

    def by_block(weight):
        columns = weight.shape[1]
        weight = weight.reshape(chips, 4, slab // 2, columns).transpose(1, 0, 2, 3)
        return weight.reshape(4, block_rows, columns)

    def shifted(key_value, far):
        return chip_shift(key_value, ctx_count, 1), chip_shift(far, ctx_count, 2)

    def sent_over(layer, queries):
        return lax.ppermute(queries, "section", [(layer, 1 - layer)])

    def attend(layer, which, low, query, key_value, window):
        own, sent = query
        near, far = window
        return call(
            functools.partial(attention_kernel, layer, which),
            [place, low],
            [own, sent, far, near, key_value],
            [(own.shape, b16)],
            [pltpu.VMEM((micro_count, 9 * BLOCK, pair), b16)],
        )[0]

    def mix(attended, across, out_weight):
        shape = (block_rows, tokens // 2)
        return call(
            mix_kernel,
            [place],
            [
                attended,
                core_swapped(attended, ctx_count),
                across,
                core_swapped(across, ctx_count),
                out_weight,
            ],
            [(shape, f32), (shape, b16)] * (attended.shape[0] // tokens),
            )

    def add(residual, keep, send):
        return call(add_kernel, [], [residual, keep, swapped(send, "tp")], [(send.shape, b16)])[0]

    def spread(piece, direct):
        over_tp, over_section = swapped(piece, "tp"), swapped(piece, "section")
        if direct:
            over_both = lax.ppermute(piece, ("section", "tp"), [(i, 3 - i) for i in range(4)])
        else:
            over_both = swapped(over_tp, "section")
        return [piece, over_tp, over_section, over_both]

    def both_cores(pieces):
        over = [core_swapped(one, ctx_count) for one in pieces]
        return pieces[:2] + over[:2] + pieces[2:] + over[2:]

    def in_order(blocks):
        by_section = [own_first(core, blocks[0], blocks[1]), own_first(core, blocks[2], blocks[3])]
        low = own_first(section, by_section[0][0], by_section[1][0])
        high = own_first(section, by_section[0][1], by_section[1][1])
        whole = jnp.stack([low[0], high[0], low[1], high[1]])
        count = whole.shape[-1]
        whole = whole.reshape(4, chips, slab // 2, count).transpose(1, 0, 2, 3)
        return whole.reshape(width, count)

    half_shape = ((slab // 2, w_out.shape[1]), b16)
    kept, sent = call(
        split_kernel,
        [later],
        [w_out[0].T],
        [half_shape] * 2,
        [pltpu.VMEM((slab, w_out.shape[1]), f32)],
    )
    own_half, cross_half = call(
        sort_kernel, [place], [kept, core_swapped(sent, ctx_count)], [half_shape] * 2
    )
    cross_half = swapped(cross_half, "section")
    x_tp, later = together(x_tp, later)
    x_both = core_swapped(x_tp, ctx_count)
    rows = (micro_count * tokens, pair)
    normed, query = [], []
    for micro in micros:
        one, *query = call(
            functools.partial(first_query_kernel, micro),
            [place, order[micro]],
            [x_in, x_tp, x_core, x_both, *tables, gains[0][None], query_weight, *query],
            [((tokens, width), b16), (rows, b16), (rows, b16)],
        )
        normed.append(one)
    *away_parts, home_parts[3], cross_half, normed[0], normed[1] = together(
        *away_parts, home_parts[3], cross_half, *normed
    )
    home_parts, away_parts = [kv_own, *home_parts], [kv_other, *away_parts]
    out_halves = call(layers_kernel, [place], [own_half, cross_half], [(own_half.shape, b16)] * 2)
    key, far = call(
        first_keys_kernel,
        [place, order.reshape(-1)],
        [*normed, *home_parts, *away_parts, *tables],
        [(rows, b16), ((micro_count * BLOCK, pair), b16)],
        [pltpu.VMEM((width, pair), b16)],
    )
    window = shifted(key, far)

    key, out_half, later = together(key, out_halves[0], place)
    out_parts = across_chips(out_half)
    query = query[0], sent_over(0, query[1])
    attended = attend(0, micros, lows.reshape(-1), query, key, window)
    across = swapped(attended, "section")
    (residuals,) = call(
        residual_kernel,
        [later],
        [x_in, x_core],
        [((micro_count, block_rows, tokens // 2), f32)],
        [pltpu.VMEM((width, BLOCK), f32)],
    )
    late_gain, late_query_weight, next_kv = call(
        late_kernel,
        [later],
        [gains[1][None], query_weight, *home_parts, *away_parts],
        [
            ((4, block_rows, BLOCK), f32),
            ((4, block_rows, 2 * pair), b16),
            ((block_rows, 4 * pair), b16),
        ],
        [pltpu.VMEM((block_rows, 4 * pair), f32)],
    )
    *out_parts, across, next_kv, residuals = together(*out_parts, across, next_kv, residuals)
    out_weight = whole([out_half, *out_parts])
    mixed = mix(attended, across, out_weight)
    mixed[1], mixed[3], out_half = together(mixed[1], mixed[3], out_halves[1])
    out_parts = across_chips(out_half)
    halves = [add(residuals[m], *mixed[2 * m : 2 * m + 2]) for m in micros]
    spreads = [spread(halves[0], True)]
    halves[1], spreads[0][1], spreads[0][2], out_parts[1] = together(
        halves[1], *spreads[0][1:3], out_parts[1]
    )
    spreads.append(spread(halves[1], False))
    *spreads[0][1:], spreads[1][1], spreads[1][2] = together(*spreads[0][1:], *spreads[1][1:3])
    *spreads[0][1:], out_parts[0], out_parts[2] = together(
        *spreads[0][1:], out_parts[0], out_parts[2]
    )
    next_out = whole([out_half, *out_parts])

    pieces, queries, before = [], [], []
    for micro in micros:
        pieces.append(both_cores(spreads[micro]))
        *before, normed = call(
            keys_kernel,
            [place, order[micro]],
            [*pieces[micro], *tables, late_gain, next_kv, *before],
            [
                (((micro + 1) * tokens, pair), b16),
                (((micro + 1) * BLOCK, pair), b16),
                ((4, block_rows, tokens), b16),
            ],
        )
        normed, before[0] = together(normed, before[0])
        query = call(
            query_kernel,
            [place, order[micro]],
            [normed, late_query_weight, *tables],
            [((tokens, pair), b16)] * 2,
        )
        queries.append(query)
        if micro == 0:
            query[0], *spreads[1] = together(query[0], *spreads[1])
    key, far = before
    window = shifted(key, far)
    queries = [(own, sent_over(1, other)) for own, other in queries]
    near, far, first, second, next_out = together(
        *window, *[sent for _, sent in queries], next_out
    )
    queries = [(queries[0][0], first), (queries[1][0], second)]
    attended = [attend(1, (m,), lows.reshape(-1), queries[m], key, (near, far)) for m in micros]
    across = [swapped(one, "section") for one in attended]
    across[0], attended[1] = together(across[0], attended[1])
    mixed = [mix(attended[0], across[0], next_out)]
    mixed[0][0], across[1] = together(mixed[0][0], across[1])
    mixed.append(mix(attended[1], across[1], next_out))
    results = [
        jnp.stack(
            [in_order([columns(one[2 * i], core, BLOCK) for i in range(4)]).T for one in pieces]
        )
    ]
    last = []
    for micro in micros:
        piece = add(halves[micro], *mixed[micro])
        blocks = []
        for one in (piece, lax.ppermute(piece, "section", [(0, 1)])):
            kept, passed = own_first(core, one[:, :BLOCK], one[:, BLOCK:])
            blocks += [kept, core_swapped(passed, ctx_count)]
        last.append(in_order(blocks).T)
    results.append(jnp.stack(last))
    return jnp.where(section == 0, results[0], results[1])[None]


def solution(mesh):
    in_specs = (
        P(None, ("ctx", "tp"), None),
        P("section", None),
        P("section", None, "tp"),
        P("section", "ctx", "tp"),
        P("section", "ctx", "tp"),
        P("section", "tp", "ctx"),
        P(),
    )
    out_specs = P("section", None, ("ctx", "tp"), None)
    sizes = mesh.shape
    fits = sizes["section"] == 2 and sizes["tp"] == 2 and sizes["ctx"] == 8
    body = split_heads if fits else local
    return jax.shard_map(body, mesh=mesh, in_specs=in_specs, out_specs=out_specs, check_vma=False)
```
